32 devices in a mesh: edge: 16 (over z, y, x), rep: 2 (over core).
Axes of the slice: x: 2, y: 2, z: 4, core: 2. Of those that a mesh axis runs over, the one named last changes fastest.
Arguments:
- nodes: bfloat16 [64, 131072], P(None, ('edge', 'rep')), may hold values from -6 to 6
- edges: bfloat16 [64, 524288], P(None, ('edge', 'rep')), may hold values from -6 to 6
- target: bfloat16 [64, 131072], P(None, ('edge', 'rep')), may hold values from -6 to 6
- senders: int32 [524288], P(('edge', 'rep')), may hold values from 0 to 4095
- receivers: int32 [524288], P(('edge', 'rep')), may hold values from 0 to 4095
- counts: int32 [512], P(('edge', 'rep')), may hold values from 1 to 1024, as said below
- levels: int32 [131072], P(('edge', 'rep')), may hold values from 0 to 3
- land: int32 [131072], P(('edge', 'rep')), may hold values 0 or 1
- channel_mask: int32 [4, 64], replicated, may hold values 0 or 1
- edge_in: bfloat16 [192, 64], replicated, may hold values from -0.4375 to 0.4375
- edge_in_bias: bfloat16 [64], replicated, may hold values from -3 to 3
- edge_out: bfloat16 [64, 64], replicated, may hold values from -0.75 to 0.75
- edge_out_bias: bfloat16 [64], replicated, may hold values from -3 to 3
- edge_gain: bfloat16 [64], replicated, may hold values from 0.25 to 1.75
- edge_shift: bfloat16 [64], replicated, may hold values from -3 to 3
- node_in: bfloat16 [128, 64], replicated, may hold values from -0.5 to 0.5
- node_in_bias: bfloat16 [64], replicated, may hold values from -3 to 3
- node_out: bfloat16 [64, 64], replicated, may hold values from -0.75 to 0.75
- node_out_bias: bfloat16 [64], replicated, may hold values from -3 to 3
- node_gain: bfloat16 [64], replicated, may hold values from 0.25 to 1.75
- node_shift: bfloat16 [64], replicated, may hold values from -3 to 3
Outputs:
- new_nodes: bfloat16 [64, 131072], P(None, ('edge', 'rep'))
- node_grad: bfloat16 [64, 131072], P(None, ('edge', 'rep'))
- edge_grad: bfloat16 [64, 524288], P(None, ('edge', 'rep'))
- edge_in_grad: float32 [192, 64], replicated
- edge_in_bias_grad: float32 [64], replicated
- edge_out_grad: float32 [64, 64], replicated
- edge_out_bias_grad: float32 [64], replicated
- edge_gain_grad: float32 [64], replicated
- edge_shift_grad: float32 [64], replicated
- node_in_grad: float32 [128, 64], replicated
- node_in_bias_grad: float32 [64], replicated
- node_out_grad: float32 [64, 64], replicated
- node_out_bias_grad: float32 [64], replicated
- node_gain_grad: float32 [64], replicated
- node_shift_grad: float32 [64], replicated
The draws below stay inside these ranges and needn't reach their ends.
Inputs may be any that keep to these rules, and one draw needn't show every extreme that they name: `counts`: in every draw some owner gets 1024 live slots from every sender block of its region, and another gets exactly 1 from every one.
All inputs are finite; a program needn't handle non-finite values. No bound on the sum of `land` on one device may be relied on, other than what follows from the above.
Results may differ from the reference program's by a relative error of at most 0.0081.
Values may be sent and summed in bfloat16 or wider, within the bound.
A program may use at most 128 MiB of HBM per device.

```python
import jax
import jax.numpy as jnp
from jax import lax

D = 64
LEVELS = 4
NODE_DEV = 4096
SLOTS_DEV = 16384
OWNERS = 16
REGIONS = 2
CAP = 1024
NODES = 131072
SLOTS = 524288


def draw_counts(key, part):
    key = jax.random.fold_in(key, 11)
    key_load, key_dip, key_full, key_small = jax.random.split(key, 4)
    owner_load = jax.random.randint(key_load, (OWNERS,), CAP // 8, CAP + 1)
    full_owner = jax.random.randint(key_full, (), 0, OWNERS)
    small_owner = (full_owner + 1 + jax.random.randint(key_small, (), 0, OWNERS - 1)) % OWNERS
    owner_index = jnp.arange(OWNERS, dtype=jnp.int32)
    owner_load = jnp.where(owner_index == full_owner, CAP, owner_load)
    owner_load = jnp.where(owner_index == small_owner, 1, owner_load)
    dip = jax.random.randint(key_dip, (OWNERS * REGIONS, OWNERS), 0, CAP // 16 + 1)
    fixed_owner = (owner_index == full_owner) | (owner_index == small_owner)
    dip = jnp.where(fixed_owner[None, :], 0, dip)
    return jnp.maximum(owner_load[None, :] - dip, 1).reshape(-1).astype(jnp.int32)


def set_ends(values, stream_key, low, high):
    longest = values.shape.index(max(values.shape))
    spots = []
    for shift in (0, 1):
        where = [jax.random.randint(jax.random.fold_in(stream_key, axis), (), 0, length) for axis, length in enumerate(values.shape)]
        where[longest] = (where[longest] + shift) % values.shape[longest]
        spots.append(tuple(where))
    return values.at[spots[0]].set(low).at[spots[1]].set(high)


def shard_levels(rng, extent, cuts, smallest, largest):
    factor_of, own = 1.0, jax.random.fold_in(rng, 6)
    for dim, shards_of in cuts:
        steps = jnp.exp(jax.random.uniform(jax.random.fold_in(own, dim), (shards_of,), jnp.float32, smallest / len(cuts), largest / len(cuts)))
        factor_of = factor_of * jnp.repeat(steps, extent[dim] // shards_of).reshape([-1 if axis == dim else 1 for axis in range(len(extent))])
    return factor_of


def scatter_about(stream_key, shape, spread, most, cuts=(), held_as=jnp.bfloat16):
    result = spread * jax.random.normal(stream_key, shape, jnp.float32)
    if cuts:
        result = result * shard_levels(stream_key, shape, cuts, -0.22, 0.18)
    return jnp.clip(result, -most, most).astype(held_as)


def setup_inputs(seed: int = 0) -> dict:
    arg_keys = jax.random.split(jax.random.key(seed), 22)
    nodes = scatter_about(arg_keys[0], (D, NODES), 1.0, 6.0, ((1, 32),))
    edges = scatter_about(arg_keys[1], (D, SLOTS), 1.0, 6.0, ((1, 32),))
    target = scatter_about(arg_keys[2], (D, NODES), 1.0, 6.0, ((1, 32),))
    senders = set_ends(jax.random.randint(arg_keys[3], (SLOTS,), 0, NODE_DEV), jax.random.fold_in(arg_keys[3], 1), 0, NODE_DEV - 1).astype(jnp.int32)
    receivers = set_ends(jax.random.randint(arg_keys[4], (SLOTS,), 0, NODE_DEV), jax.random.fold_in(arg_keys[4], 1), 0, NODE_DEV - 1).astype(jnp.int32)
    counts = draw_counts(jax.random.fold_in(arg_keys[21], 71), 0)
    levels = set_ends(jax.random.randint(arg_keys[6], (NODES,), 0, LEVELS), jax.random.fold_in(arg_keys[6], 1), 0, LEVELS - 1).astype(jnp.int32)
    land = set_ends((jax.random.randint(arg_keys[7], (NODES,), 0, 3) < 2).astype(jnp.int32), jax.random.fold_in(arg_keys[7], 1), 0, 1)
    channel_mask = set_ends((jax.random.randint(arg_keys[8], (LEVELS, D), 0, 4) < 3).astype(jnp.int32), jax.random.fold_in(arg_keys[8], 1), 0, 1)
    edge_in = scatter_about(arg_keys[9], (3 * D, D), (3 * D) ** -0.5, 0.4375)
    edge_in_bias = scatter_about(arg_keys[10], (D,), 0.5, 3.0)
    edge_out = scatter_about(arg_keys[11], (D, D), D ** -0.5, 0.75)
    edge_out_bias = scatter_about(arg_keys[12], (D,), 0.5, 3.0)
    edge_gain = jnp.clip(1.0 + 0.15 * jax.random.normal(arg_keys[13], (D,), jnp.float32), 0.25, 1.75).astype(jnp.bfloat16)
    edge_shift = scatter_about(arg_keys[14], (D,), 0.4, 3.0)
    node_in = scatter_about(arg_keys[15], (2 * D, D), (2 * D) ** -0.5, 0.5)
    node_in_bias = scatter_about(arg_keys[16], (D,), 0.5, 3.0)
    node_out = scatter_about(arg_keys[17], (D, D), D ** -0.5, 0.75)
    node_out_bias = scatter_about(arg_keys[18], (D,), 0.5, 3.0)
    node_gain = jnp.clip(1.0 + 0.15 * jax.random.normal(arg_keys[19], (D,), jnp.float32), 0.25, 1.75).astype(jnp.bfloat16)
    node_shift = scatter_about(arg_keys[20], (D,), 0.4, 3.0)
    return {"nodes": nodes, "edges": edges, "target": target, "senders": senders, "receivers": receivers, "counts": counts, "levels": levels, "land": land, "channel_mask": channel_mask, "edge_in": edge_in, "edge_in_bias": edge_in_bias, "edge_out": edge_out, "edge_out_bias": edge_out_bias, "edge_gain": edge_gain, "edge_shift": edge_shift, "node_in": node_in, "node_in_bias": node_in_bias, "node_out": node_out, "node_out_bias": node_out_bias, "node_gain": node_gain, "node_shift": node_shift}


@jax.custom_vjp
def low(v):
    return lax.optimization_barrier(v.astype(jnp.bfloat16)).astype(jnp.float32)

@jax.custom_vjp
def low_back(v):
    return v

def low_keep(v):
    return (low(v), None)

def low_pass(kept, grad):
    return (grad,)

def back_keep(v):
    return (v, None)

def back_low(kept, grad):
    return (low(grad),)
low.defvjp(low_keep, low_pass)
low_back.defvjp(back_keep, back_low)
NORM_EPS = 1e-05

def project(weight, columns):
    return jnp.einsum('io,is->os', weight, columns, precision=lax.Precision.HIGHEST)

def layer_norm(values, gain, shift):
    center = lax.optimization_barrier(jnp.mean(values, axis=0, keepdims=True))
    shifted = values - center
    variance = lax.optimization_barrier(jnp.mean(shifted * shifted, axis=0, keepdims=True))
    return shifted * lax.rsqrt(variance + NORM_EPS) * gain[:, None] + shift[:, None]

def slot_layout(senders, receivers, counts):
    blocks_all = OWNERS * REGIONS
    send_local = senders.reshape(blocks_all, SLOTS_DEV)
    owner_view = receivers.reshape(OWNERS, REGIONS, OWNERS, CAP)
    recv_local = jnp.transpose(owner_view, (2, 1, 0, 3)).reshape(blocks_all, OWNERS, CAP)
    source = jnp.arange(blocks_all, dtype=jnp.int32)
    region = source % REGIONS
    owner_block = jnp.arange(OWNERS, dtype=jnp.int32)[None, :] * REGIONS + region[:, None]
    send_global = send_local + source[:, None] * NODE_DEV
    recv_global = recv_local + (owner_block * NODE_DEV)[:, :, None]
    place = jnp.arange(CAP, dtype=jnp.int32)
    live = (place[None, None, :] < counts.reshape(blocks_all, OWNERS)[:, :, None]).astype(jnp.float32)
    return (send_global, recv_global.reshape(blocks_all, SLOTS_DEV), live.reshape(blocks_all, SLOTS_DEV))

def forward(params, node_vals, edge_vals, send_global, recv_global, live):
    edge_in, edge_in_bias, edge_out, edge_out_bias, edge_gain, edge_shift, node_in, node_in_bias, node_out, node_out_bias, node_gain, node_shift = params
    blocks_all = OWNERS * REGIONS
    edge_blocks = jnp.transpose(edge_vals.reshape(D, blocks_all, SLOTS_DEV), (1, 0, 2))

    def edge_block(inputs):
        edge_cols, send_ids, recv_ids, live_row = inputs
        sender_cols = low_back(jnp.take(node_vals, send_ids, axis=1))
        receiver_cols = low_back(jnp.take(node_vals, recv_ids, axis=1))
        stacked = jnp.concatenate([edge_cols, sender_cols, receiver_cols], axis=0)
        edge_pre = low_back(project(edge_in, stacked) + edge_in_bias[:, None])
        edge_hidden = low(jax.nn.silu(edge_pre))
        edge_outer = low_back(project(edge_out, edge_hidden) + edge_out_bias[:, None])
        updated = edge_cols + layer_norm(edge_outer, edge_gain, edge_shift)
        return low_back(low(updated * live_row[None, :]))
    messages = lax.map(jax.checkpoint(edge_block), (edge_blocks, send_global, recv_global, live))
    flat = jnp.transpose(messages, (1, 0, 2)).reshape(D, blocks_all * SLOTS_DEV)
    summed = jax.ops.segment_sum(flat.T, recv_global.reshape(-1), num_segments=NODES).T
    aggregate = low(summed)
    node_stack = jnp.concatenate([node_vals, aggregate], axis=0)
    node_pre = low_back(project(node_in, node_stack) + node_in_bias[:, None])
    node_hidden = low(jax.nn.silu(node_pre))
    node_outer = low_back(project(node_out, node_hidden) + node_out_bias[:, None])
    return node_vals + layer_norm(node_outer, node_gain, node_shift)

def reference(nodes, edges, target, senders, receivers, counts, levels, land, channel_mask, edge_in, edge_in_bias, edge_out, edge_out_bias, edge_gain, edge_shift, node_in, node_in_bias, node_out, node_out_bias, node_gain, node_shift):
    send_global, recv_global, live = slot_layout(senders, receivers, counts)
    params = tuple((weight.astype(jnp.float32) for weight in (edge_in, edge_in_bias, edge_out, edge_out_bias, edge_gain, edge_shift, node_in, node_in_bias, node_out, node_out_bias, node_gain, node_shift)))
    loss_weight = (channel_mask[levels].astype(jnp.float32) * land.astype(jnp.float32)[:, None]).T
    goal = target.astype(jnp.float32)

    def loss_of(weights, node_vals, edge_vals):
        state = forward(weights, node_vals, edge_vals, send_global, recv_global, live)
        differ = state - goal
        return (0.5 * jnp.sum(loss_weight * differ * differ), state)
    loss, pullback, state = jax.vjp(loss_of, params, nodes.astype(jnp.float32), edges.astype(jnp.float32), has_aux=True)
    weight_grads, node_grad, edge_grad = pullback(jnp.ones_like(loss))
    return (state.astype(jnp.bfloat16), node_grad.astype(jnp.bfloat16), edge_grad.astype(jnp.bfloat16), weight_grads[0], weight_grads[1], weight_grads[2], weight_grads[3], weight_grads[4], weight_grads[5], weight_grads[6], weight_grads[7], weight_grads[8], weight_grads[9], weight_grads[10], weight_grads[11])
```

```python
import functools

import jax
import jax.numpy as jnp
from jax import lax
from jax.experimental import pallas as pl
from jax.experimental.pallas import tpu as pltpu
from jax.sharding import PartitionSpec as P

NORM_EPS = 1e-05
F32 = jnp.float32
BF16 = jnp.bfloat16
LOW = 256
VMEM_LIMIT = 56 * 2**20

EB1, EB2, EG, EH, NB1, NB2, NG, NH, CM = 0, 1, 2, 3, 4, 5, 6, 7, 8


def dot(a, b):
    return jnp.dot(a, b, preferred_element_type=F32)


def dot_tn(a, b):
    return lax.dot_general(a, b, (((0,), (0,)), ((), ())), preferred_element_type=F32)


def dot_nt(a, b):
    return lax.dot_general(a, b, (((1,), (1,)), ((), ())), preferred_element_type=F32)


def one_hot_low(ids):
    low = ids & (LOW - 1)
    rows = lax.broadcasted_iota(jnp.int32, (LOW, ids.shape[1]), 0)
    return (rows == low).astype(F32).astype(BF16)


def high_of(ids, rows):
    high = ids >> (LOW.bit_length() - 1)
    return jnp.broadcast_to(high.astype(F32).astype(BF16), (rows, ids.shape[1]))


def stack_table(table_ref, value):
    rows = value.shape[0]
    for h in range(value.shape[1] // LOW):
        table_ref[h * rows : (h + 1) * rows, :] = value[:, h * LOW : (h + 1) * LOW]


def gather_columns(table, ids, rows):
    picked = dot(table, one_hot_low(ids)).astype(BF16)
    high = high_of(ids, rows)
    out = picked[:rows]
    for h in range(1, table.shape[0] // rows):
        out = jnp.where(high == BF16(h), picked[h * rows : (h + 1) * rows], out)
    return out


def scatter_columns(values, ids, count):
    rows = values.shape[0]
    high = high_of(ids, rows)
    zero = jnp.zeros_like(values)
    spread = jnp.concatenate(
        [jnp.where(high == BF16(h), values, zero) for h in range(count // LOW)], axis=0
    )
    return dot_nt(spread, one_hot_low(ids))


def unstack(table):
    rows = 64
    return jnp.concatenate(
        [table[h * rows : (h + 1) * rows] for h in range(table.shape[0] // rows)], axis=1
    )


def column(cols, index):
    return cols[:, index : index + 1]


def mean_rows(v):
    return jnp.mean(v, axis=0, keepdims=True)


def lane_sums(v):
    out = v[:, :128]
    for k in range(1, v.shape[1] // 128):
        out = out + v[:, k * 128 : (k + 1) * 128]
    return out


def branch_forward(w1, w2, b1, b2, stacked):
    pre = dot_tn(w1, stacked) + b1
    hidden = (pre * (1.0 / (1.0 + jnp.exp(-pre)))).astype(BF16)
    outer = dot_tn(w2, hidden) + b2
    shifted = outer - mean_rows(outer)
    inverse = lax.rsqrt(mean_rows(shifted * shifted) + NORM_EPS)
    return pre, hidden, shifted * inverse, inverse


def branch_backward(w2, gain, grad, pre, normal, inverse):
    q = grad * gain
    outer_grad = (
        inverse * (q - mean_rows(q) - normal * mean_rows(q * normal))
    ).astype(BF16)
    s = 1.0 / (1.0 + jnp.exp(-pre))
    pre_grad = (dot(w2, outer_grad) * (s * (1.0 + pre * (1.0 - s)))).astype(BF16)
    return outer_grad, pre_grad


def gather_kernel(cap, table_ref, ids_ref, out_ref, stacked):
    rows = table_ref.shape[0]

    @pl.when(pl.program_id(0) == 0)
    def _():
        stack_table(stacked, table_ref[...])

    got = gather_columns(stacked[...], ids_ref[...], rows)
    for k in range(out_ref.shape[0]):
        out_ref[k] = got[:, k * cap : (k + 1) * cap]


def gather_for_owners(table, ids, owners, step):
    rows, count = table.shape
    slots = ids.shape[1]
    cap = slots // owners
    return pl.pallas_call(
        functools.partial(gather_kernel, cap),
        grid=(slots // step,),
        in_specs=[
            pl.BlockSpec((rows, count), lambda i: (0, 0)),
            pl.BlockSpec((1, step), lambda i: (0, i)),
        ],
        out_specs=pl.BlockSpec((step // cap, rows, cap), lambda i: (i, 0, 0)),
        out_shape=jax.ShapeDtypeStruct((owners, rows, cap), BF16),
        scratch_shapes=[pltpu.VMEM((rows * (count // LOW), LOW), BF16)],
        compiler_params=pltpu.CompilerParams(vmem_limit_bytes=VMEM_LIMIT),
        name="gather_columns",
    )(table, ids)


def live_of(counts_ref, step, cap):
    place = lax.broadcasted_iota(jnp.int32, (1, cap), 1)
    base = pl.program_id(0) * (step // cap)
    return jnp.concatenate(
        [(place < counts_ref[base + k]).astype(F32) for k in range(step // cap)], axis=1
    )


def edge_forward_kernel(
    cap, counts_ref, nodes_ref, edges_ref, got_ref, senders_ref, w1_ref, w2_ref, cols_ref,
    message_ref, pre_ref, normal_ref, inverse_ref, stacked,
):
    rows, step = edges_ref.shape

    @pl.when(pl.program_id(0) == 0)
    def _():
        stack_table(stacked, nodes_ref[...])

    cols = cols_ref[...]
    sent = gather_columns(stacked[...], senders_ref[...], rows)
    got = jnp.concatenate([got_ref[k] for k in range(step // cap)], axis=1)
    edges = edges_ref[...]
    pre, _, normal, inverse = branch_forward(
        w1_ref[...], w2_ref[...], column(cols, EB1), column(cols, EB2),
        jnp.concatenate([edges, sent, got], axis=0),
    )
    pre_ref[...] = pre
    normal_ref[...] = normal
    inverse_ref[...] = inverse
    live = live_of(counts_ref, step, cap)
    message = (
        (edges.astype(F32) + (normal * column(cols, EG) + column(cols, EH))) * live
    ).astype(BF16)
    for k in range(step // cap):
        message_ref[k] = message[:, k * cap : (k + 1) * cap]


def edge_forward(counts, nodes, edges, got, senders, w1, w2, cols, step):
    rows, slots = edges.shape
    owners = got.shape[0]
    cap = slots // owners
    whole = lambda a: pl.BlockSpec(a.shape, lambda i: (0,) * a.ndim)
    wide = pl.BlockSpec((rows, step), lambda i: (0, i))
    split = pl.BlockSpec((step // cap, rows, cap), lambda i: (i, 0, 0))
    line = pl.BlockSpec((1, step), lambda i: (0, i))
    return pl.pallas_call(
        functools.partial(edge_forward_kernel, cap),
        grid=(slots // step,),
        in_specs=[
            pl.BlockSpec(memory_space=pltpu.SMEM), whole(nodes), wide, split, line,
            whole(w1), whole(w2), whole(cols),
        ],
        out_specs=[split, wide, wide, line],
        out_shape=[
            jax.ShapeDtypeStruct((owners, rows, cap), BF16),
            jax.ShapeDtypeStruct((rows, slots), F32),
            jax.ShapeDtypeStruct((rows, slots), F32),
            jax.ShapeDtypeStruct((1, slots), F32),
        ],
        scratch_shapes=[pltpu.VMEM((rows * (nodes.shape[1] // LOW), LOW), BF16)],
        compiler_params=pltpu.CompilerParams(vmem_limit_bytes=VMEM_LIMIT),
        name="edge_forward",
    )(counts, nodes, edges, got, senders, w1, w2, cols)


def node_kernel(
    cap, levels_count, arrived_ref, receivers_ref, nodes_ref, target_ref, levels_ref, land_ref,
    w1_ref, w2_ref, cols_ref,
    new_ref, part_ref, agg_grad_ref, first_ref, second_ref, vec_ref, total,
):
    rows, count = nodes_ref.shape
    step = receivers_ref.shape[1]

    @pl.when(pl.program_id(0) == 0)
    def _():
        total[...] = jnp.zeros_like(total)

    arrived = jnp.concatenate([arrived_ref[k] for k in range(step // cap)], axis=1)
    total[...] += scatter_columns(arrived, receivers_ref[...], count)

    @pl.when(pl.program_id(0) == pl.num_programs(0) - 1)
    def _():
        cols = cols_ref[...]
        aggregate = unstack(total[...]).astype(BF16)
        nodes = nodes_ref[...]
        stacked = jnp.concatenate([nodes, aggregate], axis=0)
        pre, hidden, normal, inverse = branch_forward(
            w1_ref[...], w2_ref[...], column(cols, NB1), column(cols, NB2), stacked
        )
        gain = column(cols, NG)
        state = nodes.astype(F32) + (normal * gain + column(cols, NH))
        new_ref[...] = state.astype(BF16)
        levels = levels_ref[...]
        weight = jnp.zeros((rows, count), F32)
        for l in range(levels_count):
            weight = jnp.where(levels == l, column(cols, CM + l), weight)
        weight = weight * land_ref[...].astype(F32)
        grad = weight * (state - target_ref[...].astype(F32))
        outer_grad, pre_grad = branch_backward(w2_ref[...], gain, grad, pre, normal, inverse)
        stacked_grad = dot(w1_ref[...], pre_grad)
        part_ref[...] = grad + stacked_grad[:rows]
        agg_grad_ref[...] = stacked_grad[rows:].astype(BF16)
        first_ref[...] = dot_nt(stacked, pre_grad)
        second_ref[...] = dot_nt(hidden, outer_grad)
        sums = [
            lane_sums(v).sum(axis=1, keepdims=True)
            for v in (pre_grad.astype(F32), outer_grad.astype(F32), grad * normal, grad)
        ]
        vec_ref[...] = jnp.concatenate(sums, axis=1)


def node_step(arrived, receivers, nodes, target, levels, land, w1, w2, cols, levels_count, step):
    owners, rows, cap = arrived.shape
    count = nodes.shape[1]
    slots = receivers.shape[1]
    whole = lambda a: pl.BlockSpec(a.shape, lambda i: (0,) * len(a.shape))
    outs = [
        jax.ShapeDtypeStruct((rows, count), BF16),
        jax.ShapeDtypeStruct((rows, count), F32),
        jax.ShapeDtypeStruct((rows, count), BF16),
        jax.ShapeDtypeStruct(w1.shape, F32),
        jax.ShapeDtypeStruct(w2.shape, F32),
        jax.ShapeDtypeStruct((rows, 4), F32),
    ]
    return pl.pallas_call(
        functools.partial(node_kernel, cap, levels_count),
        grid=(slots // step,),
        in_specs=[
            pl.BlockSpec((step // cap, rows, cap), lambda i: (i, 0, 0)),
            pl.BlockSpec((1, step), lambda i: (0, i)),
            *(whole(a) for a in (nodes, target, levels, land, w1, w2, cols)),
        ],
        out_specs=[whole(o) for o in outs],
        out_shape=outs,
        scratch_shapes=[pltpu.VMEM((rows * (count // LOW), LOW), F32)],
        compiler_params=pltpu.CompilerParams(vmem_limit_bytes=VMEM_LIMIT),
        name="sum_and_nodes",
    )(arrived, receivers, nodes, target, levels, land, w1, w2, cols)


def edge_backward_kernel(
    cap, count, counts_ref, back_ref, edges_ref, pre_ref, normal_ref, inverse_ref, senders_ref,
    w1_ref, w2_ref, cols_ref,
    edge_grad_ref, pre_grad_ref, sent_ref, pair_ref, vec_ref, sums,
):
    rows, step = edges_ref.shape

    @pl.when(pl.program_id(0) == 0)
    def _():
        sent_ref[...] = jnp.zeros_like(sent_ref)
        pair_ref[...] = jnp.zeros_like(pair_ref)
        sums[...] = jnp.zeros_like(sums)

    cols = cols_ref[...]
    live = live_of(counts_ref, step, cap)
    grad = jnp.concatenate([back_ref[k] for k in range(step // cap)], axis=1).astype(F32) * live
    pre, normal = pre_ref[...], normal_ref[...]
    outer_grad, pre_grad = branch_backward(
        w2_ref[...], column(cols, EG), grad, pre, normal, inverse_ref[...]
    )
    hidden = (pre * (1.0 / (1.0 + jnp.exp(-pre)))).astype(BF16)
    edges = edges_ref[...]
    edge_grad_ref[...] = (grad + dot(w1_ref[:rows, :], pre_grad)).astype(BF16)
    for k in range(step // cap):
        pre_grad_ref[k] = pre_grad[:, k * cap : (k + 1) * cap]
    sent_ref[...] += scatter_columns(pre_grad, senders_ref[...], count)
    pair_ref[...] += dot_nt(
        jnp.concatenate([edges, hidden], axis=0), jnp.concatenate([pre_grad, outer_grad], axis=0)
    )
    for k, v in enumerate((pre_grad.astype(F32), outer_grad.astype(F32), grad * normal, grad)):
        sums[k] += lane_sums(v)

    @pl.when(pl.program_id(0) == pl.num_programs(0) - 1)
    def _():
        vec_ref[...] = jnp.concatenate(
            [sums[k].sum(axis=1, keepdims=True) for k in range(4)], axis=1
        )


def edge_backward(counts, back, edges, pre, normal, inverse, senders, w1, w2, cols, count, step):
    rows, slots = edges.shape
    owners, _, cap = back.shape
    whole = lambda a: pl.BlockSpec(a.shape, lambda i: (0,) * len(a.shape))
    wide = pl.BlockSpec((rows, step), lambda i: (0, i))
    split = pl.BlockSpec((step // cap, rows, cap), lambda i: (i, 0, 0))
    line = pl.BlockSpec((1, step), lambda i: (0, i))
    outs = [
        jax.ShapeDtypeStruct((rows, slots), BF16),
        jax.ShapeDtypeStruct((owners, rows, cap), BF16),
        jax.ShapeDtypeStruct((rows * (count // LOW), LOW), F32),
        jax.ShapeDtypeStruct((2 * rows, 2 * rows), F32),
        jax.ShapeDtypeStruct((rows, 4), F32),
    ]
    return pl.pallas_call(
        functools.partial(edge_backward_kernel, cap, count),
        grid=(slots // step,),
        in_specs=[
            pl.BlockSpec(memory_space=pltpu.SMEM), split, wide, wide, wide, line, line,
            whole(w1), whole(w2), whole(cols),
        ],
        out_specs=[wide, split, *(whole(o) for o in outs[2:])],
        out_shape=outs,
        scratch_shapes=[pltpu.VMEM((4, rows, 128), F32)],
        compiler_params=pltpu.CompilerParams(vmem_limit_bytes=VMEM_LIMIT),
        name="edge_backward",
    )(counts, back, edges, pre, normal, inverse, senders, w1, w2, cols)


def split_dot_nt(low, wide):
    top = wide.astype(BF16)
    rest = (wide - top.astype(F32)).astype(BF16)
    return dot_nt(low, top) + dot_nt(low, rest)


def split_dot(low, wide):
    top = wide.astype(BF16)
    rest = (wide - top.astype(F32)).astype(BF16)
    return dot(low, top) + dot(low, rest)


def finish_kernel(
    cap, returned_ref, receivers_ref, nodes_ref, part_ref, sent_ref, w1_ref,
    out_ref, rest_ref, total,
):
    rows, count = nodes_ref.shape
    step = receivers_ref.shape[1]

    @pl.when(pl.program_id(0) == 0)
    def _():
        total[...] = jnp.zeros_like(total)

    returned = jnp.concatenate([returned_ref[k] for k in range(step // cap)], axis=1)
    total[...] += scatter_columns(returned, receivers_ref[...], count)

    @pl.when(pl.program_id(0) == pl.num_programs(0) - 1)
    def _():
        sent, got = unstack(sent_ref[...]), unstack(total[...])
        nodes = nodes_ref[...]
        out_ref[...] = (
            part_ref[...]
            + split_dot(w1_ref[rows : 2 * rows, :], sent)
            + split_dot(w1_ref[2 * rows :, :], got)
        ).astype(BF16)
        rest_ref[:rows, :] = split_dot_nt(nodes, sent)
        rest_ref[rows:, :] = split_dot_nt(nodes, got)


def finish(returned, receivers, nodes, part, sent, w1, step):
    owners, rows, cap = returned.shape
    count = nodes.shape[1]
    slots = receivers.shape[1]
    whole = lambda a: pl.BlockSpec(a.shape, lambda i: (0,) * len(a.shape))
    outs = [
        jax.ShapeDtypeStruct((rows, count), BF16),
        jax.ShapeDtypeStruct((2 * rows, rows), F32),
    ]
    return pl.pallas_call(
        functools.partial(finish_kernel, cap),
        grid=(slots // step,),
        in_specs=[
            pl.BlockSpec((step // cap, rows, cap), lambda i: (i, 0, 0)),
            pl.BlockSpec((1, step), lambda i: (0, i)),
            *(whole(a) for a in (nodes, part, sent, w1)),
        ],
        out_specs=[whole(o) for o in outs],
        out_shape=outs,
        scratch_shapes=[pltpu.VMEM((rows * (count // LOW), LOW), F32)],
        compiler_params=pltpu.CompilerParams(vmem_limit_bytes=VMEM_LIMIT),
        name="sum_and_finish",
    )(returned, receivers, nodes, part, sent, w1)


def exchange(blocks):
    return lax.all_to_all(blocks, "edge", split_axis=0, concat_axis=0, tiled=True)


def per_device(
    nodes, edges, target, senders, receivers, counts, levels, land, channel_mask,
    edge_in, edge_in_bias, edge_out, edge_out_bias, edge_gain, edge_shift,
    node_in, node_in_bias, node_out, node_out_bias, node_gain, node_shift,
):
    rows, count = nodes.shape
    slots = edges.shape[1]
    owners = lax.axis_size("edge")
    step = min(2048, slots)
    levels_count = channel_mask.shape[0]
    cols = jnp.stack(
        [
            v.astype(F32)
            for v in (
                edge_in_bias, edge_out_bias, edge_gain, edge_shift,
                node_in_bias, node_out_bias, node_gain, node_shift,
                *(channel_mask[l] for l in range(levels_count)),
            )
        ],
        axis=1,
    )
    senders, receivers = senders.reshape(1, slots), receivers.reshape(1, slots)
    levels, land = levels.reshape(1, count), land.reshape(1, count)
    got = exchange(gather_for_owners(nodes, receivers, owners, step))
    message, pre, normal, inverse = edge_forward(
        counts, nodes, edges, got, senders, edge_in, edge_out, cols, step
    )
    new_nodes, part, agg_grad, node_first, node_second, node_vec = node_step(
        exchange(message), receivers, nodes, target, levels, land, node_in, node_out, cols,
        levels_count, step,
    )
    back = exchange(gather_for_owners(agg_grad, receivers, owners, step))
    edge_grad, pre_grad, sent, pair, edge_vec = edge_backward(
        counts, back, edges, pre, normal, inverse, senders, edge_in, edge_out, cols, count, step
    )
    node_grad, rest = finish(exchange(pre_grad), receivers, nodes, part, sent, edge_in, step)
    left = jnp.concatenate([pair[:rows, :rows], rest, pair[rows:, rows:]], axis=0)
    right = jnp.concatenate(
        [node_first, node_second, jnp.pad(jnp.concatenate([edge_vec, node_vec], 1), ((0, 0), (0, rows - 8)))],
        axis=0,
    )
    summed = lax.psum(jnp.concatenate([left, right], axis=1), ("edge", "rep"))
    left, right = summed[:, :rows], summed[:, rows:]
    vec = right[3 * rows :, :]
    return (
        new_nodes, node_grad, edge_grad,
        left[: 3 * rows], vec[:, 0], left[3 * rows :], vec[:, 1], vec[:, 2], vec[:, 3],
        right[: 2 * rows], vec[:, 4], right[2 * rows : 3 * rows], vec[:, 5], vec[:, 6], vec[:, 7],
    )


def solution(mesh):
    over = ("edge", "rep")
    wide, line, same = P(None, over), P(over), P()
    return jax.shard_map(
        per_device,
        mesh=mesh,
        in_specs=(wide, wide, wide, line, line, line, line, line) + (same,) * 13,
        out_specs=(wide, wide, wide) + (same,) * 12,
        check_vma=False,
    )
```

```python
import functools

import jax
import jax.numpy as jnp
from jax import lax
from jax.experimental import pallas as pl
from jax.experimental.pallas import tpu as pltpu
from jax.sharding import PartitionSpec as P

NORM_EPS = 1e-05
F32 = jnp.float32
BF16 = jnp.bfloat16
LOW = 256
VMEM_LIMIT = 60 * 2**20
PLANES = 4
MESH = pl.DeviceIdType.MESH

EB1, EB2, EG, EH, NB1, NB2, NG, NH, CM = 0, 1, 2, 3, 4, 5, 6, 7, 8


def dot(a, b):
    return jnp.dot(a, b, preferred_element_type=F32)


def dot_tn(a, b):
    return lax.dot_general(a, b, (((0,), (0,)), ((), ())), preferred_element_type=F32)


def dot_nt(a, b):
    return lax.dot_general(a, b, (((1,), (1,)), ((), ())), preferred_element_type=F32)


def one_hot_low(ids):
    low = ids & (LOW - 1)
    rows = lax.broadcasted_iota(jnp.int32, (LOW, ids.shape[1]), 0)
    return (rows == low).astype(F32).astype(BF16)


def high_of(ids, rows):
    high = ids >> (LOW.bit_length() - 1)
    return jnp.broadcast_to(high.astype(F32).astype(BF16), (rows, ids.shape[1]))


def stack_table(table_ref, value):
    rows = value.shape[0]
    for h in range(value.shape[1] // LOW):
        table_ref[h * rows : (h + 1) * rows, :] = value[:, h * LOW : (h + 1) * LOW]


def gather_columns(table, ids, rows):
    picked = dot(table, one_hot_low(ids)).astype(BF16)
    high = high_of(ids, rows)
    out = picked[:rows]
    for h in range(1, table.shape[0] // rows):
        out = jnp.where(high == BF16(h), picked[h * rows : (h + 1) * rows], out)
    return out


def scatter_columns(values, ids, count):
    rows = values.shape[0]
    high = high_of(ids, rows)
    zero = jnp.zeros_like(values)
    spread = jnp.concatenate(
        [jnp.where(high == BF16(h), values, zero) for h in range(count // LOW)], axis=0
    )
    return dot_nt(spread, one_hot_low(ids))


def column(cols, index):
    return cols[:, index : index + 1]


def mean_rows(v):
    return jnp.mean(v, axis=0, keepdims=True)


def lane_sums(v):
    out = v[:, :128]
    for k in range(1, v.shape[1] // 128):
        out = out + v[:, k * 128 : (k + 1) * 128]
    return out


def branch_forward(w1, w2, b1, b2, stacked):
    pre = dot_tn(w1, stacked) + b1
    hidden = (pre * (1.0 / (1.0 + jnp.exp(-pre)))).astype(BF16)
    outer = dot_tn(w2, hidden) + b2
    shifted = outer - mean_rows(outer)
    inverse = lax.rsqrt(mean_rows(shifted * shifted) + NORM_EPS)
    return pre, hidden, shifted * inverse, inverse


def branch_backward(w2, gain, grad, pre, normal, inverse):
    q = grad * gain
    outer_grad = (
        inverse * (q - mean_rows(q) - normal * mean_rows(q * normal))
    ).astype(BF16)
    s = 1.0 / (1.0 + jnp.exp(-pre))
    pre_grad = (dot(w2, outer_grad) * (s * (1.0 + pre * (1.0 - s)))).astype(BF16)
    return outer_grad, pre_grad, (pre * s).astype(BF16)


def split_dot(low, wide):
    top = wide.astype(BF16)
    rest = (wide - top.astype(F32)).astype(BF16)
    return dot(low, top) + dot(low, rest)


def layer_kernel(
    levels_count, reps,
    counts, nodes, edges, target, senders, receivers, levels, land, ew1, ew2, nw1, nw2, cols,
    new_nodes, node_grad, edge_grad, summed,
    tabs, send_a, recv_a, sent, ids_tab, pre_s, normal_s, inverse_s, send_b, recv_b, total,
    recv_c, recv_d, part, grads, sums, pieces,
    tab_send, tab_recv, ids_send, ids_recv, a_send, a_recv, b_send, b_recv,
    piece_send, piece_recv, sum_send, sum_recv,
):
    rows, count = nodes.shape
    owners, cap = senders.shape[0], senders.shape[2]
    ring = owners // PLANES
    high_count = count // LOW
    chunks = tab_recv.shape[2]
    chunk = tabs.shape[2] // chunks
    e, rep = lax.axis_index("edge"), lax.axis_index("rep")
    z, r = e // ring, e % ring
    me, devices = e * reps + rep, owners * reps
    upper = z // 2
    order = (z, z + 1 - 2 * upper, 2 - 2 * z + 5 * upper, 3 - 3 * upper)
    middle = lax.rem(z, 3) != 0
    toward = 3 - 2 * z

    def at(plane, place):
        return (plane * ring + place, rep)

    def remote(src, dst, send, recv, device):
        return pltpu.make_async_remote_copy(
            src, dst, send, recv, device_id=device, device_id_type=MESH
        )

    def loop(low, high, body):
        def step(i, carry):
            body(i)
            return carry

        lax.fori_loop(low, high, step, 0)

    def others(body):
        def one(t):
            d = lax.rem(me + t, devices)
            body(d, (d // reps, lax.rem(d, reps)))

        loop(1, devices, one)

    barrier = pltpu.get_barrier_semaphore()
    others(
        lambda d, device: pl.semaphore_signal(
            barrier, inc=1, device_id=device, device_id_type=MESH
        )
    )
    pl.semaphore_wait(barrier, devices - 1)

    def part_of(phase, plane, c):
        return tabs.at[phase, plane, pl.ds(c * chunk, chunk)]

    def table_copy(phase, plane, c, lane, to):
        return remote(
            part_of(phase, plane, c), part_of(phase, plane, c),
            tab_send.at[phase, lane, c], tab_recv.at[phase, plane, c], at(to, r),
        )

    def await_table(phase, plane, c):
        table_copy(phase, plane, c, 0, z).wait_recv()

    def send_own(phase, c):
        @pl.when(z < PLANES - 1)
        def _():
            table_copy(phase, z, c, 0, z + 1).start()

        @pl.when(z > 0)
        def _():
            table_copy(phase, z, c, 1, z - 1).start()

    def relay(phase, slot):
        @pl.when(middle)
        def _():
            for c in range(chunks):
                if slot == 0:
                    await_table(phase, z - toward, c)
                    table_copy(phase, z - toward, c, 2, z + toward).start()
                    await_table(phase, z + toward, c)
                    table_copy(phase, z + toward, c, 3, z - toward).start()
                else:
                    await_table(phase, z + 2 * toward, c)
                    table_copy(phase, z + 2 * toward, c, 4, z - toward).start()

    def end_wait(phase, k):
        @pl.when(jnp.logical_not(middle))
        def _():
            for c in range(chunks):
                await_table(phase, order[k], c)

    def drain_tables(phase):
        for c in range(chunks):
            @pl.when(z < PLANES - 1)
            def _():
                table_copy(phase, z, c, 0, z + 1).wait_send()

            @pl.when(z > 0)
            def _():
                table_copy(phase, z, c, 1, z - 1).wait_send()

            @pl.when(middle)
            def _():
                table_copy(phase, z - toward, c, 2, z + toward).wait_send()
                table_copy(phase, z + toward, c, 3, z - toward).wait_send()
                table_copy(phase, z + 2 * toward, c, 4, z - toward).wait_send()

    def ids_copy(k):
        plane = lax.rem(z + k, PLANES)
        return remote(
            receivers.at[pl.ds(plane * ring, ring)], ids_tab.at[pl.ds(z * ring, ring)],
            ids_send.at[plane], ids_recv.at[z], at(plane, r),
        )

    def ids_arrival(plane):
        rows_of = pl.ds(plane * ring, ring)
        return remote(
            ids_tab.at[rows_of], ids_tab.at[rows_of], ids_send.at[plane], ids_recv.at[plane],
            at(plane, r),
        )

    def plane_copy(phase, plane, to, into):
        return remote(
            send_a.at[plane * ring + to], into.at[plane * ring + r],
            a_send.at[phase, plane * ring + to], a_recv.at[phase, plane * ring + r], at(z, to),
        )

    def plane_arrival(phase, j, into):
        return remote(
            send_a.at[j], into.at[j], a_send.at[phase, j], a_recv.at[phase, j], at(z, r)
        )

    def gather_step(phase, k, into):
        plane = order[k]

        def one(t):
            to = lax.rem(r + t, ring)
            got = gather_columns(tabs[phase, plane], ids_tab[plane * ring + to], rows)

            @pl.when(t < ring)
            def _():
                send_a[plane * ring + to] = got
                plane_copy(phase, plane, to, into).start()

            @pl.when(t == ring)
            def _():
                into[plane * ring + r] = got

        loop(1, ring + 1, one)

    def drain_planes(phase, into):
        for plane in range(PLANES):
            loop(1, ring, lambda t: plane_copy(phase, plane, lax.rem(r + t, ring), into).wait_send())

    def direct_copy(phase, j, into):
        return remote(
            send_b.at[phase, j], into.at[e], b_send.at[phase, j], b_recv.at[phase, e], (j, rep)
        )

    def direct_arrival(phase, a, into):
        return remote(
            send_b.at[phase, a], into.at[a], b_send.at[phase, a], b_recv.at[phase, a], (e, rep)
        )

    def edge_step(phase, k, arrived, into, block):
        plane = order[k]

        def one(t):
            j = plane * ring + lax.rem(r + ring - t, ring)

            @pl.when(t > 0)
            def _():
                plane_arrival(phase, j, arrived).wait_recv()

            out = block(j)
            if k == 0:
                @pl.when(t == 0)
                def _():
                    into[e] = out

                @pl.when(t > 0)
                def _():
                    send_b[phase, j] = out
                    direct_copy(phase, j, into).start()
            else:
                send_b[phase, j] = out
                direct_copy(phase, j, into).start()

        loop(0, ring, one)

    def sum_arrived(phase, into):
        for k in range(PLANES):
            plane = order[k]

            def one(t):
                a = plane * ring + lax.rem(r + ring - t, ring)
                if k == 0:
                    @pl.when(t > 0)
                    def _():
                        direct_arrival(phase, a, into).wait_recv()
                else:
                    direct_arrival(phase, a, into).wait_recv()
                total[...] += scatter_columns(into[a], receivers[a], count)

            loop(0, ring, one)

    def drain_direct(phase, into):
        loop(1, owners, lambda t: direct_copy(phase, lax.rem(e + t, owners), into).wait_send())

    packed = cols[...]

    def lanes(j):
        return pl.ds(pl.multiple_of(j * cap, cap), cap)

    def live_of(j):
        place = lax.broadcasted_iota(jnp.int32, (1, cap), 1)
        return (place < counts[j]).astype(F32)

    def edge_forward(j):
        own = edges[:, lanes(j)]
        pre, _, normal, inverse = branch_forward(
            ew1[...], ew2[...], column(packed, EB1), column(packed, EB2),
            jnp.concatenate([own, sent[j], recv_a[j]], axis=0),
        )
        pre_s[j] = pre
        normal_s[j] = normal
        inverse_s[j] = inverse
        updated = own.astype(F32) + (normal * column(packed, EG) + column(packed, EH))
        return (updated * live_of(j)).astype(BF16)

    def edge_backward(j):
        grad = recv_c[j].astype(F32) * live_of(j)
        normal = normal_s[j]
        outer_grad, pre_grad, hidden = branch_backward(
            ew2[...], column(packed, EG), grad, pre_s[j], normal, inverse_s[j]
        )
        own = edges[:, lanes(j)]
        edge_grad[:, lanes(j)] = (grad + dot(ew1[:rows, :], pre_grad)).astype(BF16)
        grads[...] += dot_nt(
            jnp.concatenate([own, sent[j], recv_a[j], hidden], axis=0),
            jnp.concatenate([pre_grad, outer_grad], axis=0),
        )
        for k, v in enumerate((pre_grad.astype(F32), outer_grad.astype(F32), grad * normal, grad)):
            sums[k] += lane_sums(v)
        return pre_grad

    stack_table(tabs.at[0, z], nodes[...])
    for c in range(chunks):
        send_own(0, c)
    for k in range(1, PLANES):
        ids_copy(k).start()
    ids_tab[pl.ds(z * ring, ring)] = receivers[pl.ds(z * ring, ring)]
    total[...] = jnp.zeros_like(total)
    grads[...] = jnp.zeros_like(grads)
    sums[...] = jnp.zeros_like(sums)

    def senders_of(low, high):
        def one(j):
            sent[j] = gather_columns(tabs[0, z], senders[j], rows)

        loop(low, high, one)

    gather_step(0, 0, recv_a)
    senders_of(0, owners // 2)
    relay(0, 0)
    for k in range(1, PLANES):
        ids_arrival(order[k]).wait_recv()
    end_wait(0, 1)
    gather_step(0, 1, recv_a)
    senders_of(owners // 2, owners)
    edge_step(0, 0, recv_a, recv_b, edge_forward)
    relay(0, 1)
    end_wait(0, 2)
    gather_step(0, 2, recv_a)
    edge_step(0, 1, recv_a, recv_b, edge_forward)
    end_wait(0, 3)
    gather_step(0, 3, recv_a)
    edge_step(0, 2, recv_a, recv_b, edge_forward)
    edge_step(0, 3, recv_a, recv_b, edge_forward)
    for k in range(1, PLANES):
        ids_copy(k).wait_send()
    drain_planes(0, recv_a)
    sum_arrived(0, recv_b)

    per = high_count // chunks
    wide = per * LOW
    node_first = jnp.zeros((2 * rows, rows), F32)
    node_second = jnp.zeros((rows, rows), F32)
    node_sums = [jnp.zeros((rows, 128), F32)] * 4
    for c in range(chunks):
        here = slice(c * wide, (c + 1) * wide)
        aggregate = jnp.concatenate(
            [total[h * rows : (h + 1) * rows, :] for h in range(c * per, (c + 1) * per)], axis=1
        ).astype(BF16)
        own = nodes[:, here]
        stacked = jnp.concatenate([own, aggregate], axis=0)
        pre, _, normal, inverse = branch_forward(
            nw1[...], nw2[...], column(packed, NB1), column(packed, NB2), stacked
        )
        gain = column(packed, NG)
        state = own.astype(F32) + (normal * gain + column(packed, NH))
        new_nodes[:, here] = state.astype(BF16)
        weight = jnp.zeros((rows, wide), F32)
        for l in range(levels_count):
            weight = jnp.where(levels[:, here] == l, column(packed, CM + l), weight)
        weight = weight * land[:, here].astype(F32)
        grad = weight * (state - target[:, here].astype(F32))
        outer_grad, pre_grad, hidden = branch_backward(nw2[...], gain, grad, pre, normal, inverse)
        stacked_grad = dot(nw1[...], pre_grad)
        part[:, here] = grad + stacked_grad[:rows]
        low = stacked_grad[rows:].astype(BF16)
        for h in range(per):
            tabs[1, z, (c * per + h) * rows : (c * per + h + 1) * rows, :] = low[
                :, h * LOW : (h + 1) * LOW
            ]
        send_own(1, c)
        node_first = node_first + dot_nt(stacked, pre_grad)
        node_second = node_second + dot_nt(hidden, outer_grad)
        for k, v in enumerate((pre_grad.astype(F32), outer_grad.astype(F32), grad * normal, grad)):
            node_sums[k] = node_sums[k] + lane_sums(v)
    total[...] = jnp.zeros_like(total)

    gather_step(1, 0, recv_c)
    relay(1, 0)
    end_wait(1, 1)
    gather_step(1, 1, recv_c)
    edge_step(1, 0, recv_c, recv_d, edge_backward)
    relay(1, 1)
    end_wait(1, 2)
    gather_step(1, 2, recv_c)
    edge_step(1, 1, recv_c, recv_d, edge_backward)
    end_wait(1, 3)
    gather_step(1, 3, recv_c)
    edge_step(1, 2, recv_c, recv_d, edge_backward)
    edge_step(1, 3, recv_c, recv_d, edge_backward)

    grads[: 2 * rows, rows:] = node_first
    grads[2 * rows : 3 * rows, rows:] = node_second
    grads[3 * rows :, :8] = jnp.concatenate(
        [sums[k].sum(axis=1, keepdims=True) for k in range(4)]
        + [v.sum(axis=1, keepdims=True) for v in node_sums],
        axis=1,
    )
    reducers = min(devices, grads.shape[0] // 8)
    height = grads.shape[0] // reducers

    def piece(d):
        return pl.ds(pl.multiple_of(d * height, 8), height)

    def piece_copy(d, device):
        return remote(
            grads.at[piece(d)], pieces.at[me], piece_send.at[d], piece_recv.at[me], device
        )

    def piece_arrival(d):
        return remote(
            grads.at[piece(0)], pieces.at[d], piece_send.at[0], piece_recv.at[d], (e, rep)
        )

    def sum_copy(d, device):
        return remote(
            summed.at[piece(me)], summed.at[piece(me)], sum_send.at[d], sum_recv.at[me], device
        )

    def sum_arrival(d):
        return remote(
            summed.at[piece(d)], summed.at[piece(d)], sum_send.at[0], sum_recv.at[d], (e, rep)
        )

    def to_reducers(body):
        def one(d, device):
            if reducers == devices:
                body(d, device)
            else:
                @pl.when(d < reducers)
                def _():
                    body(d, device)

        others(one)

    def as_reducer(body):
        if reducers == devices:
            body()
        else:
            pl.when(me < reducers)(body)

    to_reducers(lambda d, device: piece_copy(d, device).start())

    def by_sender(j):
        @pl.when(j != e)
        def _():
            total[...] += scatter_columns(send_b[1, j], senders[j], count)

        @pl.when(j == e)
        def _():
            total[...] += scatter_columns(recv_d[e], senders[j], count)

    loop(0, owners, by_sender)

    @as_reducer
    def _():
        pieces[me] = grads[piece(me), :]
        others(lambda d, device: piece_arrival(d).wait_recv())

        def add(d, running):
            return running + pieces[d]

        summed[piece(me), :] = lax.fori_loop(
            1, devices, add, pieces[0]
        )
        others(lambda d, device: sum_copy(d, device).start())

    def node_total(w_rows):
        for h in range(high_count):
            here = slice(h * LOW, (h + 1) * LOW)
            part[:, here] += split_dot(ew1[w_rows, :], total[h * rows : (h + 1) * rows, :])

    node_total(slice(rows, 2 * rows))
    total[...] = jnp.zeros_like(total)
    sum_arrived(1, recv_d)
    node_total(slice(2 * rows, 3 * rows))
    node_grad[...] = part[...].astype(BF16)

    drain_tables(0)
    drain_direct(0, recv_b)
    drain_tables(1)
    drain_planes(1, recv_c)
    drain_direct(1, recv_d)
    to_reducers(lambda d, device: piece_copy(d, device).wait_send())

    @as_reducer
    def _():
        others(lambda d, device: sum_copy(d, device).wait_send())

    to_reducers(lambda d, device: sum_arrival(d).wait_recv())


def layer(
    counts, nodes, edges, target, senders, receivers, levels, land, ew1, ew2, nw1, nw2, cols,
    levels_count,
):
    rows, count = nodes.shape
    owners, _, cap = senders.shape
    slots = edges.shape[1]
    reps = lax.axis_size("rep")
    devices = owners * reps
    chunks = 4 if count // LOW % 4 == 0 else 1
    ring = owners // PLANES
    grad_shape = (4 * rows, 2 * rows)
    reducers = min(devices, grad_shape[0] // 8)
    blocks = (owners, rows, cap)
    dma = pltpu.SemaphoreType.DMA
    vmem = pl.BlockSpec(memory_space=pltpu.VMEM)
    return pl.pallas_call(
        functools.partial(layer_kernel, levels_count, reps),
        in_specs=[pl.BlockSpec(memory_space=pltpu.SMEM)] + [vmem] * 12,
        out_specs=[vmem] * 4,
        out_shape=[
            jax.ShapeDtypeStruct((rows, count), BF16),
            jax.ShapeDtypeStruct((rows, count), BF16),
            jax.ShapeDtypeStruct((rows, slots), BF16),
            jax.ShapeDtypeStruct(grad_shape, F32),
        ],
        scratch_shapes=[
            pltpu.VMEM((2, PLANES, rows * (count // LOW), LOW), BF16),
            pltpu.VMEM(blocks, BF16),
            pltpu.VMEM(blocks, BF16),
            pltpu.VMEM(blocks, BF16),
            pltpu.VMEM((owners, 1, cap), jnp.int32),
            pltpu.VMEM(blocks, F32),
            pltpu.VMEM(blocks, F32),
            pltpu.VMEM((owners, 1, cap), F32),
            pltpu.VMEM((2,) + blocks, BF16),
            pltpu.VMEM(blocks, BF16),
            pltpu.VMEM((rows * (count // LOW), LOW), F32),
            pltpu.VMEM(blocks, BF16),
            pltpu.VMEM(blocks, BF16),
            pltpu.VMEM((rows, count), F32),
            pltpu.VMEM(grad_shape, F32),
            pltpu.VMEM((4, rows, 128), F32),
            pltpu.VMEM((devices, grad_shape[0] // reducers, grad_shape[1]), F32),
            dma((2, 5, chunks)),
            dma((2, PLANES, chunks)),
            dma((PLANES,)),
            dma((PLANES,)),
            dma((2, owners)),
            dma((2, owners)),
            dma((2, owners)),
            dma((2, owners)),
            dma((reducers,)),
            dma((devices,)),
            dma((devices,)),
            dma((reducers,)),
        ],
        compiler_params=pltpu.CompilerParams(
            vmem_limit_bytes=VMEM_LIMIT, collective_id=0, has_side_effects=True
        ),
        cost_estimate=pl.CostEstimate(
            flops=64 * 2**30, bytes_accessed=16 * 2**20, transcendentals=4 * 2**20
        ),
        name="layer",
    )(counts, nodes, edges, target, senders, receivers, levels, land, ew1, ew2, nw1, nw2, cols)


def unpack_kernel(packed, *outs):
    rows = packed.shape[1] // 2
    lines = packed[3 * rows :, :].T
    edge_first, edge_b1, edge_second, edge_b2, edge_g, edge_h = outs[:6]
    node_first, node_b1, node_second, node_b2, node_g, node_h = outs[6:]
    edge_first[...] = packed[: 3 * rows, :rows]
    edge_second[...] = packed[3 * rows :, rows:]
    node_first[...] = packed[: 2 * rows, rows:]
    node_second[...] = packed[2 * rows : 3 * rows, rows:]
    for k, out in enumerate((edge_b1, edge_b2, edge_g, edge_h, node_b1, node_b2, node_g, node_h)):
        out[...] = lines[k, :rows]


def unpack(packed):
    rows = packed.shape[1] // 2
    vmem = pl.BlockSpec(memory_space=pltpu.VMEM)
    shapes = [
        (3 * rows, rows), (rows,), (rows, rows), (rows,), (rows,), (rows,),
        (2 * rows, rows), (rows,), (rows, rows), (rows,), (rows,), (rows,),
    ]
    return pl.pallas_call(
        unpack_kernel,
        in_specs=[vmem],
        out_specs=[vmem] * len(shapes),
        out_shape=[jax.ShapeDtypeStruct(s, F32) for s in shapes],
        name="unpack",
    )(packed)


def per_device(
    nodes, edges, target, senders, receivers, counts, levels, land, channel_mask,
    edge_in, edge_in_bias, edge_out, edge_out_bias, edge_gain, edge_shift,
    node_in, node_in_bias, node_out, node_out_bias, node_gain, node_shift,
):
    rows, count = nodes.shape
    slots = edges.shape[1]
    owners = lax.axis_size("edge")
    cap = slots // owners
    levels_count = channel_mask.shape[0]
    cols = jnp.stack(
        [
            v.astype(F32)
            for v in (
                edge_in_bias, edge_out_bias, edge_gain, edge_shift,
                node_in_bias, node_out_bias, node_gain, node_shift,
                *(channel_mask[l] for l in range(levels_count)),
            )
        ],
        axis=1,
    )
    new_nodes, node_grad, edge_grad, packed = layer(
        counts, nodes, edges, target,
        senders.reshape(owners, 1, cap), receivers.reshape(owners, 1, cap),
        levels.reshape(1, count), land.reshape(1, count),
        edge_in, edge_out, node_in, node_out, cols, levels_count,
    )
    return (new_nodes, node_grad, edge_grad, *unpack(packed))


def solution(mesh):
    over = ("edge", "rep")
    wide, line, same = P(None, over), P(over), P()
    return jax.shard_map(
        per_device,
        mesh=mesh,
        in_specs=(wide, wide, wide, line, line, line, line, line) + (same,) * 13,
        out_specs=(wide, wide, wide) + (same,) * 12,
        check_vma=False,
    )
```

```python
import functools

import jax
import jax.numpy as jnp
from jax import lax
from jax.experimental import pallas as pl
from jax.experimental.pallas import tpu as pltpu
from jax.sharding import PartitionSpec as P

NORM_EPS = 1e-05
F32 = jnp.float32
BF16 = jnp.bfloat16
LOW = 256
VMEM_LIMIT = 60 * 2**20
PLANES = 4
MESH = pl.DeviceIdType.MESH

EB1, EB2, EG, EH, NB1, NB2, NG, NH, CM = 0, 1, 2, 3, 4, 5, 6, 7, 8


def dot(a, b):
    return jnp.dot(a, b, preferred_element_type=F32)


def dot_tn(a, b):
    return lax.dot_general(a, b, (((0,), (0,)), ((), ())), preferred_element_type=F32)


def dot_nt(a, b):
    return lax.dot_general(a, b, (((1,), (1,)), ((), ())), preferred_element_type=F32)


def one_hot_low(ids):
    low = ids & (LOW - 1)
    rows = lax.broadcasted_iota(jnp.int32, (LOW, ids.shape[1]), 0)
    return (rows == low).astype(F32).astype(BF16)


def high_of(ids, rows):
    high = ids >> (LOW.bit_length() - 1)
    return jnp.broadcast_to(high.astype(F32).astype(BF16), (rows, ids.shape[1]))


def stack_table(table_ref, value):
    rows = value.shape[0]
    for h in range(value.shape[1] // LOW):
        table_ref[h * rows : (h + 1) * rows, :] = value[:, h * LOW : (h + 1) * LOW]


def gather_columns(table, ids, rows):
    picked = dot(table, one_hot_low(ids)).astype(BF16)
    high = high_of(ids, rows)
    out = picked[:rows]
    for h in range(1, table.shape[0] // rows):
        out = jnp.where(high == BF16(h), picked[h * rows : (h + 1) * rows], out)
    return out


def scatter_columns(values, ids, count):
    rows = values.shape[0]
    high = high_of(ids, rows)
    zero = jnp.zeros_like(values)
    spread = jnp.concatenate(
        [jnp.where(high == BF16(h), values, zero) for h in range(count // LOW)], axis=0
    )
    return dot_nt(spread, one_hot_low(ids))


def column(cols, index):
    return cols[:, index : index + 1]


def mean_rows(v):
    return jnp.mean(v, axis=0, keepdims=True)


def lane_sums(v):
    out = v[:, :128]
    for k in range(1, v.shape[1] // 128):
        out = out + v[:, k * 128 : (k + 1) * 128]
    return out


def branch_forward(w1t, w2t, b1, b2, stacked):
    pre = dot(w1t, stacked) + b1
    hidden = (pre * (1.0 / (1.0 + jnp.exp(-pre)))).astype(BF16)
    outer = dot(w2t, hidden) + b2
    shifted = outer - mean_rows(outer)
    inverse = lax.rsqrt(mean_rows(shifted * shifted) + NORM_EPS)
    return pre, shifted * inverse, inverse


def branch_backward(w2, gain, grad, pre, normal, inverse):
    q = grad * gain
    outer_grad = (
        inverse * (q - mean_rows(q) - normal * mean_rows(q * normal))
    ).astype(BF16)
    s = 1.0 / (1.0 + jnp.exp(-pre))
    pre_grad = (dot(w2, outer_grad) * (s * (1.0 + pre * (1.0 - s)))).astype(BF16)
    return outer_grad, pre_grad, (pre * s).astype(BF16)


def split_dot(low, wide):
    top = wide.astype(BF16)
    rest = (wide - top.astype(F32)).astype(BF16)
    return dot(low, top) + dot(low, rest)


def layer_kernel(
    levels_count, reps,
    counts, nodes, edges, target, senders, receivers, levels, land, masks, ew1t, ew2, nw1t, nw2,
    eb1, eb2, eg, eh, nb1, nb2, ng, nh,
    new_nodes, node_grad, edge_grad, summed,
    tabs, send_a, recv_s, recv_e, mine, ids_tab, count_send, count_recv, pre_s, normal_s,
    inverse_s, recv_c, send_d, recv_d, total, part, grads, sums, pieces, ew1, ew2t, nw1, nw2t, cols,
    tab_send, tab_recv, ids_send, ids_recv, a_send, a_recv, b_send, b_recv, count_out, count_in,
    piece_send, piece_recv, sum_send, sum_recv,
):
    rows, count = nodes.shape
    owners, cap = senders.shape[0], senders.shape[2]
    ring = owners // PLANES
    high_count = count // LOW
    chunks = tab_recv.shape[2]
    chunk = tabs.shape[2] // chunks
    e, rep = lax.axis_index("edge"), lax.axis_index("rep")
    z, r = e // ring, e % ring
    me, devices = e * reps + rep, owners * reps
    upper = z // 2
    order = (z, z + 1 - 2 * upper, 2 - 2 * z + 5 * upper, 3 - 3 * upper)
    middle = lax.rem(z, 3) != 0
    toward = 3 - 2 * z

    def at(plane, place):
        return (plane * ring + place, rep)

    def remote(src, dst, send, recv, device):
        return pltpu.make_async_remote_copy(
            src, dst, send, recv, device_id=device, device_id_type=MESH
        )

    def loop(low, high, body):
        def step(i, carry):
            body(i)
            return carry

        lax.fori_loop(low, high, step, 0)

    def others(body):
        def one(t):
            d = lax.rem(me + t, devices)
            body(d, (d // reps, lax.rem(d, reps)))

        loop(1, devices, one)

    barrier = pltpu.get_barrier_semaphore()
    others(
        lambda d, device: pl.semaphore_signal(
            barrier, inc=1, device_id=device, device_id_type=MESH
        )
    )

    def eye(n):
        return (
            lax.broadcasted_iota(jnp.int32, (n, n), 0) == lax.broadcasted_iota(jnp.int32, (n, n), 1)
        ).astype(F32).astype(BF16)

    unit = eye(rows)
    ew1[...] = dot_tn(ew1t[...], unit).astype(BF16)
    nw1[...] = dot_tn(nw1t[...], unit).astype(BF16)
    ew2t[...] = dot_tn(ew2[...], unit).astype(BF16)
    nw2t[...] = dot_tn(nw2[...], unit).astype(BF16)
    lines = [v[...].astype(F32)[None, :] for v in (eb1, eb2, eg, eh, nb1, nb2, ng, nh)]
    lines.append(masks[...].astype(F32))
    lines.append(jnp.zeros((-(8 + levels_count) % 16, rows), F32))
    cols[...] = dot_nt(unit, jnp.concatenate(lines, axis=0).astype(BF16))
    stack_table(tabs.at[0, z], nodes[...])
    for j in range(owners):
        count_send[j] = jnp.full(count_send.shape[1:], counts[j], jnp.int32)
    pl.semaphore_wait(barrier, devices - 1)

    def part_of(phase, plane, c):
        return tabs.at[phase, plane, pl.ds(c * chunk, chunk)]

    def table_copy(phase, plane, c, lane, to):
        return remote(
            part_of(phase, plane, c), part_of(phase, plane, c),
            tab_send.at[phase, lane, c], tab_recv.at[phase, plane, c], at(to, r),
        )

    def await_table(phase, plane, c):
        table_copy(phase, plane, c, 0, z).wait_recv()

    def send_own(phase, c):
        @pl.when(z < PLANES - 1)
        def _():
            table_copy(phase, z, c, 0, z + 1).start()

        @pl.when(z > 0)
        def _():
            table_copy(phase, z, c, 1, z - 1).start()

    def relay(phase, slot):
        @pl.when(middle)
        def _():
            for c in range(chunks):
                if slot == 0:
                    await_table(phase, z - toward, c)
                    table_copy(phase, z - toward, c, 2, z + toward).start()
                    await_table(phase, z + toward, c)
                    table_copy(phase, z + toward, c, 3, z - toward).start()
                else:
                    await_table(phase, z + 2 * toward, c)
                    table_copy(phase, z + 2 * toward, c, 4, z - toward).start()

    def end_wait(phase, k):
        @pl.when(jnp.logical_not(middle))
        def _():
            for c in range(chunks):
                await_table(phase, order[k], c)

    def drain_tables(phase):
        for c in range(chunks):
            @pl.when(z < PLANES - 1)
            def _():
                table_copy(phase, z, c, 0, z + 1).wait_send()

            @pl.when(z > 0)
            def _():
                table_copy(phase, z, c, 1, z - 1).wait_send()

            @pl.when(middle)
            def _():
                table_copy(phase, z - toward, c, 2, z + toward).wait_send()
                table_copy(phase, z + toward, c, 3, z - toward).wait_send()
                table_copy(phase, z + 2 * toward, c, 4, z - toward).wait_send()

    def ids_copy(phase, ids, k):
        plane = lax.rem(z + k, PLANES)
        return remote(
            ids.at[pl.ds(plane * ring, ring)], ids_tab.at[phase, pl.ds(z * ring, ring)],
            ids_send.at[phase, plane], ids_recv.at[phase, z], at(plane, r),
        )

    def ids_arrival(phase, plane):
        rows_of = ids_tab.at[phase, pl.ds(plane * ring, ring)]
        return remote(
            rows_of, rows_of, ids_send.at[phase, plane], ids_recv.at[phase, plane], at(plane, r)
        )

    def plane_copy(phase, plane, to, into):
        return remote(
            send_a.at[plane * ring + to], into.at[plane * ring + r],
            a_send.at[phase, plane * ring + to], a_recv.at[phase, plane * ring + r], at(z, to),
        )

    def plane_arrival(phase, j, into):
        return remote(
            send_a.at[j], into.at[j], a_send.at[phase, j], a_recv.at[phase, j], at(z, r)
        )

    def hand_over(phase, plane, to, t, got, into):
        @pl.when(t < ring)
        def _():
            send_a[plane * ring + to] = got
            plane_copy(phase, plane, to, into).start()

        @pl.when(t == ring)
        def _():
            into[plane * ring + r] = got

    def gather_step(phase, k, into):
        plane = order[k]

        def one(t):
            to = lax.rem(r + t, ring)
            got = gather_columns(tabs[phase, plane], ids_tab[phase, plane * ring + to], rows)
            hand_over(phase, plane, to, t, got, into)

        loop(1, ring + 1, one)

    def drain_planes(phase, into):
        for plane in range(PLANES):
            loop(1, ring, lambda t: plane_copy(phase, plane, lax.rem(r + t, ring), into).wait_send())

    def lanes(j):
        return pl.ds(pl.multiple_of(j * cap, cap), cap)

    def edges_copy(j):
        return remote(
            edges.at[:, lanes(j)], recv_e.at[e], b_send.at[0, j], b_recv.at[0, e], (j, rep)
        )

    def edges_arrival(a):
        return remote(
            edges.at[:, lanes(a)], recv_e.at[a], b_send.at[0, a], b_recv.at[0, a], (e, rep)
        )

    def count_copy(j):
        return remote(
            count_send.at[j], count_recv.at[e], count_out.at[j], count_in.at[e], (j, rep)
        )

    def count_arrival(a):
        return remote(
            count_send.at[a], count_recv.at[a], count_out.at[a], count_in.at[a], (e, rep)
        )

    def back_copy(a):
        return remote(
            send_d.at[a], recv_d.at[e], b_send.at[1, a], b_recv.at[1, e], (a, rep)
        )

    def back_arrival(j):
        return remote(
            send_d.at[j], recv_d.at[j], b_send.at[1, j], b_recv.at[1, j], (e, rep)
        )

    def peers(body):
        loop(1, owners, lambda t: body(lax.rem(e + t, owners)))

    def send_edges(k):
        def one(t):
            edges_copy(order[k] * ring + lax.rem(r + t, ring)).start()

        loop(1 if k == 0 else 0, ring, one)

    packed = cols[...]
    place = lax.broadcasted_iota(jnp.int32, (1, cap), 1)

    def live_here(a):
        line = count_recv[a]
        wide = jnp.concatenate([line] * (cap // line.shape[1]), axis=1)
        return (place < wide).astype(F32)

    def edge_forward(a):
        own = recv_e[a]
        pre, normal, inverse = branch_forward(
            ew1t[...], ew2t[...], column(packed, EB1), column(packed, EB2),
            jnp.concatenate([own, recv_s[a], mine[a]], axis=0),
        )
        pre_s[a] = pre
        normal_s[a] = normal
        inverse_s[a] = inverse
        updated = own.astype(F32) + (normal * column(packed, EG) + column(packed, EH))
        return (updated * live_here(a)).astype(BF16)

    def forward_step(k):
        def one(t):
            a = order[k] * ring + lax.rem(r + ring - t, ring)

            @pl.when(t > 0)
            def _():
                plane_arrival(0, a, recv_s).wait_recv()

            if k == 0:
                @pl.when(t > 0)
                def _():
                    count_arrival(a).wait_recv()
                    edges_arrival(a).wait_recv()
            else:
                count_arrival(a).wait_recv()
                edges_arrival(a).wait_recv()
            total[...] += scatter_columns(edge_forward(a), receivers[a], count)

        loop(0, ring, one)

    def edge_backward(a, got):
        grad = got.astype(F32) * live_here(a)
        normal = normal_s[a]
        outer_grad, pre_grad, hidden = branch_backward(
            ew2[...], column(packed, EG), grad, pre_s[a], normal, inverse_s[a]
        )
        grads[...] += dot_nt(
            jnp.concatenate([recv_e[a], recv_s[a], mine[a], hidden], axis=0),
            jnp.concatenate([pre_grad, outer_grad], axis=0),
        )
        for k, v in enumerate((pre_grad.astype(F32), outer_grad.astype(F32), grad * normal, grad)):
            sums[k] += lane_sums(v)
        return pre_grad

    def backward_step(k):
        plane = order[k]

        def one(t):
            to = lax.rem(r + t, ring)
            a = plane * ring + to
            got = gather_columns(tabs[1, z], receivers[a], rows)
            if k == 0:
                hand_over(1, z, to, t, got, recv_c)
            pre_grad = edge_backward(a, got)
            send_d[a] = pre_grad
            if k == 0:
                @pl.when(t < ring)
                def _():
                    back_copy(a).start()
            else:
                back_copy(a).start()

        loop(1, ring + 1, one)

    for c in range(chunks):
        send_own(0, c)
    for k in range(1, PLANES):
        ids_copy(0, senders, k).start()
    peers(lambda j: count_copy(j).start())
    send_edges(0)
    send_edges(1)
    ids_tab[0, pl.ds(z * ring, ring)] = senders[pl.ds(z * ring, ring)]
    count_recv[e] = count_send[e]
    recv_e[e] = edges[:, lanes(e)]
    total[...] = jnp.zeros_like(total)
    grads[...] = jnp.zeros_like(grads)
    sums[...] = jnp.zeros_like(sums)

    def mine_of(low, high):
        def one(a):
            mine[a] = gather_columns(tabs[0, z], receivers[a], rows)

        loop(low, high, one)

    gather_step(0, 0, recv_s)
    mine_of(0, owners // 2)
    relay(0, 0)
    for k in range(1, PLANES):
        ids_arrival(0, order[k]).wait_recv()
    end_wait(0, 1)
    gather_step(0, 1, recv_s)
    send_edges(2)
    mine_of(owners // 2, owners)
    relay(0, 1)
    end_wait(0, 2)
    gather_step(0, 2, recv_s)
    send_edges(3)
    forward_step(0)
    end_wait(0, 3)
    gather_step(0, 3, recv_s)
    for k in range(1, PLANES):
        ids_copy(1, receivers, k).start()
    for k in range(1, PLANES):
        forward_step(k)
    drain_planes(0, recv_s)

    per = high_count // chunks
    wide = per * LOW
    node_first = jnp.zeros((2 * rows, rows), F32)
    node_second = jnp.zeros((rows, rows), F32)
    node_sums = [jnp.zeros((rows, 128), F32)] * 4
    for c in range(chunks):
        here = slice(c * wide, (c + 1) * wide)
        aggregate = jnp.concatenate(
            [total[h * rows : (h + 1) * rows, :] for h in range(c * per, (c + 1) * per)], axis=1
        ).astype(BF16)
        own = nodes[:, here]
        stacked = jnp.concatenate([own, aggregate], axis=0)
        pre, normal, inverse = branch_forward(
            nw1t[...], nw2t[...], column(packed, NB1), column(packed, NB2), stacked
        )
        gain = column(packed, NG)
        state = own.astype(F32) + (normal * gain + column(packed, NH))
        new_nodes[:, here] = state.astype(BF16)
        weight = jnp.zeros((rows, wide), F32)
        for l in range(levels_count):
            weight = jnp.where(levels[:, here] == l, column(packed, CM + l), weight)
        weight = weight * land[:, here].astype(F32)
        grad = weight * (state - target[:, here].astype(F32))
        outer_grad, pre_grad, hidden = branch_backward(nw2[...], gain, grad, pre, normal, inverse)
        stacked_grad = dot(nw1[...], pre_grad)
        part[:, here] = grad + stacked_grad[:rows]
        low = stacked_grad[rows:].astype(BF16)
        for h in range(per):
            tabs[1, z, (c * per + h) * rows : (c * per + h + 1) * rows, :] = low[
                :, h * LOW : (h + 1) * LOW
            ]
        send_own(1, c)
        node_first = node_first + dot_nt(stacked, pre_grad)
        node_second = node_second + dot_nt(hidden, outer_grad)
        for k, v in enumerate((pre_grad.astype(F32), outer_grad.astype(F32), grad * normal, grad)):
            node_sums[k] = node_sums[k] + lane_sums(v)

    backward_step(0)
    backward_step(1)
    relay(1, 0)
    for k in range(1, PLANES):
        ids_arrival(1, order[k]).wait_recv()
    end_wait(1, 1)
    gather_step(1, 1, recv_c)
    backward_step(2)
    relay(1, 1)
    end_wait(1, 2)
    gather_step(1, 2, recv_c)
    backward_step(3)

    grads[: 2 * rows, rows:] = node_first
    grads[2 * rows : 3 * rows, rows:] = node_second
    grads[3 * rows :, :8] = jnp.concatenate(
        [sums[k].sum(axis=1, keepdims=True) for k in range(4)]
        + [v.sum(axis=1, keepdims=True) for v in node_sums],
        axis=1,
    )
    reducers = min(devices, grads.shape[0] // 8)
    height = grads.shape[0] // reducers

    def piece(d):
        return pl.ds(pl.multiple_of(d * height, 8), height)

    def piece_copy(d, device):
        return remote(
            grads.at[piece(d)], pieces.at[me], piece_send.at[d], piece_recv.at[me], device
        )

    def piece_arrival(d):
        return remote(
            grads.at[piece(0)], pieces.at[d], piece_send.at[0], piece_recv.at[d], (e, rep)
        )

    def sum_copy(d, device):
        return remote(
            summed.at[piece(me)], summed.at[piece(me)], sum_send.at[d], sum_recv.at[me], device
        )

    def sum_arrival(d):
        return remote(
            summed.at[piece(d)], summed.at[piece(d)], sum_send.at[0], sum_recv.at[d], (e, rep)
        )

    def to_reducers(body):
        def one(d, device):
            if reducers == devices:
                body(d, device)
            else:
                @pl.when(d < reducers)
                def _():
                    body(d, device)

        others(one)

    def as_reducer(body):
        if reducers == devices:
            body()
        else:
            pl.when(me < reducers)(body)

    to_reducers(lambda d, device: piece_copy(d, device).start())
    end_wait(1, 3)
    gather_step(1, 3, recv_c)

    total[...] = jnp.zeros_like(total)

    def by_receiver(a):
        total[...] += scatter_columns(send_d[a], receivers[a], count)

    loop(0, owners, by_receiver)

    def node_total(w_rows):
        for h in range(high_count):
            here = slice(h * LOW, (h + 1) * LOW)
            part[:, here] += split_dot(ew1[w_rows, :], total[h * rows : (h + 1) * rows, :])

    node_total(slice(2 * rows, 3 * rows))
    total[...] = jnp.zeros_like(total)

    @as_reducer
    def _():
        pieces[me] = grads[piece(me), :]
        others(lambda d, device: piece_arrival(d).wait_recv())

        def add(d, running):
            return running + pieces[d]

        summed[piece(me), :] = lax.fori_loop(1, devices, add, pieces[0])
        others(lambda d, device: sum_copy(d, device).start())

    def finish_block(j, pre_grad):
        grad = recv_c[j].astype(F32) * (place < counts[j]).astype(F32)
        edge_grad[:, lanes(j)] = (grad + dot(ew1[:rows, :], pre_grad)).astype(BF16)
        total[...] += scatter_columns(pre_grad, senders[j], count)

    finish_block(e, send_d[e])
    for k in range(PLANES):
        def one(t):
            j = order[k] * ring + lax.rem(r + ring - t, ring)
            if k == 0:
                plane_arrival(1, j, recv_c).wait_recv()
            else:
                @pl.when(t > 0)
                def _():
                    plane_arrival(1, j, recv_c).wait_recv()
            back_arrival(j).wait_recv()
            finish_block(j, recv_d[j])

        loop(1 if k == 0 else 0, ring, one)
    node_total(slice(rows, 2 * rows))
    node_grad[...] = part[...].astype(BF16)

    drain_tables(0)
    drain_tables(1)
    drain_planes(1, recv_c)
    for k in range(1, PLANES):
        ids_copy(0, senders, k).wait_send()
        ids_copy(1, receivers, k).wait_send()
    peers(lambda j: count_copy(j).wait_send())
    peers(lambda j: edges_copy(j).wait_send())
    peers(lambda j: back_copy(j).wait_send())
    to_reducers(lambda d, device: piece_copy(d, device).wait_send())

    @as_reducer
    def _():
        others(lambda d, device: sum_copy(d, device).wait_send())

    to_reducers(lambda d, device: sum_arrival(d).wait_recv())


def layer(counts, nodes, edges, target, senders, receivers, levels, land, masks, *weights):
    rows, count = nodes.shape
    owners, _, cap = senders.shape
    slots = edges.shape[1]
    reps = lax.axis_size("rep")
    devices = owners * reps
    chunks = 4 if count // LOW % 4 == 0 else 1
    grad_shape = (4 * rows, 2 * rows)
    reducers = min(devices, grad_shape[0] // 8)
    blocks = (owners, rows, cap)
    dma = pltpu.SemaphoreType.DMA
    vmem = pl.BlockSpec(memory_space=pltpu.VMEM)
    return pl.pallas_call(
        functools.partial(layer_kernel, masks.shape[0], reps),
        in_specs=[pl.BlockSpec(memory_space=pltpu.SMEM)] + [vmem] * (8 + len(weights)),
        out_specs=[vmem] * 4,
        out_shape=[
            jax.ShapeDtypeStruct((rows, count), BF16),
            jax.ShapeDtypeStruct((rows, count), BF16),
            jax.ShapeDtypeStruct((rows, slots), BF16),
            jax.ShapeDtypeStruct(grad_shape, F32),
        ],
        scratch_shapes=[
            pltpu.VMEM((2, PLANES, rows * (count // LOW), LOW), BF16),
            pltpu.VMEM(blocks, BF16),
            pltpu.VMEM(blocks, BF16),
            pltpu.VMEM(blocks, BF16),
            pltpu.VMEM(blocks, BF16),
            pltpu.VMEM((2, owners, 1, cap), jnp.int32),
            pltpu.VMEM((owners, 1, 128), jnp.int32),
            pltpu.VMEM((owners, 1, 128), jnp.int32),
            pltpu.VMEM(blocks, F32),
            pltpu.VMEM(blocks, F32),
            pltpu.VMEM((owners, 1, cap), F32),
            pltpu.VMEM(blocks, BF16),
            pltpu.VMEM(blocks, BF16),
            pltpu.VMEM(blocks, BF16),
            pltpu.VMEM((rows * (count // LOW), LOW), F32),
            pltpu.VMEM((rows, count), F32),
            pltpu.VMEM(grad_shape, F32),
            pltpu.VMEM((4, rows, 128), F32),
            pltpu.VMEM((devices, grad_shape[0] // reducers, grad_shape[1]), F32),
            pltpu.VMEM((3 * rows, rows), BF16),
            pltpu.VMEM((rows, rows), BF16),
            pltpu.VMEM((2 * rows, rows), BF16),
            pltpu.VMEM((rows, rows), BF16),
            pltpu.VMEM((rows, 16 * -(-(8 + masks.shape[0]) // 16)), F32),
            dma((2, 5, chunks)),
            dma((2, PLANES, chunks)),
            dma((2, PLANES)),
            dma((2, PLANES)),
            dma((2, owners)),
            dma((2, owners)),
            dma((2, owners)),
            dma((2, owners)),
            dma((owners,)),
            dma((owners,)),
            dma((reducers,)),
            dma((devices,)),
            dma((devices,)),
            dma((reducers,)),
        ],
        compiler_params=pltpu.CompilerParams(
            vmem_limit_bytes=VMEM_LIMIT, collective_id=0, has_side_effects=True
        ),
        cost_estimate=pl.CostEstimate(
            flops=64 * 2**30, bytes_accessed=16 * 2**20, transcendentals=4 * 2**20
        ),
        name="layer",
    )(counts, nodes, edges, target, senders, receivers, levels, land, masks, *weights)


def hand_out_kernel(new_in, node_in, edge_in, packed, new_nodes, node_grad, edge_grad, *rest):
    outs, sems = rest[:-1], rest[-1]
    copies = [
        pltpu.make_async_copy(src, dst, sems.at[k])
        for k, (src, dst) in enumerate(
            ((edge_in, edge_grad), (new_in, new_nodes), (node_in, node_grad))
        )
    ]
    for copy in copies:
        copy.start()
    rows = packed.shape[1] // 2
    lines = packed[3 * rows :, :].T
    edge_first, edge_b1, edge_second, edge_b2, edge_g, edge_h = outs[:6]
    node_first, node_b1, node_second, node_b2, node_g, node_h = outs[6:]
    edge_first[...] = packed[: 3 * rows, :].T[:rows, :]
    edge_second[...] = packed[3 * rows :, rows:]
    node_first[...] = packed[: 2 * rows, :].T[rows:, :]
    node_second[...] = packed[2 * rows : 3 * rows, rows:]
    for k, out in enumerate((edge_b1, edge_b2, edge_g, edge_h, node_b1, node_b2, node_g, node_h)):
        out[...] = lines[k, :rows]
    for copy in copies:
        copy.wait()


def hand_out(new_nodes, node_grad, edge_grad, packed):
    rows = packed.shape[1] // 2
    vmem = pl.BlockSpec(memory_space=pltpu.VMEM)
    stay = pl.BlockSpec(memory_space=pl.ANY)
    shapes = [
        (rows, 3 * rows), (rows,), (rows, rows), (rows,), (rows,), (rows,),
        (rows, 2 * rows), (rows,), (rows, rows), (rows,), (rows,), (rows,),
    ]
    large = [jax.ShapeDtypeStruct(a.shape, a.dtype) for a in (new_nodes, node_grad, edge_grad)]
    outs = pl.pallas_call(
        hand_out_kernel,
        in_specs=[stay] * 3 + [vmem],
        out_specs=[stay] * 3 + [vmem] * len(shapes),
        out_shape=large + [jax.ShapeDtypeStruct(s, F32) for s in shapes],
        scratch_shapes=[pltpu.SemaphoreType.DMA((3,))],
        compiler_params=pltpu.CompilerParams(vmem_limit_bytes=VMEM_LIMIT),
        name="hand_out",
    )(new_nodes, node_grad, edge_grad, packed)
    outs = list(outs)
    outs[3], outs[9] = outs[3].T, outs[9].T
    return tuple(outs)


def per_device(
    nodes, edges, target, senders, receivers, counts, levels, land, channel_mask,
    edge_in, edge_in_bias, edge_out, edge_out_bias, edge_gain, edge_shift,
    node_in, node_in_bias, node_out, node_out_bias, node_gain, node_shift,
):
    count = nodes.shape[1]
    owners = lax.axis_size("edge")
    cap = edges.shape[1] // owners
    return hand_out(
        *layer(
            counts, nodes, edges, target,
            senders.reshape(owners, 1, cap), receivers.reshape(owners, 1, cap),
            levels.reshape(1, count), land.reshape(1, count), channel_mask,
            edge_in.T, edge_out, node_in.T, node_out,
            edge_in_bias, edge_out_bias, edge_gain, edge_shift,
            node_in_bias, node_out_bias, node_gain, node_shift,
        )
    )


def solution(mesh):
    over = ("edge", "rep")
    wide, line, same = P(None, over), P(over), P()
    return jax.shard_map(
        per_device,
        mesh=mesh,
        in_specs=(wide, wide, wide, line, line, line, line, line) + (same,) * 13,
        out_specs=(wide, wide, wide) + (same,) * 12,
        check_vma=False,
    )
```

```python
import functools

import jax
import jax.numpy as jnp
from jax import lax
from jax.experimental import pallas as pl
from jax.experimental.pallas import tpu as pltpu
from jax.sharding import PartitionSpec as P

NORM_EPS = 1e-05
F32 = jnp.float32
BF16 = jnp.bfloat16
LOW = 256
VMEM_LIMIT = 60 * 2**20
PLANES = 4
MESH = pl.DeviceIdType.MESH

EB1, EB2, EG, EH, NB1, NB2, NG, NH, CM = 0, 1, 2, 3, 4, 5, 6, 7, 8


def dot(a, b):
    return jnp.dot(a, b, preferred_element_type=F32)


def dot_tn(a, b):
    return lax.dot_general(a, b, (((0,), (0,)), ((), ())), preferred_element_type=F32)


def dot_nt(a, b):
    return lax.dot_general(a, b, (((1,), (1,)), ((), ())), preferred_element_type=F32)


def one_hot_low(ids):
    low = ids & (LOW - 1)
    rows = lax.broadcasted_iota(jnp.int32, (LOW, ids.shape[1]), 0)
    return (rows == low).astype(F32).astype(BF16)


def high_of(ids, rows):
    high = ids >> (LOW.bit_length() - 1)
    return jnp.broadcast_to(high.astype(F32).astype(BF16), (rows, ids.shape[1]))


def stack_table(table_ref, value):
    rows = value.shape[0]
    for h in range(value.shape[1] // LOW):
        table_ref[h * rows : (h + 1) * rows, :] = value[:, h * LOW : (h + 1) * LOW]


def gather_columns(table, ids, rows):
    picked = dot(table, one_hot_low(ids)).astype(BF16)
    high = high_of(ids, rows)
    out = picked[:rows]
    for h in range(1, table.shape[0] // rows):
        out = jnp.where(high == BF16(h), picked[h * rows : (h + 1) * rows], out)
    return out


def scatter_columns(values, ids, count):
    rows = values.shape[0]
    high = high_of(ids, rows)
    zero = jnp.zeros_like(values)
    spread = jnp.concatenate(
        [jnp.where(high == BF16(h), values, zero) for h in range(count // LOW)], axis=0
    )
    return dot_nt(spread, one_hot_low(ids))


def column(cols, index):
    return cols[:, index : index + 1]


def mean_rows(v):
    return jnp.mean(v, axis=0, keepdims=True)


def lane_sums(v):
    out = v[:, :128]
    for k in range(1, v.shape[1] // 128):
        out = out + v[:, k * 128 : (k + 1) * 128]
    return out


def branch_forward(w1t, w2t, b1, b2, stacked):
    pre = dot(w1t, stacked) + b1
    hidden = (pre * (1.0 / (1.0 + jnp.exp(-pre)))).astype(BF16)
    outer = dot(w2t, hidden) + b2
    shifted = outer - mean_rows(outer)
    inverse = lax.rsqrt(mean_rows(shifted * shifted) + NORM_EPS)
    return pre, shifted * inverse, inverse


def branch_backward(w2, gain, grad, pre, normal, inverse):
    q = grad * gain
    outer_grad = (
        inverse * (q - mean_rows(q) - normal * mean_rows(q * normal))
    ).astype(BF16)
    s = 1.0 / (1.0 + jnp.exp(-pre))
    pre_grad = (dot(w2, outer_grad) * (s * (1.0 + pre * (1.0 - s)))).astype(BF16)
    return outer_grad, pre_grad, (pre * s).astype(BF16)


def split_dot(low, wide):
    top = wide.astype(BF16)
    rest = (wide - top.astype(F32)).astype(BF16)
    return dot(low, top) + dot(low, rest)


def layer_kernel(
    levels_count, reps,
    counts, nodes, edges, target, senders, receivers, levels, land, masks, ew1t, ew2, nw1t, nw2,
    eb1, eb2, eg, eh, nb1, nb2, ng, nh,
    new_nodes, node_grad, edge_grad, summed,
    tabs, send_a, recv_s, recv_e, mine, ids_tab, count_send, count_recv, pre_s, normal_s,
    inverse_s, recv_c, send_d, recv_d, total, part, grads, sums, pieces, ew1, ew2t, nw1, nw2t, cols,
    tab_send, tab_recv, ids_send, ids_recv, a_send, a_recv, b_send, b_recv, count_out, count_in,
    piece_send, piece_recv, sum_send, sum_recv,
):
    rows, count = nodes.shape
    owners, cap = senders.shape[0], senders.shape[2]
    ring = owners // PLANES
    high_count = count // LOW
    chunks = tab_recv.shape[2]
    chunk = tabs.shape[2] // chunks
    e, rep = lax.axis_index("edge"), lax.axis_index("rep")
    z, r = e // ring, e % ring
    me, devices = e * reps + rep, owners * reps
    upper = z // 2
    order = (z, z + 1 - 2 * upper, 2 - 2 * z + 5 * upper, 3 - 3 * upper)
    middle = lax.rem(z, 3) != 0
    toward = 3 - 2 * z

    def at(plane, place):
        return (plane * ring + place, rep)

    def remote(src, dst, send, recv, device):
        return pltpu.make_async_remote_copy(
            src, dst, send, recv, device_id=device, device_id_type=MESH
        )

    def loop(low, high, body):
        def step(i, carry):
            body(i)
            return carry

        lax.fori_loop(low, high, step, 0)

    def others(body):
        def one(t):
            d = lax.rem(me + t, devices)
            body(d, (d // reps, lax.rem(d, reps)))

        loop(1, devices, one)

    barrier = pltpu.get_barrier_semaphore()
    others(
        lambda d, device: pl.semaphore_signal(
            barrier, inc=1, device_id=device, device_id_type=MESH
        )
    )

    def eye(n):
        return (
            lax.broadcasted_iota(jnp.int32, (n, n), 0) == lax.broadcasted_iota(jnp.int32, (n, n), 1)
        ).astype(F32).astype(BF16)

    unit = eye(rows)
    ew1[...] = dot_tn(ew1t[...], unit).astype(BF16)
    nw1[...] = dot_tn(nw1t[...], unit).astype(BF16)
    ew2t[...] = dot_tn(ew2[...], unit).astype(BF16)
    nw2t[...] = dot_tn(nw2[...], unit).astype(BF16)
    lines = [v[...].astype(F32)[None, :] for v in (eb1, eb2, eg, eh, nb1, nb2, ng, nh)]
    lines.append(masks[...].astype(F32))
    lines.append(jnp.zeros((-(8 + levels_count) % 16, rows), F32))
    cols[...] = dot_nt(unit, jnp.concatenate(lines, axis=0).astype(BF16))
    stack_table(tabs.at[0, z], nodes[...])
    for j in range(owners):
        count_send[j] = jnp.full(count_send.shape[1:], counts[j], jnp.int32)
    pl.semaphore_wait(barrier, devices - 1)

    def part_of(phase, plane, c):
        return tabs.at[phase, plane, pl.ds(c * chunk, chunk)]

    def table_copy(phase, plane, c, lane, to):
        return remote(
            part_of(phase, plane, c), part_of(phase, plane, c),
            tab_send.at[phase, lane, c], tab_recv.at[phase, plane, c], at(to, r),
        )

    def await_table(phase, plane, c):
        table_copy(phase, plane, c, 0, z).wait_recv()

    def send_own(phase, c):
        @pl.when(z < PLANES - 1)
        def _():
            table_copy(phase, z, c, 0, z + 1).start()

        @pl.when(z > 0)
        def _():
            table_copy(phase, z, c, 1, z - 1).start()

    def relay(phase, slot):
        @pl.when(middle)
        def _():
            for c in range(chunks):
                if slot == 0:
                    await_table(phase, z - toward, c)
                    table_copy(phase, z - toward, c, 2, z + toward).start()
                    await_table(phase, z + toward, c)
                    table_copy(phase, z + toward, c, 3, z - toward).start()
                else:
                    await_table(phase, z + 2 * toward, c)
                    table_copy(phase, z + 2 * toward, c, 4, z - toward).start()

    def end_wait(phase, k):
        @pl.when(jnp.logical_not(middle))
        def _():
            for c in range(chunks):
                await_table(phase, order[k], c)

    def drain_tables(phase):
        for c in range(chunks):
            @pl.when(z < PLANES - 1)
            def _():
                table_copy(phase, z, c, 0, z + 1).wait_send()

            @pl.when(z > 0)
            def _():
                table_copy(phase, z, c, 1, z - 1).wait_send()

            @pl.when(middle)
            def _():
                table_copy(phase, z - toward, c, 2, z + toward).wait_send()
                table_copy(phase, z + toward, c, 3, z - toward).wait_send()
                table_copy(phase, z + 2 * toward, c, 4, z - toward).wait_send()

    def ids_copy(phase, ids, k):
        plane = lax.rem(z + k, PLANES)
        return remote(
            ids.at[pl.ds(plane * ring, ring)], ids_tab.at[phase, pl.ds(z * ring, ring)],
            ids_send.at[phase, plane], ids_recv.at[phase, z], at(plane, r),
        )

    def ids_arrival(phase, plane):
        rows_of = ids_tab.at[phase, pl.ds(plane * ring, ring)]
        return remote(
            rows_of, rows_of, ids_send.at[phase, plane], ids_recv.at[phase, plane], at(plane, r)
        )

    def plane_copy(phase, plane, to, into):
        return remote(
            send_a.at[plane * ring + to], into.at[plane * ring + r],
            a_send.at[phase, plane * ring + to], a_recv.at[phase, plane * ring + r], at(z, to),
        )

    def plane_arrival(phase, j, into):
        return remote(
            send_a.at[j], into.at[j], a_send.at[phase, j], a_recv.at[phase, j], at(z, r)
        )

    def hand_over(phase, plane, to, t, got, into):
        @pl.when(t < ring)
        def _():
            send_a[plane * ring + to] = got
            plane_copy(phase, plane, to, into).start()

        @pl.when(t == ring)
        def _():
            into[plane * ring + r] = got

    def gather_step(phase, k, into):
        plane = order[k]

        def one(t):
            to = lax.rem(r + t, ring)
            got = gather_columns(tabs[phase, plane], ids_tab[phase, plane * ring + to], rows)
            hand_over(phase, plane, to, t, got, into)

        loop(1, ring + 1, one)

    def drain_planes(phase, into):
        for plane in range(PLANES):
            loop(1, ring, lambda t: plane_copy(phase, plane, lax.rem(r + t, ring), into).wait_send())

    def lanes(j):
        return pl.ds(pl.multiple_of(j * cap, cap), cap)

    def edges_copy(j):
        return remote(
            edges.at[:, lanes(j)], recv_e.at[e], b_send.at[0, j], b_recv.at[0, e], (j, rep)
        )

    def edges_arrival(a):
        return remote(
            edges.at[:, lanes(a)], recv_e.at[a], b_send.at[0, a], b_recv.at[0, a], (e, rep)
        )

    def count_copy(j):
        return remote(
            count_send.at[j], count_recv.at[e], count_out.at[j], count_in.at[e], (j, rep)
        )

    def count_arrival(a):
        return remote(
            count_send.at[a], count_recv.at[a], count_out.at[a], count_in.at[a], (e, rep)
        )

    def back_copy(a):
        return remote(
            send_d.at[a], recv_d.at[e], b_send.at[1, a], b_recv.at[1, e], (a, rep)
        )

    def back_arrival(j):
        return remote(
            send_d.at[j], recv_d.at[j], b_send.at[1, j], b_recv.at[1, j], (e, rep)
        )

    def peers(body):
        loop(1, owners, lambda t: body(lax.rem(e + t, owners)))

    def send_edges(k):
        def one(t):
            edges_copy(order[k] * ring + lax.rem(r + t, ring)).start()

        loop(1 if k == 0 else 0, ring, one)

    packed = cols[...]
    place = lax.broadcasted_iota(jnp.int32, (1, cap), 1)

    def live_here(a):
        line = count_recv[a]
        wide = jnp.concatenate([line] * (cap // line.shape[1]), axis=1)
        return (place < wide).astype(F32)

    def edge_forward(a):
        own = recv_e[a]
        pre, normal, inverse = branch_forward(
            ew1t[...], ew2t[...], column(packed, EB1), column(packed, EB2),
            jnp.concatenate([own, recv_s[a], mine[a]], axis=0),
        )
        pre_s[a] = pre
        normal_s[a] = normal
        inverse_s[a] = inverse
        updated = own.astype(F32) + (normal * column(packed, EG) + column(packed, EH))
        return (updated * live_here(a)).astype(BF16)

    def forward_step(k):
        def one(t):
            a = order[k] * ring + lax.rem(r + ring - t, ring)

            @pl.when(t > 0)
            def _():
                plane_arrival(0, a, recv_s).wait_recv()

            if k == 0:
                @pl.when(t > 0)
                def _():
                    count_arrival(a).wait_recv()
                    edges_arrival(a).wait_recv()
            else:
                count_arrival(a).wait_recv()
                edges_arrival(a).wait_recv()
            total[...] += scatter_columns(edge_forward(a), receivers[a], count)

        loop(0, ring, one)

    def edge_backward(a, got):
        grad = got.astype(F32) * live_here(a)
        normal = normal_s[a]
        outer_grad, pre_grad, hidden = branch_backward(
            ew2[...], column(packed, EG), grad, pre_s[a], normal, inverse_s[a]
        )
        grads[...] += dot_nt(
            jnp.concatenate([recv_e[a], recv_s[a], mine[a], hidden], axis=0),
            jnp.concatenate([pre_grad, outer_grad], axis=0),
        )
        for k, v in enumerate((pre_grad.astype(F32), outer_grad.astype(F32), grad * normal, grad)):
            sums[k] += lane_sums(v)
        return pre_grad

    def backward_step(k):
        plane = order[k]

        def one(t):
            to = lax.rem(r + t, ring)
            a = plane * ring + to
            got = gather_columns(tabs[1, z], receivers[a], rows)
            if k == 0:
                hand_over(1, z, to, t, got, recv_c)
            pre_grad = edge_backward(a, got)
            send_d[a] = pre_grad
            if k == 0:
                @pl.when(t < ring)
                def _():
                    back_copy(a).start()
            else:
                back_copy(a).start()
            total[...] += scatter_columns(pre_grad, receivers[a], count)

        loop(1, ring + 1, one)

    for c in range(chunks):
        send_own(0, c)
    for k in range(1, PLANES):
        ids_copy(0, senders, k).start()
    peers(lambda j: count_copy(j).start())
    send_edges(0)
    ids_tab[0, pl.ds(z * ring, ring)] = senders[pl.ds(z * ring, ring)]
    count_recv[e] = count_send[e]
    recv_e[e] = edges[:, lanes(e)]
    total[...] = jnp.zeros_like(total)
    grads[...] = jnp.zeros_like(grads)
    sums[...] = jnp.zeros_like(sums)

    def mine_of(low, high):
        def one(a):
            mine[a] = gather_columns(tabs[0, z], receivers[a], rows)

        loop(low, high, one)

    gather_step(0, 0, recv_s)
    mine_of(0, owners // 2)
    relay(0, 0)
    for k in range(1, PLANES):
        ids_arrival(0, order[k]).wait_recv()
    end_wait(0, 1)
    send_edges(1)
    gather_step(0, 1, recv_s)
    mine_of(owners // 2, owners)
    relay(0, 1)
    end_wait(0, 2)
    send_edges(2)
    gather_step(0, 2, recv_s)
    forward_step(0)
    end_wait(0, 3)
    send_edges(3)
    gather_step(0, 3, recv_s)
    for k in range(1, PLANES):
        ids_copy(1, receivers, k).start()
    for k in range(1, PLANES):
        forward_step(k)
    drain_planes(0, recv_s)

    per = high_count // chunks
    wide = per * LOW
    node_first = jnp.zeros((2 * rows, rows), F32)
    node_second = jnp.zeros((rows, rows), F32)
    node_sums = [jnp.zeros((rows, 128), F32)] * 4
    for c in range(chunks):
        here = slice(c * wide, (c + 1) * wide)
        aggregate = jnp.concatenate(
            [total[h * rows : (h + 1) * rows, :] for h in range(c * per, (c + 1) * per)], axis=1
        ).astype(BF16)
        own = nodes[:, here]
        stacked = jnp.concatenate([own, aggregate], axis=0)
        pre, normal, inverse = branch_forward(
            nw1t[...], nw2t[...], column(packed, NB1), column(packed, NB2), stacked
        )
        gain = column(packed, NG)
        state = own.astype(F32) + (normal * gain + column(packed, NH))
        new_nodes[:, here] = state.astype(BF16)
        weight = jnp.zeros((rows, wide), F32)
        for l in range(levels_count):
            weight = jnp.where(levels[:, here] == l, column(packed, CM + l), weight)
        weight = weight * land[:, here].astype(F32)
        grad = weight * (state - target[:, here].astype(F32))
        outer_grad, pre_grad, hidden = branch_backward(nw2[...], gain, grad, pre, normal, inverse)
        stacked_grad = dot(nw1[...], pre_grad)
        part[:, here] = grad + stacked_grad[:rows]
        low = stacked_grad[rows:].astype(BF16)
        for h in range(per):
            tabs[1, z, (c * per + h) * rows : (c * per + h + 1) * rows, :] = low[
                :, h * LOW : (h + 1) * LOW
            ]
        send_own(1, c)
        node_first = node_first + dot_nt(stacked, pre_grad)
        node_second = node_second + dot_nt(hidden, outer_grad)
        for k, v in enumerate((pre_grad.astype(F32), outer_grad.astype(F32), grad * normal, grad)):
            node_sums[k] = node_sums[k] + lane_sums(v)

    total[...] = jnp.zeros_like(total)
    backward_step(0)
    relay(1, 0)
    for k in range(1, PLANES):
        ids_arrival(1, order[k]).wait_recv()
    end_wait(1, 1)
    gather_step(1, 1, recv_c)
    backward_step(1)
    relay(1, 1)
    end_wait(1, 2)
    gather_step(1, 2, recv_c)
    backward_step(2)
    end_wait(1, 3)
    gather_step(1, 3, recv_c)
    backward_step(3)

    grads[: 2 * rows, rows:] = node_first
    grads[2 * rows : 3 * rows, rows:] = node_second
    grads[3 * rows :, :8] = jnp.concatenate(
        [sums[k].sum(axis=1, keepdims=True) for k in range(4)]
        + [v.sum(axis=1, keepdims=True) for v in node_sums],
        axis=1,
    )
    reducers = min(devices, grads.shape[0] // 8)
    height = grads.shape[0] // reducers

    def piece(d):
        return pl.ds(pl.multiple_of(d * height, 8), height)

    def piece_copy(d, device):
        return remote(
            grads.at[piece(d)], pieces.at[me], piece_send.at[d], piece_recv.at[me], device
        )

    def piece_arrival(d):
        return remote(
            grads.at[piece(0)], pieces.at[d], piece_send.at[0], piece_recv.at[d], (e, rep)
        )

    def sum_copy(d, device):
        return remote(
            summed.at[piece(me)], summed.at[piece(me)], sum_send.at[d], sum_recv.at[me], device
        )

    def sum_arrival(d):
        return remote(
            summed.at[piece(d)], summed.at[piece(d)], sum_send.at[0], sum_recv.at[d], (e, rep)
        )

    def to_reducers(body):
        def one(d, device):
            if reducers == devices:
                body(d, device)
            else:
                @pl.when(d < reducers)
                def _():
                    body(d, device)

        others(one)

    def as_reducer(body):
        if reducers == devices:
            body()
        else:
            pl.when(me < reducers)(body)

    to_reducers(lambda d, device: piece_copy(d, device).start())
    def node_total(w_rows):
        for h in range(high_count):
            here = slice(h * LOW, (h + 1) * LOW)
            part[:, here] += split_dot(ew1[w_rows, :], total[h * rows : (h + 1) * rows, :])

    node_total(slice(2 * rows, 3 * rows))
    total[...] = jnp.zeros_like(total)

    @as_reducer
    def _():
        pieces[me] = grads[piece(me), :]
        others(lambda d, device: piece_arrival(d).wait_recv())

        def add(d, running):
            return running + pieces[d]

        summed[piece(me), :] = lax.fori_loop(1, devices, add, pieces[0])
        others(lambda d, device: sum_copy(d, device).start())

    def finish_block(j, pre_grad):
        grad = recv_c[j].astype(F32) * (place < counts[j]).astype(F32)
        edge_grad[:, lanes(j)] = (grad + dot(ew1[:rows, :], pre_grad)).astype(BF16)
        total[...] += scatter_columns(pre_grad, senders[j], count)

    finish_block(e, send_d[e])
    for k in range(PLANES):
        def one(t):
            j = order[k] * ring + lax.rem(r + ring - t, ring)
            if k == 0:
                plane_arrival(1, j, recv_c).wait_recv()
            else:
                @pl.when(t > 0)
                def _():
                    plane_arrival(1, j, recv_c).wait_recv()
            back_arrival(j).wait_recv()
            finish_block(j, recv_d[j])

        loop(1 if k == 0 else 0, ring, one)
    node_total(slice(rows, 2 * rows))
    node_grad[...] = part[...].astype(BF16)

    drain_tables(0)
    drain_tables(1)
    drain_planes(1, recv_c)
    for k in range(1, PLANES):
        ids_copy(0, senders, k).wait_send()
        ids_copy(1, receivers, k).wait_send()
    peers(lambda j: count_copy(j).wait_send())
    peers(lambda j: edges_copy(j).wait_send())
    peers(lambda j: back_copy(j).wait_send())
    to_reducers(lambda d, device: piece_copy(d, device).wait_send())

    @as_reducer
    def _():
        others(lambda d, device: sum_copy(d, device).wait_send())

    to_reducers(lambda d, device: sum_arrival(d).wait_recv())


def layer(counts, nodes, edges, target, senders, receivers, levels, land, masks, *weights):
    rows, count = nodes.shape
    owners, _, cap = senders.shape
    slots = edges.shape[1]
    reps = lax.axis_size("rep")
    devices = owners * reps
    chunks = 4 if count // LOW % 4 == 0 else 1
    grad_shape = (4 * rows, 2 * rows)
    reducers = min(devices, grad_shape[0] // 8)
    blocks = (owners, rows, cap)
    dma = pltpu.SemaphoreType.DMA
    vmem = pl.BlockSpec(memory_space=pltpu.VMEM)
    return pl.pallas_call(
        functools.partial(layer_kernel, masks.shape[0], reps),
        in_specs=[pl.BlockSpec(memory_space=pltpu.SMEM)] + [vmem] * (8 + len(weights)),
        out_specs=[vmem] * 4,
        out_shape=[
            jax.ShapeDtypeStruct((rows, count), BF16),
            jax.ShapeDtypeStruct((rows, count), BF16),
            jax.ShapeDtypeStruct((rows, slots), BF16),
            jax.ShapeDtypeStruct(grad_shape, F32),
        ],
        scratch_shapes=[
            pltpu.VMEM((2, PLANES, rows * (count // LOW), LOW), BF16),
            pltpu.VMEM(blocks, BF16),
            pltpu.VMEM(blocks, BF16),
            pltpu.VMEM(blocks, BF16),
            pltpu.VMEM(blocks, BF16),
            pltpu.VMEM((2, owners, 1, cap), jnp.int32),
            pltpu.VMEM((owners, 1, 128), jnp.int32),
            pltpu.VMEM((owners, 1, 128), jnp.int32),
            pltpu.VMEM(blocks, F32),
            pltpu.VMEM(blocks, F32),
            pltpu.VMEM((owners, 1, cap), F32),
            pltpu.VMEM(blocks, BF16),
            pltpu.VMEM(blocks, BF16),
            pltpu.VMEM(blocks, BF16),
            pltpu.VMEM((rows * (count // LOW), LOW), F32),
            pltpu.VMEM((rows, count), F32),
            pltpu.VMEM(grad_shape, F32),
            pltpu.VMEM((4, rows, 128), F32),
            pltpu.VMEM((devices, grad_shape[0] // reducers, grad_shape[1]), F32),
            pltpu.VMEM((3 * rows, rows), BF16),
            pltpu.VMEM((rows, rows), BF16),
            pltpu.VMEM((2 * rows, rows), BF16),
            pltpu.VMEM((rows, rows), BF16),
            pltpu.VMEM((rows, 16 * -(-(8 + masks.shape[0]) // 16)), F32),
            dma((2, 5, chunks)),
            dma((2, PLANES, chunks)),
            dma((2, PLANES)),
            dma((2, PLANES)),
            dma((2, owners)),
            dma((2, owners)),
            dma((2, owners)),
            dma((2, owners)),
            dma((owners,)),
            dma((owners,)),
            dma((reducers,)),
            dma((devices,)),
            dma((devices,)),
            dma((reducers,)),
        ],
        compiler_params=pltpu.CompilerParams(
            vmem_limit_bytes=VMEM_LIMIT, collective_id=0, has_side_effects=True
        ),
        cost_estimate=pl.CostEstimate(
            flops=64 * 2**30, bytes_accessed=16 * 2**20, transcendentals=4 * 2**20
        ),
        name="layer",
    )(counts, nodes, edges, target, senders, receivers, levels, land, masks, *weights)


def hand_out_kernel(edge_in, new_in, node_in, packed, edge_grad, new_nodes, node_grad, *rest):
    outs, (hold_edge, hold_new, hold_node, sems) = rest[:-4], rest[-4:]
    parts = []
    cuts = sems.shape[1] - 2
    wide = edge_in.shape[1] // cuts
    for c in range(cuts):
        here = pl.ds(c * wide, wide)
        parts.append((edge_in.at[:, here], hold_edge.at[:, here], edge_grad.at[:, here]))
    parts.append((new_in, hold_new, new_nodes))
    parts.append((node_in, hold_node, node_grad))
    ins = [pltpu.make_async_copy(a, b, sems.at[0, k]) for k, (a, b, _) in enumerate(parts)]
    backs = [pltpu.make_async_copy(b, c, sems.at[1, k]) for k, (_, b, c) in enumerate(parts)]
    for copy in ins:
        copy.start()
    rows = packed.shape[1] // 2
    lines = packed[3 * rows :, :].T
    edge_first, edge_b1, edge_second, edge_b2, edge_g, edge_h = outs[:6]
    node_first, node_b1, node_second, node_b2, node_g, node_h = outs[6:]
    edge_first[...] = packed[: 3 * rows, :].T[:rows, :]
    edge_second[...] = packed[3 * rows :, rows:]
    node_first[...] = packed[: 2 * rows, :].T[rows:, :]
    node_second[...] = packed[2 * rows : 3 * rows, rows:]
    for k, out in enumerate((edge_b1, edge_b2, edge_g, edge_h, node_b1, node_b2, node_g, node_h)):
        out[...] = lines[k, :rows]
    for copy, back in zip(ins, backs):
        copy.wait()
        back.start()
    for back in backs:
        back.wait()


def hand_out(new_nodes, node_grad, edge_grad, packed):
    rows = packed.shape[1] // 2
    cuts = 4
    vmem = pl.BlockSpec(memory_space=pltpu.VMEM)
    stay = pl.BlockSpec(memory_space=pl.ANY)
    shapes = [
        (rows, 3 * rows), (rows,), (rows, rows), (rows,), (rows,), (rows,),
        (rows, 2 * rows), (rows,), (rows, rows), (rows,), (rows,), (rows,),
    ]
    large = (edge_grad, new_nodes, node_grad)
    edge_grad, new_nodes, node_grad, *small = pl.pallas_call(
        hand_out_kernel,
        in_specs=[stay] * 3 + [vmem],
        out_specs=[stay] * 3 + [vmem] * len(shapes),
        out_shape=[jax.ShapeDtypeStruct(a.shape, a.dtype) for a in large]
        + [jax.ShapeDtypeStruct(s, F32) for s in shapes],
        scratch_shapes=[pltpu.VMEM(a.shape, a.dtype) for a in large]
        + [pltpu.SemaphoreType.DMA((2, cuts + 2))],
        compiler_params=pltpu.CompilerParams(vmem_limit_bytes=VMEM_LIMIT),
        name="hand_out",
    )(*large, packed)
    small[0], small[6] = small[0].T, small[6].T
    return (new_nodes, node_grad, edge_grad, *small)


def per_device(
    nodes, edges, target, senders, receivers, counts, levels, land, channel_mask,
    edge_in, edge_in_bias, edge_out, edge_out_bias, edge_gain, edge_shift,
    node_in, node_in_bias, node_out, node_out_bias, node_gain, node_shift,
):
    count = nodes.shape[1]
    owners = lax.axis_size("edge")
    cap = edges.shape[1] // owners
    return hand_out(
        *layer(
            counts, nodes, edges, target,
            senders.reshape(owners, 1, cap), receivers.reshape(owners, 1, cap),
            levels.reshape(1, count), land.reshape(1, count), channel_mask,
            edge_in.T, edge_out, node_in.T, node_out,
            edge_in_bias, edge_out_bias, edge_gain, edge_shift,
            node_in_bias, node_out_bias, node_gain, node_shift,
        )
    )


def solution(mesh):
    over = ("edge", "rep")
    wide, line, same = P(None, over), P(over), P()
    return jax.shard_map(
        per_device,
        mesh=mesh,
        in_specs=(wide, wide, wide, line, line, line, line, line) + (same,) * 13,
        out_specs=(wide, wide, wide) + (same,) * 12,
        check_vma=False,
    )
```

```python
import functools

import jax
import jax.numpy as jnp
from jax import lax
from jax.experimental import pallas as pl
from jax.experimental.pallas import tpu as pltpu
from jax.sharding import PartitionSpec as P

NORM_EPS = 1e-05
F32 = jnp.float32
BF16 = jnp.bfloat16
LOW = 256
VMEM_LIMIT = 60 * 2**20
PLANES = 4
MESH = pl.DeviceIdType.MESH

EB1, EB2, EG, EH, NB1, NB2, NG, NH, CM = 0, 1, 2, 3, 4, 5, 6, 7, 8


def dot(a, b):
    return jnp.dot(a, b, preferred_element_type=F32)


def dot_tn(a, b):
    return lax.dot_general(a, b, (((0,), (0,)), ((), ())), preferred_element_type=F32)


def dot_nt(a, b):
    return lax.dot_general(a, b, (((1,), (1,)), ((), ())), preferred_element_type=F32)


def one_hot_low(ids):
    low = ids & (LOW - 1)
    rows = lax.broadcasted_iota(jnp.int32, (LOW, ids.shape[1]), 0)
    return (rows == low).astype(F32).astype(BF16)


def high_of(ids, rows):
    high = ids >> (LOW.bit_length() - 1)
    return jnp.broadcast_to(high.astype(F32).astype(BF16), (rows, ids.shape[1]))


def stack_table(table_ref, value):
    rows = value.shape[0]
    for h in range(value.shape[1] // LOW):
        table_ref[h * rows : (h + 1) * rows, :] = value[:, h * LOW : (h + 1) * LOW]


def gather_columns(table, ids, rows):
    picked = dot(table, one_hot_low(ids)).astype(BF16)
    high = high_of(ids, rows)
    out = picked[:rows]
    for h in range(1, table.shape[0] // rows):
        out = jnp.where(high == BF16(h), picked[h * rows : (h + 1) * rows], out)
    return out


def scatter_columns(values, ids, count):
    rows = values.shape[0]
    high = high_of(ids, rows)
    zero = jnp.zeros_like(values)
    spread = jnp.concatenate(
        [jnp.where(high == BF16(h), values, zero) for h in range(count // LOW)], axis=0
    )
    return dot_nt(spread, one_hot_low(ids))


def column(cols, index):
    return cols[:, index : index + 1]


def mean_rows(v):
    return jnp.mean(v, axis=0, keepdims=True)


def lane_sums(v):
    out = v[:, :128]
    for k in range(1, v.shape[1] // 128):
        out = out + v[:, k * 128 : (k + 1) * 128]
    return out


def branch_forward(w1t, w2t, b1, b2, stacked):
    pre = dot(w1t, stacked) + b1
    hidden = (pre * (1.0 / (1.0 + jnp.exp(-pre)))).astype(BF16)
    outer = dot(w2t, hidden) + b2
    shifted = outer - mean_rows(outer)
    inverse = lax.rsqrt(mean_rows(shifted * shifted) + NORM_EPS)
    return pre, shifted * inverse, inverse


def branch_backward(w2, gain, grad, pre, normal, inverse):
    q = grad * gain
    outer_grad = (
        inverse * (q - mean_rows(q) - normal * mean_rows(q * normal))
    ).astype(BF16)
    s = 1.0 / (1.0 + jnp.exp(-pre))
    pre_grad = (dot(w2, outer_grad) * (s * (1.0 + pre * (1.0 - s)))).astype(BF16)
    return outer_grad, pre_grad, (pre * s).astype(BF16)


def split_dot(low, wide):
    top = wide.astype(BF16)
    rest = (wide - top.astype(F32)).astype(BF16)
    return dot(low, top) + dot(low, rest)


def layer_kernel(
    levels_count, reps,
    counts, nodes, edges_in, target_in, senders, receivers, levels, land, masks, ew1t, ew2, nw1t,
    nw2, eb1, eb2, eg, eh, nb1, nb2, ng, nh,
    new_nodes, node_grad, edge_grad, summed,
    edges, target, tabs, send_a, recv_a, sent, ids_tab, pre_s, normal_s, inverse_s, send_m,
    recv_m, recv_r, recv_c, acc, chain_in, chain_out, part, grads, sums, pieces,
    ew1, ew2t, nw1, nw2t, cols, new_hold, node_hold,
    in_sem, out_sem, grad_sem, tab_send, tab_recv, ids_send, ids_recv, a_send, a_recv, m_send,
    m_recv, chain_send, chain_recv, piece_send, piece_recv, sum_send, sum_recv,
):
    rows, count = nodes.shape
    owners, cap = senders.shape[0], senders.shape[2]
    ring = owners // PLANES
    high_count = count // LOW
    chunks = tab_recv.shape[2]
    chunk = tabs.shape[2] // chunks
    e, rep = lax.axis_index("edge"), lax.axis_index("rep")
    z, r = e // ring, e % ring
    me, devices = e * reps + rep, owners * reps
    upper = z // 2
    toward = 1 - 2 * upper
    order = (z, z + toward, 2 - 2 * z + 5 * upper, 3 - 3 * upper)
    middle = lax.rem(z, 3) != 0
    own_sums = PLANES

    def at(plane, place):
        return (plane * ring + place, rep)

    def remote(src, dst, send, recv, device):
        return pltpu.make_async_remote_copy(
            src, dst, send, recv, device_id=device, device_id_type=MESH
        )

    def loop(low, high, body):
        def step(i, carry):
            body(i)
            return carry

        lax.fori_loop(low, high, step, 0)

    def others(body):
        def one(t):
            d = lax.rem(me + t, devices)
            body(d, (d // reps, lax.rem(d, reps)))

        loop(1, devices, one)

    def at_ends(body):
        pl.when(jnp.logical_not(middle))(body)

    def at_middle(body):
        pl.when(middle)(body)

    load_edges = pltpu.make_async_copy(edges_in, edges, in_sem.at[0])
    load_target = pltpu.make_async_copy(target_in, target, in_sem.at[1])
    load_edges.start()
    load_target.start()

    barrier = pltpu.get_barrier_semaphore()
    others(
        lambda d, device: pl.semaphore_signal(
            barrier, inc=1, device_id=device, device_id_type=MESH
        )
    )
    stack_table(tabs.at[0, z], nodes[...])
    pl.semaphore_wait(barrier, devices - 1)

    def part_of(phase, plane, c):
        return tabs.at[phase, plane, pl.ds(c * chunk, chunk)]

    def table_copy(phase, plane, c, lane, to):
        return remote(
            part_of(phase, plane, c), part_of(phase, plane, c),
            tab_send.at[phase, lane, c], tab_recv.at[phase, plane, c], at(to, r),
        )

    def await_table(phase, plane, c):
        table_copy(phase, plane, c, 0, z).wait_recv()

    def send_own(phase, c):
        @pl.when(z < PLANES - 1)
        def _():
            table_copy(phase, z, c, 0, z + 1).start()

        @pl.when(z > 0)
        def _():
            table_copy(phase, z, c, 1, z - 1).start()

    def relay(phase, slot):
        @at_middle
        def _():
            for c in range(chunks):
                if slot == 0:
                    await_table(phase, z - toward, c)
                    table_copy(phase, z - toward, c, 2, z + toward).start()
                    await_table(phase, z + toward, c)
                    table_copy(phase, z + toward, c, 3, z - toward).start()
                else:
                    await_table(phase, z + 2 * toward, c)
                    table_copy(phase, z + 2 * toward, c, 4, z - toward).start()

    def end_wait(phase, k):
        @at_ends
        def _():
            for c in range(chunks):
                await_table(phase, order[k], c)

    def drain_tables(phase):
        for c in range(chunks):
            @pl.when(z < PLANES - 1)
            def _():
                table_copy(phase, z, c, 0, z + 1).wait_send()

            @pl.when(z > 0)
            def _():
                table_copy(phase, z, c, 1, z - 1).wait_send()

            @at_middle
            def _():
                table_copy(phase, z - toward, c, 2, z + toward).wait_send()
                table_copy(phase, z + toward, c, 3, z - toward).wait_send()
                table_copy(phase, z + 2 * toward, c, 4, z - toward).wait_send()

    def ids_copy(k):
        plane = lax.rem(z + k, PLANES)
        return remote(
            receivers.at[pl.ds(plane * ring, ring)], ids_tab.at[pl.ds(z * ring, ring)],
            ids_send.at[plane], ids_recv.at[z], at(plane, r),
        )

    def ids_arrival(plane):
        rows_of = ids_tab.at[pl.ds(plane * ring, ring)]
        return remote(rows_of, rows_of, ids_send.at[plane], ids_recv.at[plane], at(plane, r))

    def plane_copy(phase, plane, to, src, into, send, recv):
        return remote(
            src.at[plane * ring + to], into.at[plane * ring + r],
            send.at[phase, plane * ring + to], recv.at[phase, plane * ring + r], at(z, to),
        )

    def plane_arrival(phase, j, src, into, send, recv):
        return remote(src.at[j], into.at[j], send.at[phase, j], recv.at[phase, j], at(z, r))

    def drain_planes(phase, src, into, send, recv):
        for plane in range(PLANES):
            loop(
                1, ring,
                lambda t: plane_copy(
                    phase, plane, lax.rem(r + t, ring), src, into, send, recv
                ).wait_send(),
            )

    def in_pairs(body):
        loop(0, ring // 2, lambda h: body((2 * h, 2 * h + 1)))

    def side_by_side(blocks):
        return jnp.concatenate(blocks, axis=1)

    def gather_step(phase, k, into):
        plane = order[k]

        def two(ts):
            tos = [lax.rem(r + t + 1, ring) for t in ts]
            got = gather_columns(
                tabs[phase, plane], side_by_side([ids_tab[plane * ring + to] for to in tos]), rows
            )
            for i, (t, to) in enumerate(zip(ts, tos)):
                block = got[:, i * cap : (i + 1) * cap]

                @pl.when(t < ring - 1)
                def _():
                    send_a[plane * ring + to] = block
                    plane_copy(phase, plane, to, send_a, into, a_send, a_recv).start()

                @pl.when(t == ring - 1)
                def _():
                    into[plane * ring + r] = block

        in_pairs(two)

    def edge_step(phase, k, arrived, into, block):
        plane = order[k]

        def two(ts):
            tos = [lax.rem(r + ring - t, ring) for t in ts]
            for t, to in zip(ts, tos):
                @pl.when(t > 0)
                def _():
                    plane_arrival(phase, plane * ring + to, send_a, arrived, a_send, a_recv).wait_recv()

            outs = [block(plane * ring + to) for to in tos]
            for t, to, out in zip(ts, tos, outs):
                send_m[plane * ring + to] = out

                @pl.when(t > 0)
                def _():
                    plane_copy(phase, plane, to, send_m, into, m_send, m_recv).start()

                @pl.when(t == 0)
                def _():
                    into[plane * ring + r] = out

        in_pairs(two)

    def sum_step(phase, k, into):
        plane = order[k]
        acc[plane] = jnp.zeros(acc.shape[1:], F32)

        def two(ts):
            froms = [plane * ring + lax.rem(r + t, ring) for t in ts]
            for t, a in zip(ts, froms):
                @pl.when(t > 0)
                def _():
                    plane_arrival(phase, a, send_m, into, m_send, m_recv).wait_recv()

            acc[plane] += scatter_columns(
                side_by_side([into[a] for a in froms]),
                side_by_side([ids_tab[a] for a in froms]), count,
            )

        in_pairs(two)

    def rows_of(c):
        return pl.ds(c * chunk, chunk)

    def own_slot(plane, direction):
        return plane + (PLANES - plane) * ((1 - direction) // 2)

    def chain_copy(phase, plane, c, slot, to):
        return remote(
            chain_out.at[plane, rows_of(c)], chain_in.at[phase, slot, rows_of(c)],
            chain_send.at[phase, plane, c], chain_recv.at[phase, slot, c], at(to, r),
        )

    def chain_arrival(phase, slot, c):
        here = chain_in.at[phase, slot, rows_of(c)]
        return remote(here, here, chain_send.at[phase, 0, c], chain_recv.at[phase, slot, c], at(z, r))

    def end_copy(phase, k, c):
        plane = order[k]
        slot = own_slot(plane, toward) if k == 1 else plane
        return chain_copy(phase, plane, c, slot, z + toward)

    def middle_copy(phase, k, c):
        plane = order[k]
        if k == 1:
            return chain_copy(phase, plane, c, own_slot(plane, toward), z + toward)
        if k == 2:
            return chain_copy(phase, plane, c, own_slot(plane, -toward), z - toward)
        return chain_copy(phase, plane, c, plane, z + toward)

    def chain_start(phase, k):
        @at_ends
        def _():
            for c in range(chunks):
                chain_out[order[k], rows_of(c)] = acc[order[k], rows_of(c)].astype(BF16)
                end_copy(phase, k, c).start()

    def chain_merge(phase, ks):
        @at_middle
        def _():
            for c in range(chunks):
                for k in ks:
                    plane = order[k]
                    chain_arrival(phase, plane, c).wait_recv()
                    chain_out[plane, rows_of(c)] = (
                        acc[plane, rows_of(c)] + chain_in[phase, plane, rows_of(c)].astype(F32)
                    ).astype(BF16)
                    middle_copy(phase, k, c).start()

    def chain_end(phase, c):
        slot = own_slot(z, -toward)
        chain_arrival(phase, slot, c).wait_recv()
        acc[z, rows_of(c)] += chain_in[phase, slot, rows_of(c)].astype(F32)

        @at_middle
        def _():
            other = own_slot(z, toward)
            chain_arrival(phase, other, c).wait_recv()
            acc[z, rows_of(c)] += chain_in[phase, other, rows_of(c)].astype(F32)

    def drain_chain(phase):
        for c in range(chunks):
            for k in range(1, PLANES):
                @at_ends
                def _():
                    end_copy(phase, k, c).wait_send()

                @at_middle
                def _():
                    middle_copy(phase, k, c).wait_send()

    def lanes(j):
        return pl.ds(pl.multiple_of(j * cap, cap), cap)

    def live_of(j):
        place = lax.broadcasted_iota(jnp.int32, (1, cap), 1)
        return (place < counts[j]).astype(F32)

    def col(index):
        return cols[:, index : index + 1]

    def edge_forward(j):
        own = edges[:, lanes(j)]
        pre, normal, inverse = branch_forward(
            ew1t[...], ew2t[...], col(EB1), col(EB2),
            jnp.concatenate([own, sent[j], recv_a[j]], axis=0),
        )
        pre_s[j] = pre
        normal_s[j] = normal
        inverse_s[j] = inverse
        updated = own.astype(F32) + (normal * col(EG) + col(EH))
        return (updated * live_of(j)).astype(BF16)

    def grad_copy(j):
        return pltpu.make_async_copy(recv_c.at[j], edge_grad.at[:, lanes(j)], grad_sem.at[j])

    def edge_backward(j):
        grad = recv_c[j].astype(F32) * live_of(j)
        normal = normal_s[j]
        outer_grad, pre_grad, hidden = branch_backward(
            ew2[...], col(EG), grad, pre_s[j], normal, inverse_s[j]
        )
        recv_c[j] = (grad + dot(ew1[:rows, :], pre_grad)).astype(BF16)
        grad_copy(j).start()
        grads[...] += dot_nt(
            jnp.concatenate([edges[:, lanes(j)], sent[j], recv_a[j], hidden], axis=0),
            jnp.concatenate([pre_grad, outer_grad], axis=0),
        )
        for k, v in enumerate((pre_grad.astype(F32), outer_grad.astype(F32), grad * normal, grad)):
            sums[k] += lane_sums(v)
        return pre_grad

    def senders_of(k):
        def two(ts):
            js = [order[k] * ring + t for t in ts]
            got = gather_columns(tabs[0, z], side_by_side([senders[j] for j in js]), rows)
            for i, j in enumerate(js):
                sent[j] = got[:, i * cap : (i + 1) * cap]

        in_pairs(two)

    def by_sender(k):
        def two(ts):
            js = [order[k] * ring + t for t in ts]
            acc[own_sums] += scatter_columns(
                side_by_side([send_m[j] for j in js]), side_by_side([senders[j] for j in js]), count
            )

        in_pairs(two)

    for c in range(chunks):
        send_own(0, c)
    for k in range(1, PLANES):
        ids_copy(k).start()
    ids_tab[pl.ds(z * ring, ring)] = receivers[pl.ds(z * ring, ring)]
    gather_step(0, 0, recv_a)

    unit = (
        (
            lax.broadcasted_iota(jnp.int32, (rows, rows), 0)
            == lax.broadcasted_iota(jnp.int32, (rows, rows), 1)
        )
        .astype(F32)
        .astype(BF16)
    )
    ew1[...] = dot_tn(ew1t[...], unit).astype(BF16)
    nw1[...] = dot_tn(nw1t[...], unit).astype(BF16)
    ew2t[...] = dot_tn(ew2[...], unit).astype(BF16)
    nw2t[...] = dot_tn(nw2[...], unit).astype(BF16)
    lines = [v[...].astype(F32)[None, :] for v in (eb1, eb2, eg, eh, nb1, nb2, ng, nh)]
    lines.append(masks[...].astype(F32))
    lines.append(jnp.zeros((-(8 + levels_count) % 16, rows), F32))
    cols[...] = dot_nt(unit, jnp.concatenate(lines, axis=0).astype(BF16))
    grads[...] = jnp.zeros_like(grads)
    sums[...] = jnp.zeros_like(sums)
    senders_of(0)
    senders_of(1)
    load_edges.wait()
    edge_step(0, 0, recv_a, recv_m, edge_forward)
    relay(0, 0)
    for k in range(1, PLANES):
        ids_arrival(order[k]).wait_recv()
    end_wait(0, 1)
    gather_step(0, 1, recv_a)
    senders_of(2)
    edge_step(0, 1, recv_a, recv_m, edge_forward)
    senders_of(3)
    sum_step(0, 1, recv_m)
    chain_start(0, 1)
    relay(0, 1)
    end_wait(0, 2)
    gather_step(0, 2, recv_a)
    edge_step(0, 2, recv_a, recv_m, edge_forward)
    sum_step(0, 2, recv_m)
    chain_start(0, 2)
    end_wait(0, 3)
    gather_step(0, 3, recv_a)
    edge_step(0, 3, recv_a, recv_m, edge_forward)
    sum_step(0, 3, recv_m)
    chain_start(0, 3)
    chain_merge(0, (1,))
    sum_step(0, 0, recv_m)
    chain_merge(0, (3, 2))
    load_target.wait()
    drain_planes(0, send_a, recv_a, a_send, a_recv)
    drain_planes(0, send_m, recv_m, m_send, m_recv)

    per = high_count // chunks
    wide = per * LOW
    node_first = jnp.zeros((2 * rows, rows), F32)
    node_second = jnp.zeros((rows, rows), F32)
    node_sums = [jnp.zeros((rows, 128), F32)] * 4

    def chunk_of(table, c):
        return side_by_side(
            [table[(c * per + h) * rows : (c * per + h + 1) * rows, :] for h in range(per)]
        )

    for c in range(chunks):
        here = slice(c * wide, (c + 1) * wide)
        chain_end(0, c)
        own = nodes[:, here]
        stacked = jnp.concatenate([own, chunk_of(acc.at[z], c).astype(BF16)], axis=0)
        pre, normal, inverse = branch_forward(nw1t[...], nw2t[...], col(NB1), col(NB2), stacked)
        gain = col(NG)
        state = own.astype(F32) + (normal * gain + col(NH))
        new_hold[:, here] = state.astype(BF16)
        weight = jnp.zeros((rows, wide), F32)
        for l in range(levels_count):
            weight = jnp.where(levels[:, here] == l, col(CM + l), weight)
        weight = weight * land[:, here].astype(F32)
        grad = weight * (state - target[:, here].astype(F32))
        outer_grad, pre_grad, hidden = branch_backward(nw2[...], gain, grad, pre, normal, inverse)
        stacked_grad = dot(nw1[...], pre_grad)
        part[:, here] = grad + stacked_grad[:rows]
        low = stacked_grad[rows:].astype(BF16)
        for h in range(per):
            tabs[1, z, (c * per + h) * rows : (c * per + h + 1) * rows, :] = low[
                :, h * LOW : (h + 1) * LOW
            ]
        send_own(1, c)
        node_first = node_first + dot_nt(stacked, pre_grad)
        node_second = node_second + dot_nt(hidden, outer_grad)
        for k, v in enumerate((pre_grad.astype(F32), outer_grad.astype(F32), grad * normal, grad)):
            node_sums[k] = node_sums[k] + lane_sums(v)
    node_vec = jnp.concatenate([v.sum(axis=1, keepdims=True) for v in node_sums], axis=1)
    new_copy = pltpu.make_async_copy(new_hold, new_nodes, out_sem.at[0])
    new_copy.start()
    drain_chain(0)

    acc[own_sums] = jnp.zeros(acc.shape[1:], F32)
    gather_step(1, 0, recv_c)
    edge_step(1, 0, recv_c, recv_r, edge_backward)
    by_sender(0)
    relay(1, 0)
    end_wait(1, 1)
    gather_step(1, 1, recv_c)
    edge_step(1, 1, recv_c, recv_r, edge_backward)
    by_sender(1)
    sum_step(1, 1, recv_r)
    chain_start(1, 1)
    relay(1, 1)
    end_wait(1, 2)
    gather_step(1, 2, recv_c)
    edge_step(1, 2, recv_c, recv_r, edge_backward)
    sum_step(1, 2, recv_r)
    chain_start(1, 2)
    end_wait(1, 3)
    gather_step(1, 3, recv_c)
    edge_step(1, 3, recv_c, recv_r, edge_backward)
    sum_step(1, 3, recv_r)
    chain_start(1, 3)
    chain_merge(1, (1,))

    grads[: 2 * rows, rows:] = node_first
    grads[2 * rows : 3 * rows, rows:] = node_second
    grads[3 * rows :, :8] = jnp.concatenate(
        [sums[k].sum(axis=1, keepdims=True) for k in range(4)] + [node_vec], axis=1
    )
    reducers = min(devices, grads.shape[0] // 8)
    height = grads.shape[0] // reducers

    def piece(d):
        return pl.ds(pl.multiple_of(d * height, 8), height)

    def piece_copy(d, device):
        return remote(
            grads.at[piece(d)], pieces.at[me], piece_send.at[d], piece_recv.at[me], device
        )

    def piece_arrival(d):
        return remote(
            grads.at[piece(0)], pieces.at[d], piece_send.at[0], piece_recv.at[d], (e, rep)
        )

    def sum_copy(d, device):
        return remote(
            summed.at[piece(me)], summed.at[piece(me)], sum_send.at[d], sum_recv.at[me], device
        )

    def sum_arrival(d):
        return remote(
            summed.at[piece(d)], summed.at[piece(d)], sum_send.at[0], sum_recv.at[d], (e, rep)
        )

    def to_reducers(body):
        def one(d, device):
            if reducers == devices:
                body(d, device)
            else:
                @pl.when(d < reducers)
                def _():
                    body(d, device)

        others(one)

    def as_reducer(body):
        if reducers == devices:
            body()
        else:
            pl.when(me < reducers)(body)

    to_reducers(lambda d, device: piece_copy(d, device).start())
    sum_step(1, 0, recv_r)
    chain_merge(1, (3, 2))
    by_sender(2)
    by_sender(3)

    @as_reducer
    def _():
        pieces[me] = grads[piece(me), :]
        others(lambda d, device: piece_arrival(d).wait_recv())

        def add(d, running):
            return running + pieces[d]

        summed[piece(me), :] = lax.fori_loop(1, devices, add, pieces[0])
        others(lambda d, device: sum_copy(d, device).start())

    for h in range(high_count):
        here = slice(h * LOW, (h + 1) * LOW)
        part[:, here] += split_dot(
            ew1[rows : 2 * rows, :], acc[own_sums, h * rows : (h + 1) * rows, :]
        )
    for c in range(chunks):
        here = slice(c * wide, (c + 1) * wide)
        chain_end(1, c)
        node_hold[:, here] = (
            part[:, here] + split_dot(ew1[2 * rows :, :], chunk_of(acc.at[z], c))
        ).astype(BF16)
    node_copy = pltpu.make_async_copy(node_hold, node_grad, out_sem.at[1])
    node_copy.start()

    drain_tables(0)
    drain_tables(1)
    drain_planes(1, send_a, recv_c, a_send, a_recv)
    drain_planes(1, send_m, recv_r, m_send, m_recv)
    drain_chain(1)
    for k in range(1, PLANES):
        ids_copy(k).wait_send()
    loop(0, owners, lambda j: grad_copy(j).wait())
    to_reducers(lambda d, device: piece_copy(d, device).wait_send())

    @as_reducer
    def _():
        others(lambda d, device: sum_copy(d, device).wait_send())

    to_reducers(lambda d, device: sum_arrival(d).wait_recv())
    new_copy.wait()
    node_copy.wait()


def layer(counts, nodes, edges, target, senders, receivers, levels, land, masks, *weights):
    rows, count = nodes.shape
    owners, _, cap = senders.shape
    slots = edges.shape[1]
    reps = lax.axis_size("rep")
    devices = owners * reps
    chunks = 4 if count // LOW % 4 == 0 else 1
    grad_shape = (4 * rows, 2 * rows)
    reducers = min(devices, grad_shape[0] // 8)
    blocks = (owners, rows, cap)
    table = (rows * (count // LOW), LOW)
    dma = pltpu.SemaphoreType.DMA
    vmem = pl.BlockSpec(memory_space=pltpu.VMEM)
    stay = pl.BlockSpec(memory_space=pl.ANY)
    return pl.pallas_call(
        functools.partial(layer_kernel, masks.shape[0], reps),
        in_specs=[pl.BlockSpec(memory_space=pltpu.SMEM), vmem, stay, stay]
        + [vmem] * (5 + len(weights)),
        out_specs=[stay, stay, stay, vmem],
        out_shape=[
            jax.ShapeDtypeStruct((rows, count), BF16),
            jax.ShapeDtypeStruct((rows, count), BF16),
            jax.ShapeDtypeStruct((rows, slots), BF16),
            jax.ShapeDtypeStruct(grad_shape, F32),
        ],
        scratch_shapes=[
            pltpu.VMEM((rows, slots), BF16),
            pltpu.VMEM((rows, count), BF16),
            pltpu.VMEM((2, PLANES) + table, BF16),
            pltpu.VMEM(blocks, BF16),
            pltpu.VMEM(blocks, BF16),
            pltpu.VMEM(blocks, BF16),
            pltpu.VMEM((owners, 1, cap), jnp.int32),
            pltpu.VMEM(blocks, F32),
            pltpu.VMEM(blocks, F32),
            pltpu.VMEM((owners, 1, cap), F32),
            pltpu.VMEM(blocks, BF16),
            pltpu.VMEM(blocks, BF16),
            pltpu.VMEM(blocks, BF16),
            pltpu.VMEM(blocks, BF16),
            pltpu.VMEM((PLANES + 1,) + table, F32),
            pltpu.VMEM((2, PLANES + 1) + table, BF16),
            pltpu.VMEM((PLANES,) + table, BF16),
            pltpu.VMEM((rows, count), F32),
            pltpu.VMEM(grad_shape, F32),
            pltpu.VMEM((4, rows, 128), F32),
            pltpu.VMEM((devices, grad_shape[0] // reducers, grad_shape[1]), F32),
            pltpu.VMEM((3 * rows, rows), BF16),
            pltpu.VMEM((rows, rows), BF16),
            pltpu.VMEM((2 * rows, rows), BF16),
            pltpu.VMEM((rows, rows), BF16),
            pltpu.VMEM((rows, 16 * -(-(8 + masks.shape[0]) // 16)), F32),
            pltpu.VMEM((rows, count), BF16),
            pltpu.VMEM((rows, count), BF16),
            dma((2,)),
            dma((2,)),
            dma((owners,)),
            dma((2, 5, chunks)),
            dma((2, PLANES, chunks)),
            dma((PLANES,)),
            dma((PLANES,)),
            dma((2, owners)),
            dma((2, owners)),
            dma((2, owners)),
            dma((2, owners)),
            dma((2, PLANES, chunks)),
            dma((2, PLANES + 1, chunks)),
            dma((reducers,)),
            dma((devices,)),
            dma((devices,)),
            dma((reducers,)),
        ],
        compiler_params=pltpu.CompilerParams(
            vmem_limit_bytes=VMEM_LIMIT, collective_id=0, has_side_effects=True
        ),
        cost_estimate=pl.CostEstimate(
            flops=64 * 2**30, bytes_accessed=16 * 2**20, transcendentals=4 * 2**20
        ),
        name="layer",
    )(counts, nodes, edges, target, senders, receivers, levels, land, masks, *weights)


def hand_out_kernel(edge_in, new_in, node_in, packed, edge_grad, new_nodes, node_grad, *rest):
    outs, (hold_edge, hold_new, hold_node, sems) = rest[:-4], rest[-4:]
    parts = []
    cuts = sems.shape[1] - 2
    wide = edge_in.shape[1] // cuts
    for c in range(cuts):
        here = pl.ds(c * wide, wide)
        parts.append((edge_in.at[:, here], hold_edge.at[:, here], edge_grad.at[:, here]))
    parts.append((new_in, hold_new, new_nodes))
    parts.append((node_in, hold_node, node_grad))
    ins = [pltpu.make_async_copy(a, b, sems.at[0, k]) for k, (a, b, _) in enumerate(parts)]
    backs = [pltpu.make_async_copy(b, c, sems.at[1, k]) for k, (_, b, c) in enumerate(parts)]
    for copy in ins:
        copy.start()
    rows = packed.shape[1] // 2
    lines = packed[3 * rows :, :].T
    edge_first, edge_b1, edge_second, edge_b2, edge_g, edge_h = outs[:6]
    node_first, node_b1, node_second, node_b2, node_g, node_h = outs[6:]
    edge_first[...] = packed[: 3 * rows, :].T[:rows, :]
    edge_second[...] = packed[3 * rows :, rows:]
    node_first[...] = packed[: 2 * rows, :].T[rows:, :]
    node_second[...] = packed[2 * rows : 3 * rows, rows:]
    for k, out in enumerate((edge_b1, edge_b2, edge_g, edge_h, node_b1, node_b2, node_g, node_h)):
        out[...] = lines[k, :rows]
    for copy, back in zip(ins, backs):
        copy.wait()
        back.start()
    for back in backs:
        back.wait()


def hand_out(new_nodes, node_grad, edge_grad, packed):
    rows = packed.shape[1] // 2
    cuts = 4
    vmem = pl.BlockSpec(memory_space=pltpu.VMEM)
    stay = pl.BlockSpec(memory_space=pl.ANY)
    shapes = [
        (rows, 3 * rows), (rows,), (rows, rows), (rows,), (rows,), (rows,),
        (rows, 2 * rows), (rows,), (rows, rows), (rows,), (rows,), (rows,),
    ]
    large = (edge_grad, new_nodes, node_grad)
    edge_grad, new_nodes, node_grad, *small = pl.pallas_call(
        hand_out_kernel,
        in_specs=[stay] * 3 + [vmem],
        out_specs=[stay] * 3 + [vmem] * len(shapes),
        out_shape=[jax.ShapeDtypeStruct(a.shape, a.dtype) for a in large]
        + [jax.ShapeDtypeStruct(s, F32) for s in shapes],
        scratch_shapes=[pltpu.VMEM(a.shape, a.dtype) for a in large]
        + [pltpu.SemaphoreType.DMA((2, cuts + 2))],
        compiler_params=pltpu.CompilerParams(vmem_limit_bytes=VMEM_LIMIT),
        name="hand_out",
    )(*large, packed)
    small[0], small[6] = small[0].T, small[6].T
    return (new_nodes, node_grad, edge_grad, *small)


def per_device(
    nodes, edges, target, senders, receivers, counts, levels, land, channel_mask,
    edge_in, edge_in_bias, edge_out, edge_out_bias, edge_gain, edge_shift,
    node_in, node_in_bias, node_out, node_out_bias, node_gain, node_shift,
):
    count = nodes.shape[1]
    owners = lax.axis_size("edge")
    cap = edges.shape[1] // owners
    return hand_out(
        *layer(
            counts, nodes, edges, target,
            senders.reshape(owners, 1, cap), receivers.reshape(owners, 1, cap),
            levels.reshape(1, count), land.reshape(1, count), channel_mask,
            edge_in.T, edge_out, node_in.T, node_out,
            edge_in_bias, edge_out_bias, edge_gain, edge_shift,
            node_in_bias, node_out_bias, node_gain, node_shift,
        )
    )


def solution(mesh):
    over = ("edge", "rep")
    wide, line, same = P(None, over), P(over), P()
    return jax.shard_map(
        per_device,
        mesh=mesh,
        in_specs=(wide, wide, wide, line, line, line, line, line) + (same,) * 13,
        out_specs=(wide, wide, wide) + (same,) * 12,
        check_vma=False,
    )
```

```python
import functools

import jax
import jax.numpy as jnp
from jax import lax
from jax.experimental import pallas as pl
from jax.experimental.pallas import tpu as pltpu
from jax.sharding import PartitionSpec as P

NORM_EPS = 1e-05
F32 = jnp.float32
BF16 = jnp.bfloat16
LOW = 256
VMEM_LIMIT = 60 * 2**20
PLANES = 4
MESH = pl.DeviceIdType.MESH

EB1, EB2, EG, EH, NB1, NB2, NG, NH, CM = 0, 1, 2, 3, 4, 5, 6, 7, 8


def dot(a, b):
    return jnp.dot(a, b, preferred_element_type=F32)


def dot_tn(a, b):
    return lax.dot_general(a, b, (((0,), (0,)), ((), ())), preferred_element_type=F32)


def dot_nt(a, b):
    return lax.dot_general(a, b, (((1,), (1,)), ((), ())), preferred_element_type=F32)


def one_hot_low(ids):
    low = ids & (LOW - 1)
    rows = lax.broadcasted_iota(jnp.int32, (LOW, ids.shape[1]), 0)
    return (rows == low).astype(F32).astype(BF16)


def high_of(ids, rows):
    high = ids >> (LOW.bit_length() - 1)
    return jnp.broadcast_to(high.astype(F32).astype(BF16), (rows, ids.shape[1]))


def stack_table(table_ref, value):
    rows = value.shape[0]
    for h in range(value.shape[1] // LOW):
        table_ref[h * rows : (h + 1) * rows, :] = value[:, h * LOW : (h + 1) * LOW]


def gather_columns(table, ids, rows):
    picked = dot(table, one_hot_low(ids)).astype(BF16)
    high = high_of(ids, rows)
    out = picked[:rows]
    for h in range(1, table.shape[0] // rows):
        out = jnp.where(high == BF16(h), picked[h * rows : (h + 1) * rows], out)
    return out


def scatter_columns(values, ids, count):
    rows = values.shape[0]
    high = high_of(ids, rows)
    zero = jnp.zeros_like(values)
    spread = jnp.concatenate(
        [jnp.where(high == BF16(h), values, zero) for h in range(count // LOW)], axis=0
    )
    return dot_nt(spread, one_hot_low(ids))


def column(cols, index):
    return cols[:, index : index + 1]


def mean_rows(v):
    return jnp.mean(v, axis=0, keepdims=True)


def lane_sums(v):
    out = v[:, :128]
    for k in range(1, v.shape[1] // 128):
        out = out + v[:, k * 128 : (k + 1) * 128]
    return out


def branch_forward(w1t, w2t, b1, b2, stacked):
    pre = dot(w1t, stacked) + b1
    hidden = (pre * (1.0 / (1.0 + jnp.exp(-pre)))).astype(BF16)
    outer = dot(w2t, hidden) + b2
    shifted = outer - mean_rows(outer)
    inverse = lax.rsqrt(mean_rows(shifted * shifted) + NORM_EPS)
    return pre, shifted * inverse, inverse


def branch_backward(w2, gain, grad, pre, normal, inverse):
    q = grad * gain
    outer_grad = (
        inverse * (q - mean_rows(q) - normal * mean_rows(q * normal))
    ).astype(BF16)
    s = 1.0 / (1.0 + jnp.exp(-pre))
    pre_grad = (dot(w2, outer_grad) * (s * (1.0 + pre * (1.0 - s)))).astype(BF16)
    return outer_grad, pre_grad, (pre * s).astype(BF16)


def split_dot(low, wide):
    top = wide.astype(BF16)
    rest = (wide - top.astype(F32)).astype(BF16)
    return dot(low, top) + dot(low, rest)


def layer_kernel(
    levels_count, reps,
    counts, nodes, edges_in, target_in, senders, receivers, levels, land, masks, ew1t, ew2, nw1t,
    nw2,
    eb1, eb2, eg, eh, nb1, nb2, ng, nh,
    new_nodes, node_grad, edge_grad, summed,
    edges, target, new_hold, node_hold, in_sem, out_sem, grad_sem, tabs, send_a, recv_s, recv_e, mine, ids_tab, count_send, count_recv, pre_s, normal_s,
    inverse_s, recv_c, send_d, recv_d, total, part, grads, sums, pieces, ew1, ew2t, nw1, nw2t, cols,
    tab_send, tab_recv, ids_send, ids_recv, a_send, a_recv, b_send, b_recv, count_out, count_in,
    piece_send, piece_recv, sum_send, sum_recv,
):
    rows, count = nodes.shape
    owners, cap = senders.shape[0], senders.shape[2]
    ring = owners // PLANES
    high_count = count // LOW
    chunks = tab_recv.shape[2]
    chunk = tabs.shape[2] // chunks
    e, rep = lax.axis_index("edge"), lax.axis_index("rep")
    z, r = e // ring, e % ring
    me, devices = e * reps + rep, owners * reps
    upper = z // 2
    order = (z, z + 1 - 2 * upper, 2 - 2 * z + 5 * upper, 3 - 3 * upper)
    middle = lax.rem(z, 3) != 0
    toward = 3 - 2 * z

    def at(plane, place):
        return (plane * ring + place, rep)

    def remote(src, dst, send, recv, device):
        return pltpu.make_async_remote_copy(
            src, dst, send, recv, device_id=device, device_id_type=MESH
        )

    def loop(low, high, body):
        def step(i, carry):
            body(i)
            return carry

        lax.fori_loop(low, high, step, 0)

    def others(body):
        def one(t):
            d = lax.rem(me + t, devices)
            body(d, (d // reps, lax.rem(d, reps)))

        loop(1, devices, one)

    load_edges = pltpu.make_async_copy(edges_in, edges, in_sem.at[0])
    load_target = pltpu.make_async_copy(target_in, target, in_sem.at[1])
    load_edges.start()
    load_target.start()

    barrier = pltpu.get_barrier_semaphore()
    others(
        lambda d, device: pl.semaphore_signal(
            barrier, inc=1, device_id=device, device_id_type=MESH
        )
    )

    stack_table(tabs.at[0, z], nodes[...])
    pl.semaphore_wait(barrier, devices - 1)

    def part_of(phase, plane, c):
        return tabs.at[phase, plane, pl.ds(c * chunk, chunk)]

    def table_copy(phase, plane, c, lane, to):
        return remote(
            part_of(phase, plane, c), part_of(phase, plane, c),
            tab_send.at[phase, lane, c], tab_recv.at[phase, plane, c], at(to, r),
        )

    def await_table(phase, plane, c):
        table_copy(phase, plane, c, 0, z).wait_recv()

    def send_own(phase, c):
        @pl.when(z < PLANES - 1)
        def _():
            table_copy(phase, z, c, 0, z + 1).start()

        @pl.when(z > 0)
        def _():
            table_copy(phase, z, c, 1, z - 1).start()

    def relay(phase, slot):
        @pl.when(middle)
        def _():
            for c in range(chunks):
                if slot == 0:
                    await_table(phase, z - toward, c)
                    table_copy(phase, z - toward, c, 2, z + toward).start()
                    await_table(phase, z + toward, c)
                    table_copy(phase, z + toward, c, 3, z - toward).start()
                else:
                    await_table(phase, z + 2 * toward, c)
                    table_copy(phase, z + 2 * toward, c, 4, z - toward).start()

    def end_wait(phase, k):
        @pl.when(jnp.logical_not(middle))
        def _():
            for c in range(chunks):
                await_table(phase, order[k], c)

    def drain_tables(phase):
        for c in range(chunks):
            @pl.when(z < PLANES - 1)
            def _():
                table_copy(phase, z, c, 0, z + 1).wait_send()

            @pl.when(z > 0)
            def _():
                table_copy(phase, z, c, 1, z - 1).wait_send()

            @pl.when(middle)
            def _():
                table_copy(phase, z - toward, c, 2, z + toward).wait_send()
                table_copy(phase, z + toward, c, 3, z - toward).wait_send()
                table_copy(phase, z + 2 * toward, c, 4, z - toward).wait_send()

    def ids_copy(phase, ids, k):
        plane = lax.rem(z + k, PLANES)
        return remote(
            ids.at[pl.ds(plane * ring, ring)], ids_tab.at[phase, pl.ds(z * ring, ring)],
            ids_send.at[phase, plane], ids_recv.at[phase, z], at(plane, r),
        )

    def ids_arrival(phase, plane):
        rows_of = ids_tab.at[phase, pl.ds(plane * ring, ring)]
        return remote(
            rows_of, rows_of, ids_send.at[phase, plane], ids_recv.at[phase, plane], at(plane, r)
        )

    def plane_copy(phase, plane, to, into):
        return remote(
            send_a.at[plane * ring + to], into.at[plane * ring + r],
            a_send.at[phase, plane * ring + to], a_recv.at[phase, plane * ring + r], at(z, to),
        )

    def plane_arrival(phase, j, into):
        return remote(
            send_a.at[j], into.at[j], a_send.at[phase, j], a_recv.at[phase, j], at(z, r)
        )

    def hand_over(phase, plane, to, t, got, into):
        @pl.when(t < ring)
        def _():
            send_a[plane * ring + to] = got
            plane_copy(phase, plane, to, into).start()

        @pl.when(t == ring)
        def _():
            into[plane * ring + r] = got

    def gather_step(phase, k, into):
        plane = order[k]

        def two(ts):
            tos = [lax.rem(r + t + 1, ring) for t in ts]
            got = gather_columns(
                tabs[phase, plane],
                side_by_side([ids_tab[phase, plane * ring + to] for to in tos]), rows,
            )
            for i, (t, to) in enumerate(zip(ts, tos)):
                hand_over(phase, plane, to, t + 1, got[:, i * cap : (i + 1) * cap], into)

        in_pairs(two)

    def drain_planes(phase, into):
        for plane in range(PLANES):
            loop(1, ring, lambda t: plane_copy(phase, plane, lax.rem(r + t, ring), into).wait_send())

    def lanes(j):
        return pl.ds(pl.multiple_of(j * cap, cap), cap)

    def edges_copy(j):
        return remote(
            edges.at[:, lanes(j)], recv_e.at[e], b_send.at[0, j], b_recv.at[0, e], (j, rep)
        )

    def edges_arrival(a):
        return remote(
            edges.at[:, lanes(a)], recv_e.at[a], b_send.at[0, a], b_recv.at[0, a], (e, rep)
        )

    def count_copy(j):
        return remote(
            count_send.at[j], count_recv.at[e], count_out.at[j], count_in.at[e], (j, rep)
        )

    def count_arrival(a):
        return remote(
            count_send.at[a], count_recv.at[a], count_out.at[a], count_in.at[a], (e, rep)
        )

    def back_copy(a):
        return remote(
            send_d.at[a], recv_d.at[e], b_send.at[1, a], b_recv.at[1, e], (a, rep)
        )

    def back_arrival(j):
        return remote(
            send_d.at[j], recv_d.at[j], b_send.at[1, j], b_recv.at[1, j], (e, rep)
        )

    def peers(body):
        loop(1, owners, lambda t: body(lax.rem(e + t, owners)))

    def in_pairs(body):
        loop(0, ring // 2, lambda h: body((2 * h, 2 * h + 1)))

    def side_by_side(blocks):
        return jnp.concatenate(blocks, axis=1)

    def send_edges(k):
        def one(t):
            edges_copy(order[k] * ring + lax.rem(r + t, ring)).start()

        loop(1 if k == 0 else 0, ring, one)

    place = lax.broadcasted_iota(jnp.int32, (1, cap), 1)

    def live_here(a):
        line = count_recv[a]
        wide = jnp.concatenate([line] * (cap // line.shape[1]), axis=1)
        return (place < wide).astype(F32)

    def edge_forward(a):
        own = recv_e[a]
        pre, normal, inverse = branch_forward(
            ew1t[...], ew2t[...], column(cols, EB1), column(cols, EB2),
            jnp.concatenate([own, recv_s[a], mine[a]], axis=0),
        )
        pre_s[a] = pre
        normal_s[a] = normal
        inverse_s[a] = inverse
        updated = own.astype(F32) + (normal * column(cols, EG) + column(cols, EH))
        return (updated * live_here(a)).astype(BF16)

    def forward_step(k):
        def two(ts):
            froms = [order[k] * ring + lax.rem(r + ring - t, ring) for t in ts]
            for t, a in zip(ts, froms):
                @pl.when(t > 0)
                def _():
                    plane_arrival(0, a, recv_s).wait_recv()

                if k == 0:
                    @pl.when(t > 0)
                    def _():
                        count_arrival(a).wait_recv()
                        edges_arrival(a).wait_recv()
                else:
                    count_arrival(a).wait_recv()
                    edges_arrival(a).wait_recv()
            total[...] += scatter_columns(
                side_by_side([edge_forward(a) for a in froms]),
                side_by_side([receivers[a] for a in froms]), count,
            )

        in_pairs(two)

    def edge_backward(a, got):
        grad = got.astype(F32) * live_here(a)
        normal = normal_s[a]
        outer_grad, pre_grad, hidden = branch_backward(
            ew2[...], column(cols, EG), grad, pre_s[a], normal, inverse_s[a]
        )
        grads[...] += dot_nt(
            jnp.concatenate([recv_e[a], recv_s[a], mine[a], hidden], axis=0),
            jnp.concatenate([pre_grad, outer_grad], axis=0),
        )
        for k, v in enumerate((pre_grad.astype(F32), outer_grad.astype(F32), grad * normal, grad)):
            sums[k] += lane_sums(v)
        return pre_grad

    def backward_step(k):
        plane = order[k]

        def two(ts):
            tos = [lax.rem(r + t + 1, ring) for t in ts]
            froms = [plane * ring + to for to in tos]
            both = gather_columns(
                tabs[1, z], side_by_side([receivers[a] for a in froms]), rows
            )
            for i, (t, to, a) in enumerate(zip(ts, tos, froms)):
                got = both[:, i * cap : (i + 1) * cap]
                if k == 0:
                    hand_over(1, z, to, t + 1, got, recv_c)
                send_d[a] = edge_backward(a, got)

        in_pairs(two)

    def send_back(k):
        def one(t):
            back_copy(order[k] * ring + lax.rem(r + t, ring)).start()

        loop(1 if k == 0 else 0, ring, one)

    for c in range(chunks):
        send_own(0, c)
    for k in range(1, PLANES):
        ids_copy(0, senders, k).start()
    load_edges.wait()
    send_edges(0)
    for j in range(owners):
        count_send[j] = jnp.full(count_send.shape[1:], counts[j], jnp.int32)
    peers(lambda j: count_copy(j).start())
    ids_tab[0, pl.ds(z * ring, ring)] = senders[pl.ds(z * ring, ring)]
    count_recv[e] = count_send[e]
    recv_e[e] = edges[:, lanes(e)]
    total[...] = jnp.zeros_like(total)
    grads[...] = jnp.zeros_like(grads)
    sums[...] = jnp.zeros_like(sums)

    def mine_of(low, high):
        def two(h):
            both = gather_columns(
                tabs[0, z], side_by_side([receivers[2 * h], receivers[2 * h + 1]]), rows
            )
            mine[2 * h] = both[:, :cap]
            mine[2 * h + 1] = both[:, cap:]

        loop(low // 2, high // 2, two)

    gather_step(0, 0, recv_s)

    def eye(n):
        return (
            lax.broadcasted_iota(jnp.int32, (n, n), 0) == lax.broadcasted_iota(jnp.int32, (n, n), 1)
        ).astype(F32).astype(BF16)

    unit = eye(rows)
    ew1[...] = dot_tn(ew1t[...], unit).astype(BF16)
    nw1[...] = dot_tn(nw1t[...], unit).astype(BF16)
    ew2t[...] = dot_tn(ew2[...], unit).astype(BF16)
    nw2t[...] = dot_tn(nw2[...], unit).astype(BF16)
    lines = [v[...].astype(F32)[None, :] for v in (eb1, eb2, eg, eh, nb1, nb2, ng, nh)]
    lines.append(masks[...].astype(F32))
    lines.append(jnp.zeros((-(8 + levels_count) % 16, rows), F32))
    cols[...] = dot_nt(unit, jnp.concatenate(lines, axis=0).astype(BF16))
    mine_of(0, owners // 2)
    relay(0, 0)
    for k in range(1, PLANES):
        ids_arrival(0, order[k]).wait_recv()
    end_wait(0, 1)
    send_edges(1)
    gather_step(0, 1, recv_s)
    mine_of(owners // 2, owners)
    relay(0, 1)
    end_wait(0, 2)
    send_edges(2)
    gather_step(0, 2, recv_s)
    forward_step(0)
    end_wait(0, 3)
    send_edges(3)
    gather_step(0, 3, recv_s)
    for k in range(1, PLANES):
        ids_copy(1, receivers, k).start()
    for k in range(1, PLANES):
        forward_step(k)
    drain_planes(0, recv_s)

    load_target.wait()

    per = high_count // chunks
    wide = per * LOW
    node_first = jnp.zeros((2 * rows, rows), F32)
    node_second = jnp.zeros((rows, rows), F32)
    node_sums = [jnp.zeros((rows, 128), F32)] * 4
    for c in range(chunks):
        here = slice(c * wide, (c + 1) * wide)
        aggregate = jnp.concatenate(
            [total[h * rows : (h + 1) * rows, :] for h in range(c * per, (c + 1) * per)], axis=1
        ).astype(BF16)
        own = nodes[:, here]
        stacked = jnp.concatenate([own, aggregate], axis=0)
        pre, normal, inverse = branch_forward(
            nw1t[...], nw2t[...], column(cols, NB1), column(cols, NB2), stacked
        )
        gain = column(cols, NG)
        state = own.astype(F32) + (normal * gain + column(cols, NH))
        new_hold[:, here] = state.astype(BF16)
        weight = jnp.zeros((rows, wide), F32)
        for l in range(levels_count):
            weight = jnp.where(levels[:, here] == l, column(cols, CM + l), weight)
        weight = weight * land[:, here].astype(F32)
        grad = weight * (state - target[:, here].astype(F32))
        outer_grad, pre_grad, hidden = branch_backward(nw2[...], gain, grad, pre, normal, inverse)
        stacked_grad = dot(nw1[...], pre_grad)
        part[:, here] = grad + stacked_grad[:rows]
        low = stacked_grad[rows:].astype(BF16)
        for h in range(per):
            tabs[1, z, (c * per + h) * rows : (c * per + h + 1) * rows, :] = low[
                :, h * LOW : (h + 1) * LOW
            ]
        send_own(1, c)
        node_first = node_first + dot_nt(stacked, pre_grad)
        node_second = node_second + dot_nt(hidden, outer_grad)
        for k, v in enumerate((pre_grad.astype(F32), outer_grad.astype(F32), grad * normal, grad)):
            node_sums[k] = node_sums[k] + lane_sums(v)

    new_copy = pltpu.make_async_copy(new_hold, new_nodes, out_sem.at[0])
    new_copy.start()

    backward_step(0)
    send_back(0)
    backward_step(1)
    relay(1, 0)
    for k in range(1, PLANES):
        ids_arrival(1, order[k]).wait_recv()
    end_wait(1, 1)
    send_back(1)
    gather_step(1, 1, recv_c)
    backward_step(2)
    relay(1, 1)
    end_wait(1, 2)
    send_back(2)
    gather_step(1, 2, recv_c)
    backward_step(3)
    total[...] = jnp.zeros_like(total)

    def by_receiver(h):
        total[...] += scatter_columns(
            side_by_side([send_d[2 * h], send_d[2 * h + 1]]),
            side_by_side([receivers[2 * h], receivers[2 * h + 1]]), count,
        )

    end_wait(1, 3)
    send_back(3)
    gather_step(1, 3, recv_c)
    loop(0, owners // 2, by_receiver)

    grads[: 2 * rows, rows:] = node_first
    grads[2 * rows : 3 * rows, rows:] = node_second
    grads[3 * rows :, :8] = jnp.concatenate(
        [sums[k].sum(axis=1, keepdims=True) for k in range(4)]
        + [v.sum(axis=1, keepdims=True) for v in node_sums],
        axis=1,
    )
    reducers = min(devices, grads.shape[0] // 8)
    height = grads.shape[0] // reducers

    def piece(d):
        return pl.ds(pl.multiple_of(d * height, 8), height)

    def piece_copy(d, device):
        return remote(
            grads.at[piece(d)], pieces.at[me], piece_send.at[d], piece_recv.at[me], device
        )

    def piece_arrival(d):
        return remote(
            grads.at[piece(0)], pieces.at[d], piece_send.at[0], piece_recv.at[d], (e, rep)
        )

    def sum_copy(d, device):
        return remote(
            summed.at[piece(me)], summed.at[piece(me)], sum_send.at[d], sum_recv.at[me], device
        )

    def sum_arrival(d):
        return remote(
            summed.at[piece(d)], summed.at[piece(d)], sum_send.at[0], sum_recv.at[d], (e, rep)
        )

    def to_reducers(body):
        def one(d, device):
            if reducers == devices:
                body(d, device)
            else:
                @pl.when(d < reducers)
                def _():
                    body(d, device)

        others(one)

    def as_reducer(body):
        if reducers == devices:
            body()
        else:
            pl.when(me < reducers)(body)

    to_reducers(lambda d, device: piece_copy(d, device).start())
    def node_total(w_rows):
        for h in range(high_count):
            here = slice(h * LOW, (h + 1) * LOW)
            part[:, here] += split_dot(ew1[w_rows, :], total[h * rows : (h + 1) * rows, :])

    node_total(slice(2 * rows, 3 * rows))
    total[...] = jnp.zeros_like(total)

    @as_reducer
    def _():
        pieces[me] = grads[piece(me), :]
        others(lambda d, device: piece_arrival(d).wait_recv())

        def add(d, running):
            return running + pieces[d]

        summed[piece(me), :] = lax.fori_loop(1, devices, add, pieces[0])
        others(lambda d, device: sum_copy(d, device).start())

    def grad_copy(j):
        return pltpu.make_async_copy(recv_c.at[j], edge_grad.at[:, lanes(j)], grad_sem.at[j])

    def finish_edges(j, pre_grad):
        grad = recv_c[j].astype(F32) * (place < counts[j]).astype(F32)
        recv_c[j] = (grad + dot(ew1[:rows, :], pre_grad)).astype(BF16)
        grad_copy(j).start()

    recv_d[e] = send_d[e]
    for k in range(PLANES):
        def two(ts):
            js = [order[k] * ring + lax.rem(r + ring - t, ring) for t in ts]
            for t, j in zip(ts, js):
                @pl.when(t > 0)
                def _():
                    plane_arrival(1, j, recv_c).wait_recv()

                if k == 0:
                    @pl.when(t > 0)
                    def _():
                        back_arrival(j).wait_recv()
                else:
                    back_arrival(j).wait_recv()
                finish_edges(j, recv_d[j])
            total[...] += scatter_columns(
                side_by_side([recv_d[j] for j in js]), side_by_side([senders[j] for j in js]), count
            )

        in_pairs(two)
    node_total(slice(rows, 2 * rows))
    node_hold[...] = part[...].astype(BF16)
    node_copy = pltpu.make_async_copy(node_hold, node_grad, out_sem.at[1])
    node_copy.start()

    drain_tables(0)
    drain_tables(1)
    drain_planes(1, recv_c)
    for k in range(1, PLANES):
        ids_copy(0, senders, k).wait_send()
        ids_copy(1, receivers, k).wait_send()
    peers(lambda j: count_copy(j).wait_send())
    peers(lambda j: edges_copy(j).wait_send())
    peers(lambda j: back_copy(j).wait_send())
    to_reducers(lambda d, device: piece_copy(d, device).wait_send())

    @as_reducer
    def _():
        others(lambda d, device: sum_copy(d, device).wait_send())

    to_reducers(lambda d, device: sum_arrival(d).wait_recv())
    loop(0, owners, lambda j: grad_copy(j).wait())
    new_copy.wait()
    node_copy.wait()


def layer(counts, nodes, edges, target, senders, receivers, levels, land, masks, *weights):
    rows, count = nodes.shape
    owners, _, cap = senders.shape
    slots = edges.shape[1]
    reps = lax.axis_size("rep")
    devices = owners * reps
    chunks = 4 if count // LOW % 4 == 0 else 1
    grad_shape = (4 * rows, 2 * rows)
    reducers = min(devices, grad_shape[0] // 8)
    blocks = (owners, rows, cap)
    dma = pltpu.SemaphoreType.DMA
    vmem = pl.BlockSpec(memory_space=pltpu.VMEM)
    stay = pl.BlockSpec(memory_space=pl.ANY)
    return pl.pallas_call(
        functools.partial(layer_kernel, masks.shape[0], reps),
        in_specs=[pl.BlockSpec(memory_space=pltpu.SMEM), vmem, stay, stay]
        + [vmem] * (5 + len(weights)),
        out_specs=[stay, stay, stay, vmem],
        out_shape=[
            jax.ShapeDtypeStruct((rows, count), BF16),
            jax.ShapeDtypeStruct((rows, count), BF16),
            jax.ShapeDtypeStruct((rows, slots), BF16),
            jax.ShapeDtypeStruct(grad_shape, F32),
        ],
        scratch_shapes=[
            pltpu.VMEM((rows, slots), BF16),
            pltpu.VMEM((rows, count), BF16),
            pltpu.VMEM((rows, count), BF16),
            pltpu.VMEM((rows, count), BF16),
            dma((2,)),
            dma((2,)),
            dma((owners,)),
            pltpu.VMEM((2, PLANES, rows * (count // LOW), LOW), BF16),
            pltpu.VMEM(blocks, BF16),
            pltpu.VMEM(blocks, BF16),
            pltpu.VMEM(blocks, BF16),
            pltpu.VMEM(blocks, BF16),
            pltpu.VMEM((2, owners, 1, cap), jnp.int32),
            pltpu.VMEM((owners, 1, 128), jnp.int32),
            pltpu.VMEM((owners, 1, 128), jnp.int32),
            pltpu.VMEM(blocks, F32),
            pltpu.VMEM(blocks, F32),
            pltpu.VMEM((owners, 1, cap), F32),
            pltpu.VMEM(blocks, BF16),
            pltpu.VMEM(blocks, BF16),
            pltpu.VMEM(blocks, BF16),
            pltpu.VMEM((rows * (count // LOW), LOW), F32),
            pltpu.VMEM((rows, count), F32),
            pltpu.VMEM(grad_shape, F32),
            pltpu.VMEM((4, rows, 128), F32),
            pltpu.VMEM((devices, grad_shape[0] // reducers, grad_shape[1]), F32),
            pltpu.VMEM((3 * rows, rows), BF16),
            pltpu.VMEM((rows, rows), BF16),
            pltpu.VMEM((2 * rows, rows), BF16),
            pltpu.VMEM((rows, rows), BF16),
            pltpu.VMEM((rows, 16 * -(-(8 + masks.shape[0]) // 16)), F32),
            dma((2, 5, chunks)),
            dma((2, PLANES, chunks)),
            dma((2, PLANES)),
            dma((2, PLANES)),
            dma((2, owners)),
            dma((2, owners)),
            dma((2, owners)),
            dma((2, owners)),
            dma((owners,)),
            dma((owners,)),
            dma((reducers,)),
            dma((devices,)),
            dma((devices,)),
            dma((reducers,)),
        ],
        compiler_params=pltpu.CompilerParams(
            vmem_limit_bytes=VMEM_LIMIT, collective_id=0, has_side_effects=True
        ),
        cost_estimate=pl.CostEstimate(
            flops=64 * 2**30, bytes_accessed=16 * 2**20, transcendentals=4 * 2**20
        ),
        name="layer",
    )(counts, nodes, edges, target, senders, receivers, levels, land, masks, *weights)


def hand_out_kernel(edge_in, new_in, node_in, packed, edge_grad, new_nodes, node_grad, *rest):
    outs, (hold_edge, hold_new, hold_node, sems) = rest[:-4], rest[-4:]
    parts = []
    cuts = sems.shape[1] - 2
    wide = edge_in.shape[1] // cuts
    for c in range(cuts):
        here = pl.ds(c * wide, wide)
        parts.append((edge_in.at[:, here], hold_edge.at[:, here], edge_grad.at[:, here]))
    parts.append((new_in, hold_new, new_nodes))
    parts.append((node_in, hold_node, node_grad))
    ins = [pltpu.make_async_copy(a, b, sems.at[0, k]) for k, (a, b, _) in enumerate(parts)]
    backs = [pltpu.make_async_copy(b, c, sems.at[1, k]) for k, (_, b, c) in enumerate(parts)]
    for copy in ins:
        copy.start()
    rows = packed.shape[1] // 2
    lines = packed[3 * rows :, :].T
    edge_first, edge_b1, edge_second, edge_b2, edge_g, edge_h = outs[:6]
    node_first, node_b1, node_second, node_b2, node_g, node_h = outs[6:]
    edge_first[...] = packed[: 3 * rows, :].T[:rows, :]
    edge_second[...] = packed[3 * rows :, rows:]
    node_first[...] = packed[: 2 * rows, :].T[rows:, :]
    node_second[...] = packed[2 * rows : 3 * rows, rows:]
    for k, out in enumerate((edge_b1, edge_b2, edge_g, edge_h, node_b1, node_b2, node_g, node_h)):
        out[...] = lines[k, :rows]
    for copy, back in zip(ins, backs):
        copy.wait()
        back.start()
    for back in backs:
        back.wait()


def hand_out(new_nodes, node_grad, edge_grad, packed):
    rows = packed.shape[1] // 2
    cuts = 8
    vmem = pl.BlockSpec(memory_space=pltpu.VMEM)
    stay = pl.BlockSpec(memory_space=pl.ANY)
    shapes = [
        (rows, 3 * rows), (rows,), (rows, rows), (rows,), (rows,), (rows,),
        (rows, 2 * rows), (rows,), (rows, rows), (rows,), (rows,), (rows,),
    ]
    large = (edge_grad, new_nodes, node_grad)
    edge_grad, new_nodes, node_grad, *small = pl.pallas_call(
        hand_out_kernel,
        in_specs=[stay] * 3 + [vmem],
        out_specs=[stay] * 3 + [vmem] * len(shapes),
        out_shape=[jax.ShapeDtypeStruct(a.shape, a.dtype) for a in large]
        + [jax.ShapeDtypeStruct(s, F32) for s in shapes],
        scratch_shapes=[pltpu.VMEM(a.shape, a.dtype) for a in large]
        + [pltpu.SemaphoreType.DMA((2, cuts + 2))],
        compiler_params=pltpu.CompilerParams(vmem_limit_bytes=VMEM_LIMIT),
        name="hand_out",
    )(*large, packed)
    small[0], small[6] = small[0].T, small[6].T
    return (new_nodes, node_grad, edge_grad, *small)


def per_device(
    nodes, edges, target, senders, receivers, counts, levels, land, channel_mask,
    edge_in, edge_in_bias, edge_out, edge_out_bias, edge_gain, edge_shift,
    node_in, node_in_bias, node_out, node_out_bias, node_gain, node_shift,
):
    count = nodes.shape[1]
    owners = lax.axis_size("edge")
    cap = edges.shape[1] // owners
    return hand_out(
        *layer(
            counts, nodes, edges, target,
            senders.reshape(owners, 1, cap), receivers.reshape(owners, 1, cap),
            levels.reshape(1, count), land.reshape(1, count), channel_mask,
            edge_in.T, edge_out, node_in.T, node_out,
            edge_in_bias, edge_out_bias, edge_gain, edge_shift,
            node_in_bias, node_out_bias, node_gain, node_shift,
        )
    )


def solution(mesh):
    over = ("edge", "rep")
    wide, line, same = P(None, over), P(over), P()
    return jax.shard_map(
        per_device,
        mesh=mesh,
        in_specs=(wide, wide, wide, line, line, line, line, line) + (same,) * 13,
        out_specs=(wide, wide, wide) + (same,) * 12,
        check_vma=False,
    )
```

```python
import functools

import jax
import jax.numpy as jnp
from jax import lax
from jax.experimental import pallas as pl
from jax.experimental.pallas import tpu as pltpu
from jax.sharding import PartitionSpec as P

NORM_EPS = 1e-05
F32 = jnp.float32
BF16 = jnp.bfloat16
LOW = 256
VMEM_LIMIT = 60 * 2**20
PLANES = 4
EDGE_PLAN = {
    ('table', 1): ((1, 0), (1, 1), (1, 2), (1, 3)),
    ('table', 2): ((2, 0), (2, 1), (2, 2), (2, 3)),
    ('table', 3): ((3, 0),),
    ('edges', 0): ((3, 1),),
    ('edges', 2): ((3, 2),),
    ('edges', 5): ((3, 3),),
}
BACK_PLAN = {
    ('table', 1): ((1, 0), (1, 1), (1, 2), (1, 3)),
    ('table', 2): ((2, 0), (2, 1), (2, 2), (2, 3)),
    ('table', 3): ((3, 0),),
    ('sums', 1): ((3, 1),),
    ('sums', 7): ((3, 2),),
    ('finish', 2): ((3, 3),),
}
MESH = pl.DeviceIdType.MESH

EB1, EB2, EG, EH, NB1, NB2, NG, NH, CM = 0, 1, 2, 3, 4, 5, 6, 7, 8


def dot(a, b):
    return jnp.dot(a, b, preferred_element_type=F32)


def dot_tn(a, b):
    return lax.dot_general(a, b, (((0,), (0,)), ((), ())), preferred_element_type=F32)


def dot_nt(a, b):
    return lax.dot_general(a, b, (((1,), (1,)), ((), ())), preferred_element_type=F32)


def one_hot_low(ids):
    low = ids & (LOW - 1)
    rows = lax.broadcasted_iota(jnp.int32, (LOW, ids.shape[1]), 0)
    return (rows == low).astype(F32).astype(BF16)


def high_of(ids, rows):
    high = ids >> (LOW.bit_length() - 1)
    return jnp.broadcast_to(high.astype(F32).astype(BF16), (rows, ids.shape[1]))


def stack_table(table_ref, value):
    rows = value.shape[0]
    for h in range(value.shape[1] // LOW):
        table_ref[h * rows : (h + 1) * rows, :] = value[:, h * LOW : (h + 1) * LOW]


def gather_columns(table, ids, rows):
    picked = dot(table, one_hot_low(ids)).astype(BF16)
    high = high_of(ids, rows)
    out = picked[:rows]
    for h in range(1, table.shape[0] // rows):
        out = jnp.where(high == BF16(h), picked[h * rows : (h + 1) * rows], out)
    return out


def scatter_columns(values, ids, count):
    rows = values.shape[0]
    high = high_of(ids, rows)
    zero = jnp.zeros_like(values)
    spread = jnp.concatenate(
        [jnp.where(high == BF16(h), values, zero) for h in range(count // LOW)], axis=0
    )
    return dot_nt(spread, one_hot_low(ids))


def column(cols, index):
    return cols[:, index : index + 1]


def mean_rows(v):
    return jnp.mean(v, axis=0, keepdims=True)


def lane_sums(v):
    out = v[:, :128]
    for k in range(1, v.shape[1] // 128):
        out = out + v[:, k * 128 : (k + 1) * 128]
    return out


def branch_forward(w1t, w2t, b1, b2, stacked):
    pre = dot(w1t, stacked) + b1
    hidden = (pre * (1.0 / (1.0 + jnp.exp(-pre)))).astype(BF16)
    outer = dot(w2t, hidden) + b2
    shifted = outer - mean_rows(outer)
    inverse = lax.rsqrt(mean_rows(shifted * shifted) + NORM_EPS)
    return pre, shifted * inverse, inverse


def branch_backward(w2, gain, grad, pre, normal, inverse):
    q = grad * gain
    outer_grad = (
        inverse * (q - mean_rows(q) - normal * mean_rows(q * normal))
    ).astype(BF16)
    s = 1.0 / (1.0 + jnp.exp(-pre))
    pre_grad = (dot(w2, outer_grad) * (s * (1.0 + pre * (1.0 - s)))).astype(BF16)
    return outer_grad, pre_grad, (pre * s).astype(BF16)


def split_dot(low, wide):
    top = wide.astype(BF16)
    rest = (wide - top.astype(F32)).astype(BF16)
    return dot(low, top) + dot(low, rest)


def layer_kernel(
    levels_count, reps,
    counts, nodes, edges_in, target_in, senders, receivers, levels, land, masks, ew1t, ew2, nw1t,
    nw2,
    eb1, eb2, eg, eh, nb1, nb2, ng, nh,
    new_nodes, node_grad, edge_grad, summed,
    edges, target, new_hold, node_hold, in_sem, out_sem, grad_sem, tabs, send_a, recv_s, recv_e, mine, ids_tab, count_send, count_recv, pre_s, normal_s,
    inverse_s, recv_c, send_d, recv_d, total, part, grads, sums, pieces, ew1, ew2t, nw1, nw2t, cols,
    tab_send, tab_recv, ids_send, ids_recv, a_send, a_recv, b_send, b_recv, count_out, count_in,
    piece_send, piece_recv, sum_send, sum_recv,
):
    rows, count = nodes.shape
    owners, cap = senders.shape[0], senders.shape[2]
    ring = owners // PLANES
    high_count = count // LOW
    chunks = tab_recv.shape[2]
    chunk = tabs.shape[2] // chunks
    e, rep = lax.axis_index("edge"), lax.axis_index("rep")
    z, r = e // ring, e % ring
    me, devices = e * reps + rep, owners * reps
    upper = z // 2

    def plane_at(k):
        low = z + upper * (3 - 2 * z)
        turned = lax.rem(k + 1, 3) * (1 - k // 3) + 3 * (k // 3)
        place = k * (1 - low) + turned * low
        return place + upper * (3 - 2 * place)

    order = tuple(plane_at(k) for k in range(PLANES))
    middle = lax.rem(z, 3) != 0
    toward = 3 - 2 * z

    def at(plane, place):
        return (plane * ring + place, rep)

    def remote(src, dst, send, recv, device):
        return pltpu.make_async_remote_copy(
            src, dst, send, recv, device_id=device, device_id_type=MESH
        )

    def loop(low, high, body):
        def step(i, carry):
            body(i)
            return carry

        lax.fori_loop(low, high, step, 0)

    def others(body):
        def one(t):
            d = lax.rem(me + t, devices)
            body(d, (d // reps, lax.rem(d, reps)))

        loop(1, devices, one)

    load_edges = pltpu.make_async_copy(edges_in, edges, in_sem.at[0])
    load_target = pltpu.make_async_copy(target_in, target, in_sem.at[1])
    load_edges.start()
    load_target.start()

    barrier = pltpu.get_barrier_semaphore()
    others(
        lambda d, device: pl.semaphore_signal(
            barrier, inc=1, device_id=device, device_id_type=MESH
        )
    )

    stack_table(tabs.at[0, z], nodes[...])
    pl.semaphore_wait(barrier, devices - 1)

    def part_of(phase, plane, c):
        return tabs.at[phase, plane, pl.ds(c * chunk, chunk)]

    def table_copy(phase, plane, c, lane, to):
        return remote(
            part_of(phase, plane, c), part_of(phase, plane, c),
            tab_send.at[phase, lane, c], tab_recv.at[phase, plane, c], at(to, r),
        )

    def await_table(phase, plane, c):
        table_copy(phase, plane, c, 0, z).wait_recv()

    def send_own(phase, c):
        @pl.when(z < PLANES - 1)
        def _():
            table_copy(phase, z, c, 0, z + 1).start()

        @pl.when(z > 0)
        def _():
            table_copy(phase, z, c, 1, z - 1).start()

    def relay(phase, slot):
        @pl.when(middle)
        def _():
            for c in range(chunks):
                if slot == 0:
                    await_table(phase, z - toward, c)
                    table_copy(phase, z - toward, c, 2, z + toward).start()
                    await_table(phase, z + toward, c)
                    table_copy(phase, z + toward, c, 3, z - toward).start()
                else:
                    await_table(phase, z + 2 * toward, c)
                    table_copy(phase, z + 2 * toward, c, 4, z - toward).start()

    def end_wait(phase, k):
        @pl.when(jnp.logical_not(middle))
        def _():
            for c in range(chunks):
                await_table(phase, order[k], c)

    def drain_tables(phase):
        for c in range(chunks):
            @pl.when(z < PLANES - 1)
            def _():
                table_copy(phase, z, c, 0, z + 1).wait_send()

            @pl.when(z > 0)
            def _():
                table_copy(phase, z, c, 1, z - 1).wait_send()

            @pl.when(middle)
            def _():
                table_copy(phase, z - toward, c, 2, z + toward).wait_send()
                table_copy(phase, z + toward, c, 3, z - toward).wait_send()
                table_copy(phase, z + 2 * toward, c, 4, z - toward).wait_send()

    def ids_copy(phase, ids, k):
        plane = lax.rem(z + k, PLANES)
        return remote(
            ids.at[pl.ds(plane * ring, ring)], ids_tab.at[phase, pl.ds(z * ring, ring)],
            ids_send.at[phase, plane], ids_recv.at[phase, z], at(plane, r),
        )

    def ids_arrival(phase, plane):
        rows_of = ids_tab.at[phase, pl.ds(plane * ring, ring)]
        return remote(
            rows_of, rows_of, ids_send.at[phase, plane], ids_recv.at[phase, plane], at(plane, r)
        )

    def plane_copy(phase, plane, to, into):
        return remote(
            send_a.at[plane * ring + to], into.at[plane * ring + r],
            a_send.at[phase, plane * ring + to], a_recv.at[phase, plane * ring + r], at(z, to),
        )

    def plane_arrival(phase, j, into):
        return remote(
            send_a.at[j], into.at[j], a_send.at[phase, j], a_recv.at[phase, j], at(z, r)
        )

    def hand_over(phase, plane, to, t, got, into):
        @pl.when(t < ring)
        def _():
            send_a[plane * ring + to] = got
            plane_copy(phase, plane, to, into).start()

        @pl.when(t == ring)
        def _():
            into[plane * ring + r] = got

    def gather_step(phase, k, into):
        plane = plane_at(k)

        def two(ts):
            tos = [lax.rem(r + t + 1, ring) for t in ts]
            got = gather_columns(
                tabs[phase, plane],
                side_by_side([ids_tab[phase, plane * ring + to] for to in tos]), rows,
            )
            for i, (t, to) in enumerate(zip(ts, tos)):
                hand_over(phase, plane, to, t + 1, got[:, i * cap : (i + 1) * cap], into)

        in_pairs(two)

    def drain_planes(phase, into):
        for plane in range(PLANES):
            loop(1, ring, lambda t: plane_copy(phase, plane, lax.rem(r + t, ring), into).wait_send())

    def lanes(j):
        return pl.ds(pl.multiple_of(j * cap, cap), cap)

    def edges_copy(j):
        return remote(
            edges.at[:, lanes(j)], recv_e.at[e], b_send.at[0, j], b_recv.at[0, e], (j, rep)
        )

    def edges_arrival(a):
        return remote(
            edges.at[:, lanes(a)], recv_e.at[a], b_send.at[0, a], b_recv.at[0, a], (e, rep)
        )

    def count_copy(j):
        return remote(
            count_send.at[j], count_recv.at[e], count_out.at[j], count_in.at[e], (j, rep)
        )

    def count_arrival(a):
        return remote(
            count_send.at[a], count_recv.at[a], count_out.at[a], count_in.at[a], (e, rep)
        )

    def back_copy(a):
        return remote(
            send_d.at[a], recv_d.at[e], b_send.at[1, a], b_recv.at[1, e], (a, rep)
        )

    def back_arrival(j):
        return remote(
            send_d.at[j], recv_d.at[j], b_send.at[1, j], b_recv.at[1, j], (e, rep)
        )

    def peers(body):
        loop(1, owners, lambda t: body(lax.rem(e + t, owners)))

    def in_pairs(body):
        loop(0, ring // 2, lambda h: body((2 * h, 2 * h + 1)))

    def steps(body):
        loop(0, PLANES, body)

    def step_in_pairs(body, before):
        def one(i):
            k, h = i // (ring // 2), lax.rem(i, ring // 2)
            ts = (2 * h, 2 * h + 1)
            before(i)
            body(plane_at(k), ts, [k + t > 0 for t in ts])

        loop(0, PLANES * (ring // 2), one)

    def side_by_side(blocks):
        return jnp.concatenate(blocks, axis=1)

    def send_edges(k, low, high):
        loop(low, high, lambda t: edges_copy(order[k] * ring + lax.rem(r + t, ring)).start())

    place = lax.broadcasted_iota(jnp.int32, (1, cap), 1)

    def live_here(a):
        line = count_recv[a]
        wide = jnp.concatenate([line] * (cap // line.shape[1]), axis=1)
        return (place < wide).astype(F32)

    def edge_forward(a):
        own = recv_e[a]
        pre, normal, inverse = branch_forward(
            ew1t[...], ew2t[...], column(cols, EB1), column(cols, EB2),
            jnp.concatenate([own, recv_s[a], mine[a]], axis=0),
        )
        pre_s[a] = pre
        normal_s[a] = normal
        inverse_s[a] = inverse
        updated = own.astype(F32) + (normal * column(cols, EG) + column(cols, EH))
        return (updated * live_here(a)).astype(BF16)

    def forward_steps():
        def two(plane, ts, remotes):
            froms = [plane * ring + lax.rem(r + ring - t, ring) for t in ts]
            for t, a, there in zip(ts, froms, remotes):
                @pl.when(t > 0)
                def _():
                    plane_arrival(0, a, recv_s).wait_recv()

                @pl.when(there)
                def _():
                    count_arrival(a).wait_recv()
                    edges_arrival(a).wait_recv()

            total[...] += scatter_columns(
                side_by_side([edge_forward(a) for a in froms]),
                side_by_side([receivers[a] for a in froms]), count,
            )

        turns = PLANES * (ring // 2)
        step_in_pairs(two, lambda i: emit_at(EDGE_PLAN, "edges", i, turns, send_edges))

    def edge_backward(a, got):
        grad = got.astype(F32) * live_here(a)
        normal = normal_s[a]
        outer_grad, pre_grad, hidden = branch_backward(
            ew2[...], column(cols, EG), grad, pre_s[a], normal, inverse_s[a]
        )
        grads[...] += dot_nt(
            jnp.concatenate([recv_e[a], recv_s[a], mine[a], hidden], axis=0),
            jnp.concatenate([pre_grad, outer_grad], axis=0),
        )
        for k, v in enumerate((pre_grad.astype(F32), outer_grad.astype(F32), grad * normal, grad)):
            sums[k] += lane_sums(v)
        return pre_grad

    def backward_step(k):
        plane = plane_at(k)

        def two(ts):
            tos = [lax.rem(r + t + 1, ring) for t in ts]
            froms = [plane * ring + to for to in tos]
            both = gather_columns(
                tabs[1, z], side_by_side([receivers[a] for a in froms]), rows
            )
            for i, (t, to, a) in enumerate(zip(ts, tos, froms)):
                got = both[:, i * cap : (i + 1) * cap]

                @pl.when(k == 0)
                def _():
                    hand_over(1, z, to, t + 1, got, recv_c)

                send_d[a] = edge_backward(a, got)

        in_pairs(two)

    def send_back(k, low, high):
        loop(low, high, lambda t: back_copy(order[k] * ring + lax.rem(r + t, ring)).start())

    def emit(plan, slot, send):
        for k, q in plan.get(slot, ()):
            send(k, q * ring // 4, (q + 1) * ring // 4)

    def emit_at(plan, slot, turn, turns, send):
        for i in range(turns):
            if (slot, i) in plan:
                @pl.when(turn == i)
                def _():
                    emit(plan, (slot, i), send)

    for c in range(chunks):
        send_own(0, c)
    for k in range(1, PLANES):
        ids_copy(0, senders, k).start()
    load_edges.wait()
    send_edges(0, 1, ring)
    for j in range(owners):
        count_send[j] = jnp.full(count_send.shape[1:], counts[j], jnp.int32)
    peers(lambda j: count_copy(j).start())
    ids_tab[0, pl.ds(z * ring, ring)] = senders[pl.ds(z * ring, ring)]
    count_recv[e] = count_send[e]
    recv_e[e] = edges[:, lanes(e)]
    total[...] = jnp.zeros_like(total)
    grads[...] = jnp.zeros_like(grads)
    sums[...] = jnp.zeros_like(sums)

    def eye(n):
        return (
            lax.broadcasted_iota(jnp.int32, (n, n), 0) == lax.broadcasted_iota(jnp.int32, (n, n), 1)
        ).astype(F32).astype(BF16)

    unit = eye(rows)
    ew1[...] = dot_tn(ew1t[...], unit).astype(BF16)
    nw1[...] = dot_tn(nw1t[...], unit).astype(BF16)
    ew2t[...] = dot_tn(ew2[...], unit).astype(BF16)
    nw2t[...] = dot_tn(nw2[...], unit).astype(BF16)
    lines = [v[...].astype(F32)[None, :] for v in (eb1, eb2, eg, eh, nb1, nb2, ng, nh)]
    lines.append(masks[...].astype(F32))
    lines.append(jnp.zeros((-(8 + levels_count) % 16, rows), F32))
    cols[...] = dot_nt(unit, jnp.concatenate(lines, axis=0).astype(BF16))

    def forward_gathers(k):
        @pl.when(k == 1)
        def _():
            relay(0, 0)
            for other in range(1, PLANES):
                ids_arrival(0, order[other]).wait_recv()
            end_wait(0, 1)

        @pl.when(k == 2)
        def _():
            relay(0, 1)
            end_wait(0, 2)

        @pl.when(k == 3)
        def _():
            end_wait(0, 3)

        emit_at(EDGE_PLAN, "table", k, PLANES, send_edges)
        gather_step(0, k, recv_s)
        emit_at(EDGE_PLAN, "gather", k, PLANES, send_edges)

        def two(ts):
            js = [k * ring + t for t in ts]
            both = gather_columns(tabs[0, z], side_by_side([receivers[j] for j in js]), rows)
            for i, j in enumerate(js):
                mine[j] = both[:, i * cap : (i + 1) * cap]

        in_pairs(two)

    steps(forward_gathers)
    for k in range(1, PLANES):
        ids_copy(1, receivers, k).start()
    forward_steps()
    drain_planes(0, recv_s)

    load_target.wait()

    per = high_count // chunks
    wide = per * LOW
    node_first = jnp.zeros((2 * rows, rows), F32)
    node_second = jnp.zeros((rows, rows), F32)
    node_sums = [jnp.zeros((rows, 128), F32)] * 4
    for c in range(chunks):
        here = slice(c * wide, (c + 1) * wide)
        aggregate = jnp.concatenate(
            [total[h * rows : (h + 1) * rows, :] for h in range(c * per, (c + 1) * per)], axis=1
        ).astype(BF16)
        own = nodes[:, here]
        stacked = jnp.concatenate([own, aggregate], axis=0)
        pre, normal, inverse = branch_forward(
            nw1t[...], nw2t[...], column(cols, NB1), column(cols, NB2), stacked
        )
        gain = column(cols, NG)
        state = own.astype(F32) + (normal * gain + column(cols, NH))
        new_hold[:, here] = state.astype(BF16)
        weight = jnp.zeros((rows, wide), F32)
        for l in range(levels_count):
            weight = jnp.where(levels[:, here] == l, column(cols, CM + l), weight)
        weight = weight * land[:, here].astype(F32)
        grad = weight * (state - target[:, here].astype(F32))
        outer_grad, pre_grad, hidden = branch_backward(nw2[...], gain, grad, pre, normal, inverse)
        stacked_grad = dot(nw1[...], pre_grad)
        part[:, here] = grad + stacked_grad[:rows]
        low = stacked_grad[rows:].astype(BF16)
        for h in range(per):
            tabs[1, z, (c * per + h) * rows : (c * per + h + 1) * rows, :] = low[
                :, h * LOW : (h + 1) * LOW
            ]
        send_own(1, c)
        node_first = node_first + dot_nt(stacked, pre_grad)
        node_second = node_second + dot_nt(hidden, outer_grad)
        for k, v in enumerate((pre_grad.astype(F32), outer_grad.astype(F32), grad * normal, grad)):
            node_sums[k] = node_sums[k] + lane_sums(v)

    new_copy = pltpu.make_async_copy(new_hold, new_nodes, out_sem.at[0])
    new_copy.start()

    def backward_steps(k):
        backward_step(k)

        @pl.when(k == 0)
        def _():
            send_back(0, 1, ring)

        @pl.when(k == 1)
        def _():
            relay(1, 0)
            for other in range(1, PLANES):
                ids_arrival(1, order[other]).wait_recv()
            end_wait(1, 1)

        @pl.when(k == 2)
        def _():
            relay(1, 1)
            end_wait(1, 2)

        @pl.when(k == 3)
        def _():
            end_wait(1, 3)

        emit_at(BACK_PLAN, "table", k, PLANES, send_back)

        @pl.when(k > 0)
        def _():
            gather_step(1, k, recv_c)

        emit_at(BACK_PLAN, "gather", k, PLANES, send_back)

    steps(backward_steps)
    total[...] = jnp.zeros_like(total)

    def by_receiver(h):
        emit_at(BACK_PLAN, "sums", h, owners // 2, send_back)
        total[...] += scatter_columns(
            side_by_side([send_d[2 * h], send_d[2 * h + 1]]),
            side_by_side([receivers[2 * h], receivers[2 * h + 1]]), count,
        )

    loop(0, owners // 2, by_receiver)

    grads[: 2 * rows, rows:] = node_first
    grads[2 * rows : 3 * rows, rows:] = node_second
    grads[3 * rows :, :8] = jnp.concatenate(
        [sums[k].sum(axis=1, keepdims=True) for k in range(4)]
        + [v.sum(axis=1, keepdims=True) for v in node_sums],
        axis=1,
    )
    reducers = min(devices, grads.shape[0] // 8)
    height = grads.shape[0] // reducers

    def piece(d):
        return pl.ds(pl.multiple_of(d * height, 8), height)

    def piece_copy(d, device):
        return remote(
            grads.at[piece(d)], pieces.at[me], piece_send.at[d], piece_recv.at[me], device
        )

    def piece_arrival(d):
        return remote(
            grads.at[piece(0)], pieces.at[d], piece_send.at[0], piece_recv.at[d], (e, rep)
        )

    def sum_copy(d, device):
        return remote(
            summed.at[piece(me)], summed.at[piece(me)], sum_send.at[d], sum_recv.at[me], device
        )

    def sum_arrival(d):
        return remote(
            summed.at[piece(d)], summed.at[piece(d)], sum_send.at[0], sum_recv.at[d], (e, rep)
        )

    def to_reducers(body):
        def one(d, device):
            if reducers == devices:
                body(d, device)
            else:
                @pl.when(d < reducers)
                def _():
                    body(d, device)

        others(one)

    def as_reducer(body):
        if reducers == devices:
            body()
        else:
            pl.when(me < reducers)(body)

    to_reducers(lambda d, device: piece_copy(d, device).start())
    def node_total(w_rows):
        for h in range(high_count):
            here = slice(h * LOW, (h + 1) * LOW)
            part[:, here] += split_dot(ew1[w_rows, :], total[h * rows : (h + 1) * rows, :])

    node_total(slice(2 * rows, 3 * rows))
    total[...] = jnp.zeros_like(total)

    @as_reducer
    def _():
        pieces[me] = grads[piece(me), :]
        others(lambda d, device: piece_arrival(d).wait_recv())

        def add(d, running):
            return running + pieces[d]

        summed[piece(me), :] = lax.fori_loop(1, devices, add, pieces[0])
        others(lambda d, device: sum_copy(d, device).start())

    def grad_copy(j):
        return pltpu.make_async_copy(recv_c.at[j], edge_grad.at[:, lanes(j)], grad_sem.at[j])

    def finish_edges(j, pre_grad):
        grad = recv_c[j].astype(F32) * (place < counts[j]).astype(F32)
        recv_c[j] = (grad + dot(ew1[:rows, :], pre_grad)).astype(BF16)
        grad_copy(j).start()

    recv_d[e] = send_d[e]

    def finish(plane, ts, remotes):
        js = [plane * ring + lax.rem(r + ring - t, ring) for t in ts]
        for t, j, there in zip(ts, js, remotes):
            @pl.when(t > 0)
            def _():
                plane_arrival(1, j, recv_c).wait_recv()

            @pl.when(there)
            def _():
                back_arrival(j).wait_recv()

            finish_edges(j, recv_d[j])
        total[...] += scatter_columns(
            side_by_side([recv_d[j] for j in js]), side_by_side([senders[j] for j in js]), count
        )

    turns = PLANES * (ring // 2)
    step_in_pairs(finish, lambda i: emit_at(BACK_PLAN, "finish", i, turns, send_back))
    node_total(slice(rows, 2 * rows))
    node_hold[...] = part[...].astype(BF16)
    node_copy = pltpu.make_async_copy(node_hold, node_grad, out_sem.at[1])
    node_copy.start()

    drain_tables(0)
    drain_tables(1)
    drain_planes(1, recv_c)
    for k in range(1, PLANES):
        ids_copy(0, senders, k).wait_send()
        ids_copy(1, receivers, k).wait_send()
    peers(lambda j: count_copy(j).wait_send())
    peers(lambda j: edges_copy(j).wait_send())
    peers(lambda j: back_copy(j).wait_send())
    to_reducers(lambda d, device: piece_copy(d, device).wait_send())

    @as_reducer
    def _():
        others(lambda d, device: sum_copy(d, device).wait_send())

    to_reducers(lambda d, device: sum_arrival(d).wait_recv())
    loop(0, owners, lambda j: grad_copy(j).wait())
    new_copy.wait()
    node_copy.wait()


def layer(counts, nodes, edges, target, senders, receivers, levels, land, masks, *weights):
    rows, count = nodes.shape
    owners, _, cap = senders.shape
    slots = edges.shape[1]
    reps = lax.axis_size("rep")
    devices = owners * reps
    chunks = 4 if count // LOW % 4 == 0 else 1
    grad_shape = (4 * rows, 2 * rows)
    reducers = min(devices, grad_shape[0] // 8)
    blocks = (owners, rows, cap)
    dma = pltpu.SemaphoreType.DMA
    vmem = pl.BlockSpec(memory_space=pltpu.VMEM)
    stay = pl.BlockSpec(memory_space=pl.ANY)
    return pl.pallas_call(
        functools.partial(layer_kernel, masks.shape[0], reps),
        in_specs=[pl.BlockSpec(memory_space=pltpu.SMEM), vmem, stay, stay]
        + [vmem] * (5 + len(weights)),
        out_specs=[stay, stay, stay, vmem],
        out_shape=[
            jax.ShapeDtypeStruct((rows, count), BF16),
            jax.ShapeDtypeStruct((rows, count), BF16),
            jax.ShapeDtypeStruct((rows, slots), BF16),
            jax.ShapeDtypeStruct(grad_shape, F32),
        ],
        scratch_shapes=[
            pltpu.VMEM((rows, slots), BF16),
            pltpu.VMEM((rows, count), BF16),
            pltpu.VMEM((rows, count), BF16),
            pltpu.VMEM((rows, count), BF16),
            dma((2,)),
            dma((2,)),
            dma((owners,)),
            pltpu.VMEM((2, PLANES, rows * (count // LOW), LOW), BF16),
            pltpu.VMEM(blocks, BF16),
            pltpu.VMEM(blocks, BF16),
            pltpu.VMEM(blocks, BF16),
            pltpu.VMEM(blocks, BF16),
            pltpu.VMEM((2, owners, 1, cap), jnp.int32),
            pltpu.VMEM((owners, 1, 128), jnp.int32),
            pltpu.VMEM((owners, 1, 128), jnp.int32),
            pltpu.VMEM(blocks, F32),
            pltpu.VMEM(blocks, F32),
            pltpu.VMEM((owners, 1, cap), F32),
            pltpu.VMEM(blocks, BF16),
            pltpu.VMEM(blocks, BF16),
            pltpu.VMEM(blocks, BF16),
            pltpu.VMEM((rows * (count // LOW), LOW), F32),
            pltpu.VMEM((rows, count), F32),
            pltpu.VMEM(grad_shape, F32),
            pltpu.VMEM((4, rows, 128), F32),
            pltpu.VMEM((devices, grad_shape[0] // reducers, grad_shape[1]), F32),
            pltpu.VMEM((3 * rows, rows), BF16),
            pltpu.VMEM((rows, rows), BF16),
            pltpu.VMEM((2 * rows, rows), BF16),
            pltpu.VMEM((rows, rows), BF16),
            pltpu.VMEM((rows, 16 * -(-(8 + masks.shape[0]) // 16)), F32),
            dma((2, 5, chunks)),
            dma((2, PLANES, chunks)),
            dma((2, PLANES)),
            dma((2, PLANES)),
            dma((2, owners)),
            dma((2, owners)),
            dma((2, owners)),
            dma((2, owners)),
            dma((owners,)),
            dma((owners,)),
            dma((reducers,)),
            dma((devices,)),
            dma((devices,)),
            dma((reducers,)),
        ],
        compiler_params=pltpu.CompilerParams(
            vmem_limit_bytes=VMEM_LIMIT, collective_id=0, has_side_effects=True
        ),
        cost_estimate=pl.CostEstimate(
            flops=64 * 2**30, bytes_accessed=16 * 2**20, transcendentals=4 * 2**20
        ),
        name="layer",
    )(counts, nodes, edges, target, senders, receivers, levels, land, masks, *weights)


def hand_out_kernel(edge_in, new_in, node_in, packed, edge_grad, new_nodes, node_grad, *outs):
    edge_grad[...] = edge_in[...]
    new_nodes[...] = new_in[...]
    node_grad[...] = node_in[...]
    rows = packed.shape[1] // 2
    lines = packed[3 * rows :, :].T
    edge_first, edge_b1, edge_second, edge_b2, edge_g, edge_h = outs[:6]
    node_first, node_b1, node_second, node_b2, node_g, node_h = outs[6:]
    edge_first[...] = packed[: 3 * rows, :].T[:rows, :]
    edge_second[...] = packed[3 * rows :, rows:]
    node_first[...] = packed[: 2 * rows, :].T[rows:, :]
    node_second[...] = packed[2 * rows : 3 * rows, rows:]
    for k, out in enumerate((edge_b1, edge_b2, edge_g, edge_h, node_b1, node_b2, node_g, node_h)):
        out[...] = lines[k, :rows]


def hand_out(new_nodes, node_grad, edge_grad, packed):
    rows = packed.shape[1] // 2
    vmem = pl.BlockSpec(memory_space=pltpu.VMEM)
    shapes = [
        (rows, 3 * rows), (rows,), (rows, rows), (rows,), (rows,), (rows,),
        (rows, 2 * rows), (rows,), (rows, rows), (rows,), (rows,), (rows,),
    ]
    large = (edge_grad, new_nodes, node_grad)
    edge_grad, new_nodes, node_grad, *small = pl.pallas_call(
        hand_out_kernel,
        in_specs=[vmem] * 4,
        out_specs=[vmem] * (3 + len(shapes)),
        out_shape=[jax.ShapeDtypeStruct(a.shape, a.dtype) for a in large]
        + [jax.ShapeDtypeStruct(s, F32) for s in shapes],
        compiler_params=pltpu.CompilerParams(vmem_limit_bytes=VMEM_LIMIT),
        name="hand_out",
    )(*large, packed)
    small[0], small[6] = small[0].T, small[6].T
    return (new_nodes, node_grad, edge_grad, *small)


def per_device(
    nodes, edges, target, senders, receivers, counts, levels, land, channel_mask,
    edge_in, edge_in_bias, edge_out, edge_out_bias, edge_gain, edge_shift,
    node_in, node_in_bias, node_out, node_out_bias, node_gain, node_shift,
):
    count = nodes.shape[1]
    owners = lax.axis_size("edge")
    cap = edges.shape[1] // owners
    return hand_out(
        *layer(
            counts, nodes, edges, target,
            senders.reshape(owners, 1, cap), receivers.reshape(owners, 1, cap),
            levels.reshape(1, count), land.reshape(1, count), channel_mask,
            edge_in.T, edge_out, node_in.T, node_out,
            edge_in_bias, edge_out_bias, edge_gain, edge_shift,
            node_in_bias, node_out_bias, node_gain, node_shift,
        )
    )


def solution(mesh):
    over = ("edge", "rep")
    wide, line, same = P(None, over), P(over), P()
    return jax.shard_map(
        per_device,
        mesh=mesh,
        in_specs=(wide, wide, wide, line, line, line, line, line) + (same,) * 13,
        out_specs=(wide, wide, wide) + (same,) * 12,
        check_vma=False,
    )
```

```python
import functools
import math

import jax
import jax.numpy as jnp
from jax import lax
from jax.experimental import pallas as pl
from jax.experimental.pallas import tpu as pltpu
from jax.sharding import PartitionSpec as P

NORM_EPS = 1e-05
F32 = jnp.float32
BF16 = jnp.bfloat16
LOW = 256
VMEM_LIMIT = 60 * 2**20
PLANES = 4
LAG = 3
TABLE_PARTS = 4
NODE_PARTS = 4
EDGE_PLAN = {
    ('table', 1): ((1, 0), (1, 1), (1, 2), (1, 3)),
    ('table', 2): ((2, 0), (2, 1), (2, 2), (2, 3)),
    ('edges', 0): ((3, 0),),
    ('table', 3): ((3, 1),),
    ('edges', 2): ((3, 2),),
    ('edges', 4): ((3, 3),),
}
BACK_PLAN = {
    ('table', 1): ((1, 0), (1, 1), (1, 2), (1, 3)),
    ('table', 2): ((2, 0), (2, 1), (2, 2), (2, 3)),
    ('table', 3): ((3, 0),),
    ('gather', 3): ((3, 1),),
    ('finish', 1): ((3, 2),),
    ('finish', 3): ((3, 3),),
}
MESH = pl.DeviceIdType.MESH

EB1, EB2, EG, EH, NB1, NB2, NG, NH, CM = 0, 1, 2, 3, 4, 5, 6, 7, 8


def dot(a, b):
    return jnp.dot(a, b, preferred_element_type=F32)


def dot_tn(a, b):
    return lax.dot_general(a, b, (((0,), (0,)), ((), ())), preferred_element_type=F32)


def dot_nt(a, b):
    return lax.dot_general(a, b, (((1,), (1,)), ((), ())), preferred_element_type=F32)


def one_hot_low(ids):
    low = ids & (LOW - 1)
    rows = lax.broadcasted_iota(jnp.int32, (LOW, ids.shape[1]), 0)
    return (rows == low).astype(F32).astype(BF16)


def high_of(ids, rows):
    high = ids >> (LOW.bit_length() - 1)
    return jnp.broadcast_to(high.astype(F32).astype(BF16), (rows, ids.shape[1]))


def stack_table(table_ref, value):
    rows = value.shape[0]
    for h in range(value.shape[1] // LOW):
        table_ref[h * rows : (h + 1) * rows, :] = value[:, h * LOW : (h + 1) * LOW]


def gather_columns(table, ids, rows):
    picked = dot(table, one_hot_low(ids)).astype(BF16)
    high = high_of(ids, rows)
    out = picked[:rows]
    for h in range(1, table.shape[0] // rows):
        out = jnp.where(high == BF16(h), picked[h * rows : (h + 1) * rows], out)
    return out


def scatter_columns(values, ids, count):
    rows = values.shape[0]
    high = high_of(ids, rows)
    zero = jnp.zeros_like(values)
    spread = jnp.concatenate(
        [jnp.where(high == BF16(h), values, zero) for h in range(count // LOW)], axis=0
    )
    return dot_nt(spread, one_hot_low(ids))


def column(cols, index):
    return cols[:, index : index + 1]


def mean_rows(v):
    return jnp.mean(v, axis=0, keepdims=True)


def lane_sums(v):
    out = v[:, :128]
    for k in range(1, v.shape[1] // 128):
        out = out + v[:, k * 128 : (k + 1) * 128]
    return out


def branch_forward(w1t, w2t, b1, b2, stacked):
    pre = dot(w1t, stacked) + b1
    hidden = (pre * (1.0 / (1.0 + jnp.exp(-pre)))).astype(BF16)
    outer = dot(w2t, hidden) + b2
    shifted = outer - mean_rows(outer)
    inverse = lax.rsqrt(mean_rows(shifted * shifted) + NORM_EPS)
    return pre, shifted * inverse, inverse


def branch_backward(w2, gain, grad, pre, normal, inverse):
    q = grad * gain
    outer_grad = (
        inverse * (q - mean_rows(q) - normal * mean_rows(q * normal))
    ).astype(BF16)
    s = 1.0 / (1.0 + jnp.exp(-pre))
    pre_grad = (dot(w2, outer_grad) * (s * (1.0 + pre * (1.0 - s)))).astype(BF16)
    return outer_grad, pre_grad, (pre * s).astype(BF16)


def split_dot(low, wide):
    top = wide.astype(BF16)
    rest = (wide - top.astype(F32)).astype(BF16)
    return dot(low, top) + dot(low, rest)


def layer_kernel(
    levels_count, reps,
    counts, nodes, edges_in, target_in, senders, receivers, levels, land, masks, ew1t, ew2, nw1t,
    nw2,
    eb1, eb2, eg, eh, nb1, nb2, ng, nh,
    new_nodes, node_grad, edge_grad, summed,
    edges, target, new_hold, node_hold, in_sem, out_sem, grad_sem, tabs, send_a, recv_s, recv_e, mine, ids_tab, count_send, count_recv, pre_s, normal_s,
    inverse_s, recv_c, send_d, recv_d, total, part, grads, sums, pieces, ew1, ew2t, nw1, nw2t, cols,
    tab_send, tab_recv, ids_send, ids_recv, a_send, a_recv, b_send, b_recv, count_out, count_in,
    plane_sums, piece_send, piece_recv, plane_send, plane_recv, sum_send, sum_recv,
):
    rows, count = nodes.shape
    owners = count_send.shape[0]
    cap = senders.shape[0] * senders.shape[1] // owners
    lines_of = cap // senders.shape[1]
    ring = owners // PLANES
    high_count = count // LOW
    chunks = tab_recv.shape[2]
    chunk = tabs.shape[2] // chunks
    e, rep = lax.axis_index("edge"), lax.axis_index("rep")
    z, r = e // ring, e % ring
    upper = z // 2

    def plane_at(k):
        low = z + upper * (3 - 2 * z)
        turned = lax.rem(k + 1, 3) * (1 - k // 3) + 3 * (k // 3)
        place = k * (1 - low) + turned * low
        return place + upper * (3 - 2 * place)

    order = tuple(plane_at(k) for k in range(PLANES))
    middle = lax.rem(z, 3) != 0
    toward = 3 - 2 * z

    def at(plane, place):
        return (plane * ring + place, rep)

    def remote(src, dst, send, recv, device):
        return pltpu.make_async_remote_copy(
            src, dst, send, recv, device_id=device, device_id_type=MESH
        )

    def loop(low, high, body):
        def step(i, carry):
            body(i)
            return carry

        lax.fori_loop(low, high, step, 0)

    group, mine_of_group = ring * reps, r * reps + rep

    def group_device(g):
        return (z * ring + g // reps, lax.rem(g, reps))

    def others(body):
        def one(t):
            g = lax.rem(mine_of_group + t, group)
            body(g, group_device(g))

        loop(1, group, one)

    load_edges = pltpu.make_async_copy(edges_in, edges, in_sem.at[0])
    load_target = pltpu.make_async_copy(target_in, target, in_sem.at[1])
    load_edges.start()
    load_target.start()

    barrier = pltpu.get_barrier_semaphore()

    def greet(device):
        pl.semaphore_signal(barrier, inc=1, device_id=device, device_id_type=MESH)

    loop(1, owners, lambda t: greet((lax.rem(e + t, owners), rep)))

    def greet_other_cores(t):
        loop(0, ring, lambda place: greet((z * ring + place, lax.rem(rep + t, reps))))

    loop(1, reps, greet_other_cores)
    stack_table(tabs.at[0, z], nodes[...])
    pl.semaphore_wait(barrier, owners - 1 + ring * (reps - 1))

    def part_of(phase, plane, c):
        return tabs.at[phase, plane, pl.ds(c * chunk, chunk)]

    def table_copy(phase, plane, c, lane, to):
        return remote(
            part_of(phase, plane, c), part_of(phase, plane, c),
            tab_send.at[phase, lane, c], tab_recv.at[phase, plane, c], at(to, r),
        )

    def await_table(phase, plane, c):
        table_copy(phase, plane, c, 0, z).wait_recv()

    def send_own(phase, c):
        @pl.when(z < PLANES - 1)
        def _():
            table_copy(phase, z, c, 0, z + 1).start()

        @pl.when(z > 0)
        def _():
            table_copy(phase, z, c, 1, z - 1).start()

    def relay(phase, slot, low=0, high=None):
        @pl.when(middle)
        def _():
            for c in range(low, chunks if high is None else high):
                if slot == 0:
                    await_table(phase, z - toward, c)
                    table_copy(phase, z - toward, c, 2, z + toward).start()
                    await_table(phase, z + toward, c)
                    table_copy(phase, z + toward, c, 3, z - toward).start()
                else:
                    await_table(phase, z + 2 * toward, c)
                    table_copy(phase, z + 2 * toward, c, 4, z - toward).start()

    def end_wait(phase, k):
        @pl.when(jnp.logical_not(middle))
        def _():
            for c in range(chunks):
                await_table(phase, order[k], c)

    def drain_tables(phase):
        for c in range(chunks):
            @pl.when(z < PLANES - 1)
            def _():
                table_copy(phase, z, c, 0, z + 1).wait_send()

            @pl.when(z > 0)
            def _():
                table_copy(phase, z, c, 1, z - 1).wait_send()

            @pl.when(middle)
            def _():
                table_copy(phase, z - toward, c, 2, z + toward).wait_send()
                table_copy(phase, z + toward, c, 3, z - toward).wait_send()
                table_copy(phase, z + 2 * toward, c, 4, z - toward).wait_send()

    def ids_rows(plane):
        size = ring * lines_of
        return pl.ds(pl.multiple_of(plane * size, size), size)

    def ids_of(ids, j):
        block = ids[pl.ds(pl.multiple_of(j * lines_of, lines_of), lines_of), :]
        return side_by_side([block[i : i + 1] for i in range(lines_of)])

    def ids_copy(phase, ids, k):
        plane = lax.rem(z + k, PLANES)
        return remote(
            ids.at[ids_rows(plane)], ids_tab.at[phase, ids_rows(z)],
            ids_send.at[phase, plane], ids_recv.at[phase, z], at(plane, r),
        )

    def ids_arrival(phase, plane):
        rows_of = ids_tab.at[phase, ids_rows(plane)]
        return remote(
            rows_of, rows_of, ids_send.at[phase, plane], ids_recv.at[phase, plane], at(plane, r)
        )

    def plane_copy(phase, plane, to, into):
        return remote(
            send_a.at[plane * ring + to], into.at[plane * ring + r],
            a_send.at[phase, plane * ring + to], a_recv.at[phase, plane * ring + r], at(z, to),
        )

    def plane_arrival(phase, j, into):
        return remote(
            send_a.at[j], into.at[j], a_send.at[phase, j], a_recv.at[phase, j], at(z, r)
        )

    def hand_over(phase, plane, to, t, got, into):
        @pl.when(t < ring)
        def _():
            send_a[plane * ring + to] = got
            plane_copy(phase, plane, to, into).start()

        @pl.when(t == ring)
        def _():
            into[plane * ring + r] = got

    def gather_step(phase, k, into):
        plane = plane_at(k)

        def two(ts):
            tos = [lax.rem(r + t + 1, ring) for t in ts]
            got = gather_columns(
                tabs[phase, plane],
                side_by_side([ids_of(ids_tab.at[phase], plane * ring + to) for to in tos]), rows,
            )
            for i, (t, to) in enumerate(zip(ts, tos)):
                hand_over(phase, plane, to, t + 1, got[:, i * cap : (i + 1) * cap], into)

        in_pairs(two)

    def drain_planes(phase, into):
        for plane in range(PLANES):
            loop(1, ring, lambda t: plane_copy(phase, plane, lax.rem(r + t, ring), into).wait_send())

    def lanes(j):
        return pl.ds(pl.multiple_of(j * cap, cap), cap)

    def edges_copy(j):
        return remote(
            edges.at[:, lanes(j)], recv_e.at[e], b_send.at[0, j], b_recv.at[0, e], (j, rep)
        )

    def edges_arrival(a):
        return remote(
            edges.at[:, lanes(a)], recv_e.at[a], b_send.at[0, a], b_recv.at[0, a], (e, rep)
        )

    def count_copy(j):
        return remote(
            count_send.at[j], count_recv.at[e], count_out.at[j], count_in.at[e], (j, rep)
        )

    def count_arrival(a):
        return remote(
            count_send.at[a], count_recv.at[a], count_out.at[a], count_in.at[a], (e, rep)
        )

    def back_copy(a):
        return remote(
            send_d.at[a], recv_d.at[e], b_send.at[1, a], b_recv.at[1, e], (a, rep)
        )

    def back_arrival(j):
        return remote(
            send_d.at[j], recv_d.at[j], b_send.at[1, j], b_recv.at[1, j], (e, rep)
        )

    def peers(body):
        loop(1, owners, lambda t: body(lax.rem(e + t, owners)))

    def in_pairs(body):
        loop(0, ring // 2, lambda h: body((2 * h, 2 * h + 1)))

    def pairs_of(k, body):
        half = ring // 2

        def one(h):
            ts = (2 * h, 2 * h + 1)
            body(k * half + h, plane_at(k), ts, [k + t > 0 for t in ts])

        loop(0, half, one)

    def side_by_side(blocks):
        return jnp.concatenate(blocks, axis=1)

    def send_edges(k, low, high):
        loop(low, high, lambda t: edges_copy(order[k] * ring + lax.rem(r + t, ring)).start())

    place = lax.broadcasted_iota(jnp.int32, (1, cap), 1)

    def live_here(a):
        line = count_recv[a]
        wide = jnp.concatenate([line] * (cap // line.shape[1]), axis=1)
        return (place < wide).astype(F32)

    def edge_forward(a):
        own = recv_e[a]
        pre, normal, inverse = branch_forward(
            ew1t[...], ew2t[...], column(cols, EB1), column(cols, EB2),
            jnp.concatenate([own, recv_s[a], mine[a]], axis=0),
        )
        pre_s[a] = pre
        normal_s[a] = normal
        inverse_s[a] = inverse
        updated = own.astype(F32) + (normal * column(cols, EG) + column(cols, EH))
        return (updated * live_here(a)).astype(BF16)

    turns = PLANES * (ring // 2)

    def forward_pair(turn, plane, ts, remotes):
        emit_at(EDGE_PLAN, "edges", turn, turns, send_edges)
        froms = [plane * ring + lax.rem(r + ring - t, ring) for t in ts]
        for t, a, there in zip(ts, froms, remotes):
            @pl.when(t > 0)
            def _():
                plane_arrival(0, a, recv_s).wait_recv()

            @pl.when(there)
            def _():
                count_arrival(a).wait_recv()
                edges_arrival(a).wait_recv()

        total[...] += scatter_columns(
            side_by_side([edge_forward(a) for a in froms]),
            side_by_side([ids_of(receivers, a) for a in froms]), count,
        )

    def edge_backward(a, got):
        grad = got.astype(F32) * live_here(a)
        normal = normal_s[a]
        outer_grad, pre_grad, hidden = branch_backward(
            ew2[...], column(cols, EG), grad, pre_s[a], normal, inverse_s[a]
        )
        grads[...] += dot_nt(
            jnp.concatenate([recv_e[a], recv_s[a], mine[a], hidden], axis=0),
            jnp.concatenate([pre_grad, outer_grad], axis=0),
        )
        for k, v in enumerate((pre_grad.astype(F32), outer_grad.astype(F32), grad * normal, grad)):
            sums[k] += lane_sums(v)
        return pre_grad

    def backward_step(k):
        plane = plane_at(k)

        def two(ts):
            tos = [lax.rem(r + t + 1, ring) for t in ts]
            froms = [plane * ring + to for to in tos]
            both = gather_columns(
                tabs[1, z], side_by_side([ids_of(receivers, a) for a in froms]), rows
            )
            for i, (t, to, a) in enumerate(zip(ts, tos, froms)):
                got = both[:, i * cap : (i + 1) * cap]

                @pl.when(k == 0)
                def _():
                    hand_over(1, z, to, t + 1, got, recv_c)

                send_d[a] = edge_backward(a, got)

        in_pairs(two)

    def send_back(k, low, high):
        loop(low, high, lambda t: back_copy(order[k] * ring + lax.rem(r + t, ring)).start())

    def emit(plan, slot, send):
        for k, q in plan.get(slot, ()):
            send(k, q * ring // 4, (q + 1) * ring // 4)

    def emit_at(plan, slot, turn, turns, send):
        for i in range(turns):
            if (slot, i) in plan:
                @pl.when(turn == i)
                def _():
                    emit(plan, (slot, i), send)

    for c in range(chunks):
        send_own(0, c)
    for k in range(1, PLANES):
        ids_copy(0, senders, k).start()
    load_edges.wait()
    send_edges(0, 1, ring)
    for j in range(owners):
        count_send[j] = jnp.full(count_send.shape[1:], counts[j], jnp.int32)
    peers(lambda j: count_copy(j).start())
    for k in range(1, PLANES):
        ids_copy(1, receivers, k).start()
    ids_tab[0, ids_rows(z)] = senders[ids_rows(z)]
    count_recv[e] = count_send[e]
    recv_e[e] = edges[:, lanes(e)]
    total[...] = jnp.zeros_like(total)
    grads[...] = jnp.zeros_like(grads)
    sums[...] = jnp.zeros_like(sums)

    def eye(n):
        return (
            lax.broadcasted_iota(jnp.int32, (n, n), 0) == lax.broadcasted_iota(jnp.int32, (n, n), 1)
        ).astype(F32).astype(BF16)

    unit = eye(rows)
    ew1[...] = dot_tn(ew1t[...], unit).astype(BF16)
    nw1[...] = dot_tn(nw1t[...], unit).astype(BF16)
    ew2t[...] = dot_tn(ew2[...], unit).astype(BF16)
    nw2t[...] = dot_tn(nw2[...], unit).astype(BF16)
    lines = [v[...].astype(F32)[None, :] for v in (eb1, eb2, eg, eh, nb1, nb2, ng, nh)]
    lines.append(masks[...].astype(F32))
    lines.append(jnp.zeros((-(8 + levels_count) % 16, rows), F32))
    cols[...] = dot_nt(unit, jnp.concatenate(lines, axis=0).astype(BF16))

    def forward_gathers(k):
        @pl.when(k == 1)
        def _():
            relay(0, 0)
            for other in range(1, PLANES):
                ids_arrival(0, order[other]).wait_recv()
            end_wait(0, 1)

        @pl.when(k == 2)
        def _():
            relay(0, 1)
            end_wait(0, 2)

        @pl.when(k == 3)
        def _():
            end_wait(0, 3)

        emit_at(EDGE_PLAN, "table", k, PLANES, send_edges)
        gather_step(0, k, recv_s)
        emit_at(EDGE_PLAN, "gather", k, PLANES, send_edges)

        def two(ts):
            js = [plane_at(k) * ring + t for t in ts]
            both = gather_columns(tabs[0, z], side_by_side([ids_of(receivers, j) for j in js]), rows)
            for i, j in enumerate(js):
                mine[j] = both[:, i * cap : (i + 1) * cap]

        in_pairs(two)

    def forward_steps(k):
        @pl.when(k >= LAG)
        def _():
            pairs_of(k - LAG, forward_pair)

        @pl.when(k < PLANES)
        def _():
            forward_gathers(k)

    loop(0, PLANES + LAG, forward_steps)
    drain_planes(0, recv_s)

    load_target.wait()

    node_parts = math.gcd(high_count, NODE_PARTS)
    per = high_count // node_parts
    wide = per * LOW
    node_first = jnp.zeros((2 * rows, rows), F32)
    node_second = jnp.zeros((rows, rows), F32)
    node_sums = [jnp.zeros((rows, 128), F32)] * 4
    for c in range(node_parts):
        here = slice(c * wide, (c + 1) * wide)
        aggregate = jnp.concatenate(
            [total[h * rows : (h + 1) * rows, :] for h in range(c * per, (c + 1) * per)], axis=1
        ).astype(BF16)
        own = nodes[:, here]
        stacked = jnp.concatenate([own, aggregate], axis=0)
        pre, normal, inverse = branch_forward(
            nw1t[...], nw2t[...], column(cols, NB1), column(cols, NB2), stacked
        )
        gain = column(cols, NG)
        state = own.astype(F32) + (normal * gain + column(cols, NH))
        new_hold[:, here] = state.astype(BF16)
        weight = jnp.zeros((rows, wide), F32)
        for l in range(levels_count):
            weight = jnp.where(levels[:, here] == l, column(cols, CM + l), weight)
        weight = weight * land[:, here].astype(F32)
        grad = weight * (state - target[:, here].astype(F32))
        outer_grad, pre_grad, hidden = branch_backward(nw2[...], gain, grad, pre, normal, inverse)
        stacked_grad = dot(nw1[...], pre_grad)
        part[:, here] = grad + stacked_grad[:rows]
        low = stacked_grad[rows:].astype(BF16)
        for h in range(per):
            tabs[1, z, (c * per + h) * rows : (c * per + h + 1) * rows, :] = low[
                :, h * LOW : (h + 1) * LOW
            ]
        for part_c in range(c * chunks // node_parts, (c + 1) * chunks // node_parts):
            send_own(1, part_c)
        node_first = node_first + dot_nt(stacked, pre_grad)
        node_second = node_second + dot_nt(hidden, outer_grad)
        for k, v in enumerate((pre_grad.astype(F32), outer_grad.astype(F32), grad * normal, grad)):
            node_sums[k] = node_sums[k] + lane_sums(v)

    new_copy = pltpu.make_async_copy(new_hold, new_nodes, out_sem.at[0])
    new_copy.start()

    def backward_steps(k):
        backward_step(k)

        @pl.when(k == 0)
        def _():
            send_back(0, 1, ring)

        @pl.when(k == 1)
        def _():
            relay(1, 0)
            for other in range(1, PLANES):
                ids_arrival(1, order[other]).wait_recv()
            end_wait(1, 1)

        @pl.when(k == 2)
        def _():
            relay(1, 1)
            end_wait(1, 2)

        @pl.when((k == 1) | (k == 2))
        def _():
            emit_at(BACK_PLAN, "table", k, PLANES, send_back)
            gather_step(1, k, recv_c)
            emit_at(BACK_PLAN, "gather", k, PLANES, send_back)

    loop(0, PLANES, backward_steps)

    grads[: 2 * rows, rows:] = node_first
    grads[2 * rows : 3 * rows, rows:] = node_second
    grads[3 * rows :, :8] = jnp.concatenate(
        [sums[k].sum(axis=1, keepdims=True) for k in range(4)]
        + [v.sum(axis=1, keepdims=True) for v in node_sums],
        axis=1,
    )
    reducers = min(group, grads.shape[0] // 8)
    height = grads.shape[0] // reducers

    def piece(g):
        return pl.ds(pl.multiple_of(g * height, 8), height)

    def piece_copy(g, device):
        return remote(
            grads.at[piece(g)], pieces.at[mine_of_group],
            piece_send.at[g], piece_recv.at[mine_of_group], device,
        )

    def piece_arrival(g):
        return remote(
            grads.at[piece(0)], pieces.at[g], piece_send.at[0], piece_recv.at[g], (e, rep)
        )

    def plane_sum_copy(k):
        plane = lax.rem(z + k, PLANES)
        return remote(
            plane_sums.at[z], plane_sums.at[z], plane_send.at[plane], plane_recv.at[z],
            at(plane, r),
        )

    def plane_sum_arrival(k):
        plane = lax.rem(z + k, PLANES)
        here = plane_sums.at[plane]
        return remote(here, here, plane_send.at[plane], plane_recv.at[plane], (e, rep))

    def sum_copy(g, device):
        return remote(
            summed.at[piece(mine_of_group)], summed.at[piece(mine_of_group)],
            sum_send.at[g], sum_recv.at[mine_of_group], device,
        )

    def sum_arrival(g):
        return remote(
            summed.at[piece(g)], summed.at[piece(g)], sum_send.at[0], sum_recv.at[g], (e, rep)
        )

    def to_reducers(body):
        def one(g, device):
            if reducers == group:
                body(g, device)
            else:
                @pl.when(g < reducers)
                def _():
                    body(g, device)

        others(one)

    def as_reducer(body):
        if reducers == group:
            body()
        else:
            pl.when(mine_of_group < reducers)(body)

    to_reducers(lambda g, device: piece_copy(g, device).start())

    total[...] = jnp.zeros_like(total)

    def by_receiver(h):
        emit_at(BACK_PLAN, "sums", h, owners // 2, send_back)
        total[...] += scatter_columns(
            side_by_side([send_d[2 * h], send_d[2 * h + 1]]),
            side_by_side([ids_of(receivers, 2 * h), ids_of(receivers, 2 * h + 1)]), count,
        )

    loop(0, owners // 2, by_receiver)

    def node_total(w_rows):
        sums_here = side_by_side([total[h * rows : (h + 1) * rows, :] for h in range(high_count)])
        part[...] += split_dot(ew1[w_rows, :], sums_here)

    node_total(slice(2 * rows, 3 * rows))
    total[...] = jnp.zeros_like(total)

    @as_reducer
    def _():
        pieces[mine_of_group] = grads[piece(mine_of_group), :]
        others(lambda g, device: piece_arrival(g).wait_recv())
        running = pieces[0]
        for g in range(1, group):
            running = running + pieces[g]
        plane_sums[z] = running
        for k in range(1, PLANES):
            plane_sum_copy(k).start()

    end_wait(1, 3)
    emit_at(BACK_PLAN, "table", PLANES - 1, PLANES, send_back)
    gather_step(1, PLANES - 1, recv_c)
    emit_at(BACK_PLAN, "gather", PLANES - 1, PLANES, send_back)

    def grad_copy(j):
        return pltpu.make_async_copy(recv_c.at[j], edge_grad.at[:, lanes(j)], grad_sem.at[j])

    def finish_edges(j, pre_grad):
        grad = recv_c[j].astype(F32) * (place < counts[j]).astype(F32)
        recv_c[j] = (grad + dot(ew1[:rows, :], pre_grad)).astype(BF16)
        grad_copy(j).start()

    recv_d[e] = send_d[e]

    def finish(turn, plane, ts, remotes):
        emit_at(BACK_PLAN, "finish", turn, turns, send_back)
        js = [plane * ring + lax.rem(r + ring - t, ring) for t in ts]
        for t, j, there in zip(ts, js, remotes):
            @pl.when(t > 0)
            def _():
                plane_arrival(1, j, recv_c).wait_recv()

            @pl.when(there)
            def _():
                back_arrival(j).wait_recv()

            finish_edges(j, recv_d[j])
        total[...] += scatter_columns(
            side_by_side([recv_d[j] for j in js]), side_by_side([ids_of(senders, j) for j in js]), count
        )

    def finish_step(k):
        @pl.when(k == 2)
        def _():
            @as_reducer
            def _():
                for other in range(1, PLANES):
                    plane_sum_arrival(other).wait_recv()
                running = plane_sums[0]
                for plane in range(1, PLANES):
                    running = running + plane_sums[plane]
                summed[piece(mine_of_group), :] = running
                others(lambda g, device: sum_copy(g, device).start())

        pairs_of(k, finish)

    loop(0, PLANES, finish_step)
    node_total(slice(rows, 2 * rows))
    node_hold[...] = part[...].astype(BF16)
    node_copy = pltpu.make_async_copy(node_hold, node_grad, out_sem.at[1])
    node_copy.start()

    drain_tables(0)
    drain_tables(1)
    drain_planes(1, recv_c)
    for k in range(1, PLANES):
        ids_copy(0, senders, k).wait_send()
        ids_copy(1, receivers, k).wait_send()
    peers(lambda j: count_copy(j).wait_send())
    peers(lambda j: edges_copy(j).wait_send())
    peers(lambda j: back_copy(j).wait_send())
    to_reducers(lambda g, device: piece_copy(g, device).wait_send())

    @as_reducer
    def _():
        for k in range(1, PLANES):
            plane_sum_copy(k).wait_send()
        others(lambda g, device: sum_copy(g, device).wait_send())

    to_reducers(lambda g, device: sum_arrival(g).wait_recv())
    loop(0, owners, lambda j: grad_copy(j).wait())
    new_copy.wait()
    node_copy.wait()


def layer(counts, nodes, edges, target, senders, receivers, levels, land, masks, *weights):
    rows, count = nodes.shape
    owners = lax.axis_size("edge")
    slots = edges.shape[1]
    cap = slots // owners
    reps = lax.axis_size("rep")
    group = owners // PLANES * reps
    chunks = math.gcd(count // LOW, TABLE_PARTS)
    grad_shape = (4 * rows, 2 * rows)
    reducers = min(group, grad_shape[0] // 8)
    blocks = (owners, rows, cap)
    dma = pltpu.SemaphoreType.DMA
    vmem = pl.BlockSpec(memory_space=pltpu.VMEM)
    stay = pl.BlockSpec(memory_space=pl.ANY)
    return pl.pallas_call(
        functools.partial(layer_kernel, masks.shape[0], reps),
        in_specs=[pl.BlockSpec(memory_space=pltpu.SMEM), vmem, stay, stay]
        + [vmem] * (5 + len(weights)),
        out_specs=[stay, stay, stay, vmem],
        out_shape=[
            jax.ShapeDtypeStruct((rows, count), BF16),
            jax.ShapeDtypeStruct((rows, count), BF16),
            jax.ShapeDtypeStruct((rows, slots), BF16),
            jax.ShapeDtypeStruct(grad_shape, F32),
        ],
        scratch_shapes=[
            pltpu.VMEM((rows, slots), BF16),
            pltpu.VMEM((rows, count), BF16),
            pltpu.VMEM((rows, count), BF16),
            pltpu.VMEM((rows, count), BF16),
            dma((2,)),
            dma((2,)),
            dma((owners,)),
            pltpu.VMEM((2, PLANES, rows * (count // LOW), LOW), BF16),
            pltpu.VMEM(blocks, BF16),
            pltpu.VMEM(blocks, BF16),
            pltpu.VMEM(blocks, BF16),
            pltpu.VMEM(blocks, BF16),
            pltpu.VMEM((2,) + senders.shape, jnp.int32),
            pltpu.VMEM((owners, 1, 128), jnp.int32),
            pltpu.VMEM((owners, 1, 128), jnp.int32),
            pltpu.VMEM(blocks, F32),
            pltpu.VMEM(blocks, F32),
            pltpu.VMEM((owners, 1, cap), F32),
            pltpu.VMEM(blocks, BF16),
            pltpu.VMEM(blocks, BF16),
            pltpu.VMEM(blocks, BF16),
            pltpu.VMEM((rows * (count // LOW), LOW), F32),
            pltpu.VMEM((rows, count), F32),
            pltpu.VMEM(grad_shape, F32),
            pltpu.VMEM((4, rows, 128), F32),
            pltpu.VMEM((group, grad_shape[0] // reducers, grad_shape[1]), F32),
            pltpu.VMEM((3 * rows, rows), BF16),
            pltpu.VMEM((rows, rows), BF16),
            pltpu.VMEM((2 * rows, rows), BF16),
            pltpu.VMEM((rows, rows), BF16),
            pltpu.VMEM((rows, 16 * -(-(8 + masks.shape[0]) // 16)), F32),
            dma((2, 5, chunks)),
            dma((2, PLANES, chunks)),
            dma((2, PLANES)),
            dma((2, PLANES)),
            dma((2, owners)),
            dma((2, owners)),
            dma((2, owners)),
            dma((2, owners)),
            dma((owners,)),
            dma((owners,)),
            pltpu.VMEM((PLANES, grad_shape[0] // reducers, grad_shape[1]), F32),
            dma((group,)),
            dma((group,)),
            dma((PLANES,)),
            dma((PLANES,)),
            dma((group,)),
            dma((group,)),
        ],
        compiler_params=pltpu.CompilerParams(
            vmem_limit_bytes=VMEM_LIMIT, collective_id=0, has_side_effects=True
        ),
        cost_estimate=pl.CostEstimate(
            flops=64 * 2**30, bytes_accessed=16 * 2**20, transcendentals=4 * 2**20
        ),
        name="layer",
    )(counts, nodes, edges, target, senders, receivers, levels, land, masks, *weights)


def hand_out_kernel(edge_in, new_in, node_in, packed, edge_grad, new_nodes, node_grad, *outs):
    edge_grad[...] = edge_in[...]
    new_nodes[...] = new_in[...]
    node_grad[...] = node_in[...]
    rows = packed.shape[1] // 2
    lines = packed[3 * rows :, :].T
    edge_first, edge_b1, edge_second, edge_b2, edge_g, edge_h = outs[:6]
    node_first, node_b1, node_second, node_b2, node_g, node_h = outs[6:]
    edge_first[...] = packed[: 3 * rows, :].T[:rows, :]
    edge_second[...] = packed[3 * rows :, rows:]
    node_first[...] = packed[: 2 * rows, :].T[rows:, :]
    node_second[...] = packed[2 * rows : 3 * rows, rows:]
    for k, out in enumerate((edge_b1, edge_b2, edge_g, edge_h, node_b1, node_b2, node_g, node_h)):
        out[...] = lines[k, :rows]


def hand_out(new_nodes, node_grad, edge_grad, packed):
    rows = packed.shape[1] // 2
    vmem = pl.BlockSpec(memory_space=pltpu.VMEM)
    shapes = [
        (rows, 3 * rows), (rows,), (rows, rows), (rows,), (rows,), (rows,),
        (rows, 2 * rows), (rows,), (rows, rows), (rows,), (rows,), (rows,),
    ]
    large = (edge_grad, new_nodes, node_grad)
    edge_grad, new_nodes, node_grad, *small = pl.pallas_call(
        hand_out_kernel,
        in_specs=[vmem] * 4,
        out_specs=[vmem] * (3 + len(shapes)),
        out_shape=[jax.ShapeDtypeStruct(a.shape, a.dtype) for a in large]
        + [jax.ShapeDtypeStruct(s, F32) for s in shapes],
        compiler_params=pltpu.CompilerParams(vmem_limit_bytes=VMEM_LIMIT),
        name="hand_out",
    )(*large, packed)
    small[0], small[6] = small[0].T, small[6].T
    return (new_nodes, node_grad, edge_grad, *small)


def per_device(
    nodes, edges, target, senders, receivers, counts, levels, land, channel_mask,
    edge_in, edge_in_bias, edge_out, edge_out_bias, edge_gain, edge_shift,
    node_in, node_in_bias, node_out, node_out_bias, node_gain, node_shift,
):
    count = nodes.shape[1]
    return hand_out(
        *layer(
            counts, nodes, edges, target,
            senders.reshape(-1, 128), receivers.reshape(-1, 128),
            levels.reshape(1, count), land.reshape(1, count), channel_mask,
            edge_in.T, edge_out, node_in.T, node_out,
            edge_in_bias, edge_out_bias, edge_gain, edge_shift,
            node_in_bias, node_out_bias, node_gain, node_shift,
        )
    )


def solution(mesh):
    over = ("edge", "rep")
    wide, line, same = P(None, over), P(over), P()
    return jax.shard_map(
        per_device,
        mesh=mesh,
        in_specs=(wide, wide, wide, line, line, line, line, line) + (same,) * 13,
        out_specs=(wide, wide, wide) + (same,) * 12,
        check_vma=False,
    )
```

```python
import functools
import math

import jax
import jax.numpy as jnp
from jax import lax
from jax.experimental import pallas as pl
from jax.experimental.pallas import tpu as pltpu
from jax.sharding import PartitionSpec as P

NORM_EPS = 1e-05
F32 = jnp.float32
BF16 = jnp.bfloat16
LOW = 256
VMEM_LIMIT = 60 * 2**20
PLANES = 4
TABLE_PARTS = 4
NODE_PARTS = 4
EDGE_PLAN = {
    ('edges', 0): (((2, 0), (2, 1), (2, 2), (2, 3)), ()),
    ('edges', 2): ((), ((3, 1),)),
    ('edges', 3): (((3, 2),), ()),
    ('edges', 4): ((), ((3, 3),)),
    ('edges', 5): (((3, 3),), ((3, 2),)),
    ('gather', 3): ((), ((3, 0),)),
    ('table', 1): (((1, 0), (1, 1), (1, 2), (1, 3)), ((1, 0), (1, 1), (1, 2), (1, 3))),
    ('table', 2): ((), ((2, 0), (2, 1), (2, 2), (2, 3))),
    ('table', 3): (((3, 0), (3, 1)), ()),
}
BACK_PLAN = {
    ('sums', 6): (((3, 3),), ()),
    ('table', 1): (((1, 0), (1, 1), (1, 2), (1, 3)), ((1, 0), (1, 1), (1, 2), (1, 3))),
    ('table', 2): (((2, 0), (2, 1), (2, 2), (2, 3)), ((2, 0), (2, 1), (2, 2), (2, 3))),
    ('table', 3): (((3, 0), (3, 1), (3, 2)), ((3, 0), (3, 1), (3, 2), (3, 3))),
}
MESH = pl.DeviceIdType.MESH

EB1, EB2, EG, EH, NB1, NB2, NG, NH, CM = 0, 1, 2, 3, 4, 5, 6, 7, 8


def dot(a, b):
    return jnp.dot(a, b, preferred_element_type=F32)


def dot_tn(a, b):
    return lax.dot_general(a, b, (((0,), (0,)), ((), ())), preferred_element_type=F32)


def dot_nt(a, b):
    return lax.dot_general(a, b, (((1,), (1,)), ((), ())), preferred_element_type=F32)


def one_hot_low(ids):
    low = ids & (LOW - 1)
    rows = lax.broadcasted_iota(jnp.int32, (LOW, ids.shape[1]), 0)
    return (rows == low).astype(F32).astype(BF16)


def high_of(ids, rows):
    high = ids >> (LOW.bit_length() - 1)
    return jnp.broadcast_to(high.astype(F32).astype(BF16), (rows, ids.shape[1]))


def stack_table(table_ref, value):
    rows = value.shape[0]
    for h in range(value.shape[1] // LOW):
        table_ref[h * rows : (h + 1) * rows, :] = value[:, h * LOW : (h + 1) * LOW]


def gather_columns(table, ids, rows):
    picked = dot(table, one_hot_low(ids)).astype(BF16)
    high = high_of(ids, rows)
    out = picked[:rows]
    for h in range(1, table.shape[0] // rows):
        out = jnp.where(high == BF16(h), picked[h * rows : (h + 1) * rows], out)
    return out


def scatter_columns(values, ids, count):
    rows = values.shape[0]
    high = high_of(ids, rows)
    zero = jnp.zeros_like(values)
    spread = jnp.concatenate(
        [jnp.where(high == BF16(h), values, zero) for h in range(count // LOW)], axis=0
    )
    return dot_nt(spread, one_hot_low(ids))


def column(cols, index):
    return cols[:, index : index + 1]


def mean_rows(v):
    return jnp.mean(v, axis=0, keepdims=True)


def lane_sums(v):
    out = v[:, :128]
    for k in range(1, v.shape[1] // 128):
        out = out + v[:, k * 128 : (k + 1) * 128]
    return out


def branch_forward(w1t, w2t, b1, b2, stacked):
    pre = dot(w1t, stacked) + b1
    hidden = (pre * (1.0 / (1.0 + jnp.exp(-pre)))).astype(BF16)
    outer = dot(w2t, hidden) + b2
    shifted = outer - mean_rows(outer)
    inverse = lax.rsqrt(mean_rows(shifted * shifted) + NORM_EPS)
    return pre, shifted * inverse, inverse


def branch_backward(w2, gain, grad, pre, normal, inverse):
    q = grad * gain
    outer_grad = (
        inverse * (q - mean_rows(q) - normal * mean_rows(q * normal))
    ).astype(BF16)
    s = 1.0 / (1.0 + jnp.exp(-pre))
    pre_grad = (dot(w2, outer_grad) * (s * (1.0 + pre * (1.0 - s)))).astype(BF16)
    return outer_grad, pre_grad, (pre * s).astype(BF16)


def split_dot(low, wide):
    top = wide.astype(BF16)
    rest = (wide - top.astype(F32)).astype(BF16)
    return dot(low, top) + dot(low, rest)


def layer_kernel(
    levels_count, reps,
    counts, nodes, edges_in, target_in, senders, receivers, levels, land, masks, ew1t, ew2, nw1t,
    nw2,
    eb1, eb2, eg, eh, nb1, nb2, ng, nh,
    new_nodes, node_grad, edge_grad, summed,
    edges, target, new_hold, node_hold, in_sem, out_sem, grad_sem, tabs, send_a, recv_s, recv_e, mine, ids_tab, count_send, count_recv, pre_s, normal_s,
    inverse_s, recv_c, send_d, recv_d, total, part, grads, sums, pieces, ew1, ew2t, nw1, nw2t, cols,
    tab_send, tab_recv, ids_send, ids_recv, a_send, a_recv, b_send, b_recv, count_out, count_in,
    plane_sums, piece_send, piece_recv, plane_send, plane_recv, sum_send, sum_recv,
):
    rows, count = nodes.shape
    owners = count_send.shape[0]
    cap = senders.shape[0] * senders.shape[1] // owners
    lines_of = cap // senders.shape[1]
    ring = owners // PLANES
    high_count = count // LOW
    chunks = tab_recv.shape[2]
    chunk = tabs.shape[2] // chunks
    e, rep = lax.axis_index("edge"), lax.axis_index("rep")
    z, r = e // ring, e % ring
    upper = z // 2

    def plane_at(k):
        low = z + upper * (3 - 2 * z)
        turned = lax.rem(k + 1, 3) * (1 - k // 3) + 3 * (k // 3)
        place = k * (1 - low) + turned * low
        return place + upper * (3 - 2 * place)

    order = tuple(plane_at(k) for k in range(PLANES))
    middle = lax.rem(z, 3) != 0
    toward = 3 - 2 * z

    def at(plane, place):
        return (plane * ring + place, rep)

    def remote(src, dst, send, recv, device):
        return pltpu.make_async_remote_copy(
            src, dst, send, recv, device_id=device, device_id_type=MESH
        )

    def loop(low, high, body):
        def step(i, carry):
            body(i)
            return carry

        lax.fori_loop(low, high, step, 0)

    group, mine_of_group = ring * reps, r * reps + rep

    def group_device(g):
        return (z * ring + g // reps, lax.rem(g, reps))

    def others(body):
        def one(t):
            g = lax.rem(mine_of_group + t, group)
            body(g, group_device(g))

        loop(1, group, one)

    load_edges = pltpu.make_async_copy(edges_in, edges, in_sem.at[0])
    load_target = pltpu.make_async_copy(target_in, target, in_sem.at[1])
    load_edges.start()
    load_target.start()

    barrier = pltpu.get_barrier_semaphore()

    def greet(device):
        pl.semaphore_signal(barrier, inc=1, device_id=device, device_id_type=MESH)

    loop(1, owners, lambda t: greet((lax.rem(e + t, owners), rep)))

    def greet_other_cores(t):
        loop(0, ring, lambda place: greet((z * ring + place, lax.rem(rep + t, reps))))

    loop(1, reps, greet_other_cores)
    stack_table(tabs.at[0, z], nodes[...])
    pl.semaphore_wait(barrier, owners - 1 + ring * (reps - 1))

    def part_of(phase, plane, c):
        return tabs.at[phase, plane, pl.ds(c * chunk, chunk)]

    def table_copy(phase, plane, c, lane, to):
        return remote(
            part_of(phase, plane, c), part_of(phase, plane, c),
            tab_send.at[phase, lane, c], tab_recv.at[phase, plane, c], at(to, r),
        )

    def await_table(phase, plane, c):
        table_copy(phase, plane, c, 0, z).wait_recv()

    def send_own(phase, c):
        @pl.when(z < PLANES - 1)
        def _():
            table_copy(phase, z, c, 0, z + 1).start()

        @pl.when(z > 0)
        def _():
            table_copy(phase, z, c, 1, z - 1).start()

    def relay(phase, slot, low=0, high=None):
        @pl.when(middle)
        def _():
            for c in range(low, chunks if high is None else high):
                if slot == 0:
                    await_table(phase, z - toward, c)
                    table_copy(phase, z - toward, c, 2, z + toward).start()
                    await_table(phase, z + toward, c)
                    table_copy(phase, z + toward, c, 3, z - toward).start()
                else:
                    await_table(phase, z + 2 * toward, c)
                    table_copy(phase, z + 2 * toward, c, 4, z - toward).start()

    def end_wait(phase, k):
        @pl.when(jnp.logical_not(middle))
        def _():
            for c in range(chunks):
                await_table(phase, order[k], c)

    def drain_tables(phase):
        for c in range(chunks):
            @pl.when(z < PLANES - 1)
            def _():
                table_copy(phase, z, c, 0, z + 1).wait_send()

            @pl.when(z > 0)
            def _():
                table_copy(phase, z, c, 1, z - 1).wait_send()

            @pl.when(middle)
            def _():
                table_copy(phase, z - toward, c, 2, z + toward).wait_send()
                table_copy(phase, z + toward, c, 3, z - toward).wait_send()
                table_copy(phase, z + 2 * toward, c, 4, z - toward).wait_send()

    def ids_rows(plane):
        size = ring * lines_of
        return pl.ds(pl.multiple_of(plane * size, size), size)

    def ids_of(ids, j):
        block = ids[pl.ds(pl.multiple_of(j * lines_of, lines_of), lines_of), :]
        return side_by_side([block[i : i + 1] for i in range(lines_of)])

    def ids_copy(phase, ids, k):
        plane = lax.rem(z + k, PLANES)
        return remote(
            ids.at[ids_rows(plane)], ids_tab.at[phase, ids_rows(z)],
            ids_send.at[phase, plane], ids_recv.at[phase, z], at(plane, r),
        )

    def ids_arrival(phase, plane):
        rows_of = ids_tab.at[phase, ids_rows(plane)]
        return remote(
            rows_of, rows_of, ids_send.at[phase, plane], ids_recv.at[phase, plane], at(plane, r)
        )

    def plane_copy(phase, plane, to, into):
        return remote(
            send_a.at[plane * ring + to], into.at[plane * ring + r],
            a_send.at[phase, plane * ring + to], a_recv.at[phase, plane * ring + r], at(z, to),
        )

    def plane_arrival(phase, j, into):
        return remote(
            send_a.at[j], into.at[j], a_send.at[phase, j], a_recv.at[phase, j], at(z, r)
        )

    def hand_over(phase, plane, to, t, got, into):
        @pl.when(t < ring)
        def _():
            send_a[plane * ring + to] = got
            plane_copy(phase, plane, to, into).start()

        @pl.when(t == ring)
        def _():
            into[plane * ring + r] = got

    def gather_step(phase, k, into):
        plane = plane_at(k)

        def two(ts):
            tos = [lax.rem(r + t + 1, ring) for t in ts]
            got = gather_columns(
                tabs[phase, plane],
                side_by_side([ids_of(ids_tab.at[phase], plane * ring + to) for to in tos]), rows,
            )
            for i, (t, to) in enumerate(zip(ts, tos)):
                hand_over(phase, plane, to, t + 1, got[:, i * cap : (i + 1) * cap], into)

        in_pairs(two)

    def drain_planes(phase, into):
        for plane in range(PLANES):
            loop(1, ring, lambda t: plane_copy(phase, plane, lax.rem(r + t, ring), into).wait_send())

    def lanes(j):
        return pl.ds(pl.multiple_of(j * cap, cap), cap)

    def edges_copy(j):
        return remote(
            edges.at[:, lanes(j)], recv_e.at[e], b_send.at[0, j], b_recv.at[0, e], (j, rep)
        )

    def edges_arrival(a):
        return remote(
            edges.at[:, lanes(a)], recv_e.at[a], b_send.at[0, a], b_recv.at[0, a], (e, rep)
        )

    def count_copy(j):
        return remote(
            count_send.at[j], count_recv.at[e], count_out.at[j], count_in.at[e], (j, rep)
        )

    def count_arrival(a):
        return remote(
            count_send.at[a], count_recv.at[a], count_out.at[a], count_in.at[a], (e, rep)
        )

    def back_copy(a):
        return remote(
            send_d.at[a], recv_d.at[e], b_send.at[1, a], b_recv.at[1, e], (a, rep)
        )

    def back_arrival(j):
        return remote(
            send_d.at[j], recv_d.at[j], b_send.at[1, j], b_recv.at[1, j], (e, rep)
        )

    def peers(body):
        loop(1, owners, lambda t: body(lax.rem(e + t, owners)))

    def in_pairs(body):
        loop(0, ring // 2, lambda h: body((2 * h, 2 * h + 1)))

    half = ring // 2

    def turns_of(low, high, body):
        def one(turn):
            k, h = turn // half, lax.rem(turn, half)
            ts = (2 * h, 2 * h + 1)
            body(turn, plane_at(k), ts, [k + t > 0 for t in ts])

        loop(low, high, one)

    def side_by_side(blocks):
        return jnp.concatenate(blocks, axis=1)

    def send_edges(k, low, high):
        loop(low, high, lambda t: edges_copy(order[k] * ring + lax.rem(r + t, ring)).start())

    place = lax.broadcasted_iota(jnp.int32, (1, cap), 1)

    def live_here(a):
        line = count_recv[a]
        wide = jnp.concatenate([line] * (cap // line.shape[1]), axis=1)
        return (place < wide).astype(F32)

    def edge_forward(a):
        own = recv_e[a]
        pre, normal, inverse = branch_forward(
            ew1t[...], ew2t[...], column(cols, EB1), column(cols, EB2),
            jnp.concatenate([own, recv_s[a], mine[a]], axis=0),
        )
        pre_s[a] = pre
        normal_s[a] = normal
        inverse_s[a] = inverse
        updated = own.astype(F32) + (normal * column(cols, EG) + column(cols, EH))
        return (updated * live_here(a)).astype(BF16)

    turns = PLANES * (ring // 2)

    def forward_pair(turn, plane, ts, remotes):
        emit_at(EDGE_PLAN, "edges", turn, turns, send_edges)
        froms = [plane * ring + lax.rem(r + ring - t, ring) for t in ts]
        for t, a, there in zip(ts, froms, remotes):
            @pl.when(t > 0)
            def _():
                plane_arrival(0, a, recv_s).wait_recv()

            @pl.when(there)
            def _():
                count_arrival(a).wait_recv()
                edges_arrival(a).wait_recv()

        total[...] += scatter_columns(
            side_by_side([edge_forward(a) for a in froms]),
            side_by_side([ids_of(receivers, a) for a in froms]), count,
        )

    def edge_backward(a, got):
        grad = got.astype(F32) * live_here(a)
        normal = normal_s[a]
        outer_grad, pre_grad, hidden = branch_backward(
            ew2[...], column(cols, EG), grad, pre_s[a], normal, inverse_s[a]
        )
        grads[...] += dot_nt(
            jnp.concatenate([recv_e[a], recv_s[a], mine[a], hidden], axis=0),
            jnp.concatenate([pre_grad, outer_grad], axis=0),
        )
        for k, v in enumerate((pre_grad.astype(F32), outer_grad.astype(F32), grad * normal, grad)):
            sums[k] += lane_sums(v)
        return pre_grad

    def backward_step(k):
        plane = plane_at(k)

        def two(ts):
            tos = [lax.rem(r + t + 1, ring) for t in ts]
            froms = [plane * ring + to for to in tos]
            both = gather_columns(
                tabs[1, z], side_by_side([ids_of(receivers, a) for a in froms]), rows
            )
            for i, (t, to, a) in enumerate(zip(ts, tos, froms)):
                got = both[:, i * cap : (i + 1) * cap]

                @pl.when(k == 0)
                def _():
                    hand_over(1, z, to, t + 1, got, recv_c)

                send_d[a] = edge_backward(a, got)

        in_pairs(two)

    def send_back(k, low, high):
        loop(low, high, lambda t: back_copy(order[k] * ring + lax.rem(r + t, ring)).start())

    def emit(plan, slot, send):
        for body_at, parts in zip((at_ends, at_middle), plan.get(slot, ((), ()))):
            if parts:
                @body_at
                def _():
                    for k, q in parts:
                        send(k, q * ring // 4, (q + 1) * ring // 4)

    def at_ends(body):
        pl.when(jnp.logical_not(middle))(body)

    def at_middle(body):
        pl.when(middle)(body)

    def emit_at(plan, slot, turn, turns, send):
        for i in range(turns):
            if (slot, i) in plan:
                @pl.when(turn == i)
                def _():
                    emit(plan, (slot, i), send)

    for c in range(chunks):
        send_own(0, c)
    for k in range(1, PLANES):
        ids_copy(0, senders, k).start()
    load_edges.wait()
    send_edges(0, 1, ring)
    for j in range(owners):
        count_send[j] = jnp.full(count_send.shape[1:], counts[j], jnp.int32)
    peers(lambda j: count_copy(j).start())
    for k in range(1, PLANES):
        ids_copy(1, receivers, k).start()
    ids_tab[0, ids_rows(z)] = senders[ids_rows(z)]
    count_recv[e] = count_send[e]
    recv_e[e] = edges[:, lanes(e)]
    total[...] = jnp.zeros_like(total)
    grads[...] = jnp.zeros_like(grads)
    sums[...] = jnp.zeros_like(sums)

    def eye(n):
        return (
            lax.broadcasted_iota(jnp.int32, (n, n), 0) == lax.broadcasted_iota(jnp.int32, (n, n), 1)
        ).astype(F32).astype(BF16)

    unit = eye(rows)
    ew1[...] = dot_tn(ew1t[...], unit).astype(BF16)
    nw1[...] = dot_tn(nw1t[...], unit).astype(BF16)
    ew2t[...] = dot_tn(ew2[...], unit).astype(BF16)
    nw2t[...] = dot_tn(nw2[...], unit).astype(BF16)
    lines = [v[...].astype(F32)[None, :] for v in (eb1, eb2, eg, eh, nb1, nb2, ng, nh)]
    lines.append(masks[...].astype(F32))
    lines.append(jnp.zeros((-(8 + levels_count) % 16, rows), F32))
    cols[...] = dot_nt(unit, jnp.concatenate(lines, axis=0).astype(BF16))

    def forward_gathers(k):
        @pl.when(k == 1)
        def _():
            relay(0, 0)
            for other in range(1, PLANES):
                ids_arrival(0, order[other]).wait_recv()
            end_wait(0, 1)

        @pl.when(k == 2)
        def _():
            relay(0, 1)
            end_wait(0, 2)

        @pl.when(k == 3)
        def _():
            end_wait(0, 3)

        emit_at(EDGE_PLAN, "table", k, PLANES, send_edges)
        gather_step(0, k, recv_s)
        emit_at(EDGE_PLAN, "gather", k, PLANES, send_edges)

        def mine_pair(turn, plane, ts, _):
            js = [plane * ring + t for t in ts]
            both = gather_columns(tabs[0, z], side_by_side([ids_of(receivers, j) for j in js]), rows)
            for i, j in enumerate(js):
                mine[j] = both[:, i * cap : (i + 1) * cap]

        @pl.when(k < 3)
        def _():
            turns_of((k + k // 2) * half, (k + 1 + (k + 1) // 2) * half, mine_pair)

    early = half * (2 - z * (3 - z) // 2)

    def forward_steps(k):
        last = k // PLANES
        turns_of(last * early, k // 3 * early + last * (turns - early), forward_pair)

        @pl.when(k < PLANES)
        def _():
            forward_gathers(k)

    loop(0, PLANES + 1, forward_steps)
    drain_planes(0, recv_s)

    load_target.wait()

    node_parts = math.gcd(high_count, NODE_PARTS)
    per = high_count // node_parts
    wide = per * LOW
    node_first = jnp.zeros((2 * rows, rows), F32)
    node_second = jnp.zeros((rows, rows), F32)
    node_sums = [jnp.zeros((rows, 128), F32)] * 4
    for c in range(node_parts):
        here = slice(c * wide, (c + 1) * wide)
        aggregate = jnp.concatenate(
            [total[h * rows : (h + 1) * rows, :] for h in range(c * per, (c + 1) * per)], axis=1
        ).astype(BF16)
        own = nodes[:, here]
        stacked = jnp.concatenate([own, aggregate], axis=0)
        pre, normal, inverse = branch_forward(
            nw1t[...], nw2t[...], column(cols, NB1), column(cols, NB2), stacked
        )
        gain = column(cols, NG)
        state = own.astype(F32) + (normal * gain + column(cols, NH))
        new_hold[:, here] = state.astype(BF16)
        weight = jnp.zeros((rows, wide), F32)
        for l in range(levels_count):
            weight = jnp.where(levels[:, here] == l, column(cols, CM + l), weight)
        weight = weight * land[:, here].astype(F32)
        grad = weight * (state - target[:, here].astype(F32))
        outer_grad, pre_grad, hidden = branch_backward(nw2[...], gain, grad, pre, normal, inverse)
        stacked_grad = dot(nw1[...], pre_grad)
        part[:, here] = grad + stacked_grad[:rows]
        low = stacked_grad[rows:].astype(BF16)
        for h in range(per):
            tabs[1, z, (c * per + h) * rows : (c * per + h + 1) * rows, :] = low[
                :, h * LOW : (h + 1) * LOW
            ]
        for part_c in range(c * chunks // node_parts, (c + 1) * chunks // node_parts):
            send_own(1, part_c)
        node_first = node_first + dot_nt(stacked, pre_grad)
        node_second = node_second + dot_nt(hidden, outer_grad)
        for k, v in enumerate((pre_grad.astype(F32), outer_grad.astype(F32), grad * normal, grad)):
            node_sums[k] = node_sums[k] + lane_sums(v)

    new_copy = pltpu.make_async_copy(new_hold, new_nodes, out_sem.at[0])
    new_copy.start()

    def backward_steps(k):
        backward_step(k)

        @pl.when(k == 0)
        def _():
            send_back(0, 1, ring)

        @pl.when(k == 1)
        def _():
            relay(1, 0)
            for other in range(1, PLANES):
                ids_arrival(1, order[other]).wait_recv()
            end_wait(1, 1)

        @pl.when(k == 2)
        def _():
            relay(1, 1)
            end_wait(1, 2)

        @pl.when((k == 1) | (k == 2))
        def _():
            emit_at(BACK_PLAN, "table", k, PLANES, send_back)
            gather_step(1, k, recv_c)
            emit_at(BACK_PLAN, "gather", k, PLANES, send_back)

    loop(0, PLANES, backward_steps)

    grads[: 2 * rows, rows:] = node_first
    grads[2 * rows : 3 * rows, rows:] = node_second
    grads[3 * rows :, :8] = jnp.concatenate(
        [sums[k].sum(axis=1, keepdims=True) for k in range(4)]
        + [v.sum(axis=1, keepdims=True) for v in node_sums],
        axis=1,
    )
    reducers = min(group, grads.shape[0] // 8)
    height = grads.shape[0] // reducers

    def piece(g):
        return pl.ds(pl.multiple_of(g * height, 8), height)

    def piece_copy(g, device):
        return remote(
            grads.at[piece(g)], pieces.at[mine_of_group],
            piece_send.at[g], piece_recv.at[mine_of_group], device,
        )

    def piece_arrival(g):
        return remote(
            grads.at[piece(0)], pieces.at[g], piece_send.at[0], piece_recv.at[g], (e, rep)
        )

    def plane_sum_copy(k):
        plane = lax.rem(z + k, PLANES)
        return remote(
            plane_sums.at[z], plane_sums.at[z], plane_send.at[plane], plane_recv.at[z],
            at(plane, r),
        )

    def plane_sum_arrival(k):
        plane = lax.rem(z + k, PLANES)
        here = plane_sums.at[plane]
        return remote(here, here, plane_send.at[plane], plane_recv.at[plane], (e, rep))

    def sum_copy(g, device):
        return remote(
            summed.at[piece(mine_of_group)], summed.at[piece(mine_of_group)],
            sum_send.at[g], sum_recv.at[mine_of_group], device,
        )

    def sum_arrival(g):
        return remote(
            summed.at[piece(g)], summed.at[piece(g)], sum_send.at[0], sum_recv.at[g], (e, rep)
        )

    def to_reducers(body):
        def one(g, device):
            if reducers == group:
                body(g, device)
            else:
                @pl.when(g < reducers)
                def _():
                    body(g, device)

        others(one)

    def as_reducer(body):
        if reducers == group:
            body()
        else:
            pl.when(mine_of_group < reducers)(body)

    to_reducers(lambda g, device: piece_copy(g, device).start())

    total[...] = jnp.zeros_like(total)

    def by_receiver(h):
        emit_at(BACK_PLAN, "sums", h, owners // 2, send_back)
        total[...] += scatter_columns(
            side_by_side([send_d[2 * h], send_d[2 * h + 1]]),
            side_by_side([ids_of(receivers, 2 * h), ids_of(receivers, 2 * h + 1)]), count,
        )

    loop(0, owners // 2, by_receiver)

    def node_total(w_rows):
        sums_here = side_by_side([total[h * rows : (h + 1) * rows, :] for h in range(high_count)])
        part[...] += split_dot(ew1[w_rows, :], sums_here)

    node_total(slice(2 * rows, 3 * rows))
    total[...] = jnp.zeros_like(total)

    @as_reducer
    def _():
        pieces[mine_of_group] = grads[piece(mine_of_group), :]
        others(lambda g, device: piece_arrival(g).wait_recv())
        running = pieces[0]
        for g in range(1, group):
            running = running + pieces[g]
        plane_sums[z] = running
        for k in range(1, PLANES):
            plane_sum_copy(k).start()

    end_wait(1, 3)
    emit_at(BACK_PLAN, "table", PLANES - 1, PLANES, send_back)
    gather_step(1, PLANES - 1, recv_c)
    emit_at(BACK_PLAN, "gather", PLANES - 1, PLANES, send_back)

    def grad_copy(j):
        return pltpu.make_async_copy(recv_c.at[j], edge_grad.at[:, lanes(j)], grad_sem.at[j])

    def finish_edges(j, pre_grad):
        grad = recv_c[j].astype(F32) * (place < counts[j]).astype(F32)
        recv_c[j] = (grad + dot(ew1[:rows, :], pre_grad)).astype(BF16)
        grad_copy(j).start()

    recv_d[e] = send_d[e]

    def finish(turn, plane, ts, remotes):
        emit_at(BACK_PLAN, "finish", turn, turns, send_back)
        js = [plane * ring + lax.rem(r + ring - t, ring) for t in ts]
        for t, j, there in zip(ts, js, remotes):
            @pl.when(t > 0)
            def _():
                plane_arrival(1, j, recv_c).wait_recv()

            @pl.when(there)
            def _():
                back_arrival(j).wait_recv()

            finish_edges(j, recv_d[j])
        total[...] += scatter_columns(
            side_by_side([recv_d[j] for j in js]), side_by_side([ids_of(senders, j) for j in js]), count
        )

    def finish_step(k):
        @pl.when(k == 2)
        def _():
            @as_reducer
            def _():
                for other in range(1, PLANES):
                    plane_sum_arrival(other).wait_recv()
                running = plane_sums[0]
                for plane in range(1, PLANES):
                    running = running + plane_sums[plane]
                summed[piece(mine_of_group), :] = running
                others(lambda g, device: sum_copy(g, device).start())

        turns_of(k * half, (k + 1) * half, finish)

    loop(0, PLANES, finish_step)
    node_total(slice(rows, 2 * rows))
    node_hold[...] = part[...].astype(BF16)
    node_copy = pltpu.make_async_copy(node_hold, node_grad, out_sem.at[1])
    node_copy.start()

    drain_tables(0)
    drain_tables(1)
    drain_planes(1, recv_c)
    for k in range(1, PLANES):
        ids_copy(0, senders, k).wait_send()
        ids_copy(1, receivers, k).wait_send()
    peers(lambda j: count_copy(j).wait_send())
    peers(lambda j: edges_copy(j).wait_send())
    peers(lambda j: back_copy(j).wait_send())
    to_reducers(lambda g, device: piece_copy(g, device).wait_send())

    @as_reducer
    def _():
        for k in range(1, PLANES):
            plane_sum_copy(k).wait_send()
        others(lambda g, device: sum_copy(g, device).wait_send())

    to_reducers(lambda g, device: sum_arrival(g).wait_recv())
    loop(0, owners, lambda j: grad_copy(j).wait())
    new_copy.wait()
    node_copy.wait()


def layer(counts, nodes, edges, target, senders, receivers, levels, land, masks, *weights):
    rows, count = nodes.shape
    owners = lax.axis_size("edge")
    slots = edges.shape[1]
    cap = slots // owners
    reps = lax.axis_size("rep")
    group = owners // PLANES * reps
    chunks = math.gcd(count // LOW, TABLE_PARTS)
    grad_shape = (4 * rows, 2 * rows)
    reducers = min(group, grad_shape[0] // 8)
    blocks = (owners, rows, cap)
    dma = pltpu.SemaphoreType.DMA
    vmem = pl.BlockSpec(memory_space=pltpu.VMEM)
    stay = pl.BlockSpec(memory_space=pl.ANY)
    return pl.pallas_call(
        functools.partial(layer_kernel, masks.shape[0], reps),
        in_specs=[pl.BlockSpec(memory_space=pltpu.SMEM), vmem, stay, stay]
        + [vmem] * (5 + len(weights)),
        out_specs=[stay, stay, stay, vmem],
        out_shape=[
            jax.ShapeDtypeStruct((rows, count), BF16),
            jax.ShapeDtypeStruct((rows, count), BF16),
            jax.ShapeDtypeStruct((rows, slots), BF16),
            jax.ShapeDtypeStruct(grad_shape, F32),
        ],
        scratch_shapes=[
            pltpu.VMEM((rows, slots), BF16),
            pltpu.VMEM((rows, count), BF16),
            pltpu.VMEM((rows, count), BF16),
            pltpu.VMEM((rows, count), BF16),
            dma((2,)),
            dma((2,)),
            dma((owners,)),
            pltpu.VMEM((2, PLANES, rows * (count // LOW), LOW), BF16),
            pltpu.VMEM(blocks, BF16),
            pltpu.VMEM(blocks, BF16),
            pltpu.VMEM(blocks, BF16),
            pltpu.VMEM(blocks, BF16),
            pltpu.VMEM((2,) + senders.shape, jnp.int32),
            pltpu.VMEM((owners, 1, 128), jnp.int32),
            pltpu.VMEM((owners, 1, 128), jnp.int32),
            pltpu.VMEM(blocks, F32),
            pltpu.VMEM(blocks, F32),
            pltpu.VMEM((owners, 1, cap), F32),
            pltpu.VMEM(blocks, BF16),
            pltpu.VMEM(blocks, BF16),
            pltpu.VMEM(blocks, BF16),
            pltpu.VMEM((rows * (count // LOW), LOW), F32),
            pltpu.VMEM((rows, count), F32),
            pltpu.VMEM(grad_shape, F32),
            pltpu.VMEM((4, rows, 128), F32),
            pltpu.VMEM((group, grad_shape[0] // reducers, grad_shape[1]), F32),
            pltpu.VMEM((3 * rows, rows), BF16),
            pltpu.VMEM((rows, rows), BF16),
            pltpu.VMEM((2 * rows, rows), BF16),
            pltpu.VMEM((rows, rows), BF16),
            pltpu.VMEM((rows, 16 * -(-(8 + masks.shape[0]) // 16)), F32),
            dma((2, 5, chunks)),
            dma((2, PLANES, chunks)),
            dma((2, PLANES)),
            dma((2, PLANES)),
            dma((2, owners)),
            dma((2, owners)),
            dma((2, owners)),
            dma((2, owners)),
            dma((owners,)),
            dma((owners,)),
            pltpu.VMEM((PLANES, grad_shape[0] // reducers, grad_shape[1]), F32),
            dma((group,)),
            dma((group,)),
            dma((PLANES,)),
            dma((PLANES,)),
            dma((group,)),
            dma((group,)),
        ],
        compiler_params=pltpu.CompilerParams(
            vmem_limit_bytes=VMEM_LIMIT, collective_id=0, has_side_effects=True
        ),
        cost_estimate=pl.CostEstimate(
            flops=64 * 2**30, bytes_accessed=16 * 2**20, transcendentals=4 * 2**20
        ),
        name="layer",
    )(counts, nodes, edges, target, senders, receivers, levels, land, masks, *weights)


def hand_out_kernel(edge_in, new_in, node_in, packed, edge_grad, new_nodes, node_grad, *outs):
    edge_grad[...] = edge_in[...]
    new_nodes[...] = new_in[...]
    node_grad[...] = node_in[...]
    rows = packed.shape[1] // 2
    lines = packed[3 * rows :, :].T
    edge_first, edge_b1, edge_second, edge_b2, edge_g, edge_h = outs[:6]
    node_first, node_b1, node_second, node_b2, node_g, node_h = outs[6:]
    edge_first[...] = packed[: 3 * rows, :].T[:rows, :]
    edge_second[...] = packed[3 * rows :, rows:]
    node_first[...] = packed[: 2 * rows, :].T[rows:, :]
    node_second[...] = packed[2 * rows : 3 * rows, rows:]
    for k, out in enumerate((edge_b1, edge_b2, edge_g, edge_h, node_b1, node_b2, node_g, node_h)):
        out[...] = lines[k, :rows]


def hand_out(new_nodes, node_grad, edge_grad, packed):
    rows = packed.shape[1] // 2
    vmem = pl.BlockSpec(memory_space=pltpu.VMEM)
    shapes = [
        (rows, 3 * rows), (rows,), (rows, rows), (rows,), (rows,), (rows,),
        (rows, 2 * rows), (rows,), (rows, rows), (rows,), (rows,), (rows,),
    ]
    large = (edge_grad, new_nodes, node_grad)
    edge_grad, new_nodes, node_grad, *small = pl.pallas_call(
        hand_out_kernel,
        in_specs=[vmem] * 4,
        out_specs=[vmem] * (3 + len(shapes)),
        out_shape=[jax.ShapeDtypeStruct(a.shape, a.dtype) for a in large]
        + [jax.ShapeDtypeStruct(s, F32) for s in shapes],
        compiler_params=pltpu.CompilerParams(vmem_limit_bytes=VMEM_LIMIT),
        name="hand_out",
    )(*large, packed)
    small[0], small[6] = small[0].T, small[6].T
    return (new_nodes, node_grad, edge_grad, *small)


def per_device(
    nodes, edges, target, senders, receivers, counts, levels, land, channel_mask,
    edge_in, edge_in_bias, edge_out, edge_out_bias, edge_gain, edge_shift,
    node_in, node_in_bias, node_out, node_out_bias, node_gain, node_shift,
):
    count = nodes.shape[1]
    return hand_out(
        *layer(
            counts, nodes, edges, target,
            senders.reshape(-1, 128), receivers.reshape(-1, 128),
            levels.reshape(1, count), land.reshape(1, count), channel_mask,
            edge_in.T, edge_out, node_in.T, node_out,
            edge_in_bias, edge_out_bias, edge_gain, edge_shift,
            node_in_bias, node_out_bias, node_gain, node_shift,
        )
    )


def solution(mesh):
    over = ("edge", "rep")
    wide, line, same = P(None, over), P(over), P()
    return jax.shard_map(
        per_device,
        mesh=mesh,
        in_specs=(wide, wide, wide, line, line, line, line, line) + (same,) * 13,
        out_specs=(wide, wide, wide) + (same,) * 12,
        check_vma=False,
    )
```

```python
import functools
import math

import jax
import jax.numpy as jnp
from jax import lax
from jax.experimental import pallas as pl
from jax.experimental.pallas import tpu as pltpu
from jax.sharding import PartitionSpec as P

NORM_EPS = 1e-05
F32 = jnp.float32
BF16 = jnp.bfloat16
LOW = 256
VMEM_LIMIT = 60 * 2**20
PLANES = 4
TABLE_PARTS = 4
NODE_PARTS = 4
EDGE_PLAN = {
    ('edges', 0): (((2, 0), (2, 1)), ()),
    ('edges', 1): (((2, 2), (2, 3)), ()),
    ('edges', 2): ((), ((3, 1),)),
    ('edges', 3): (((3, 2),), ()),
    ('edges', 4): ((), ((3, 3),)),
    ('edges', 5): (((3, 3),), ((3, 2),)),
    ('gather', 3): ((), ((3, 0),)),
    ('table', 1): (((1, 0), (1, 1), (1, 2), (1, 3)), ((1, 0), (1, 1), (1, 2), (1, 3))),
    ('table', 2): ((), ((2, 0), (2, 1), (2, 2), (2, 3))),
    ('table', 3): (((3, 0), (3, 1)), ()),
}
BACK_PLAN = {
    ('finish', 1): (((3, 2),), ()),
    ('sums', 6): (((3, 3),), ()),
    ('table', 1): (((1, 0), (1, 1), (1, 2), (1, 3)), ((1, 0), (1, 1), (1, 2), (1, 3))),
    ('table', 2): (((2, 0), (2, 1), (2, 2), (2, 3)), ((2, 0), (2, 1), (2, 2), (2, 3))),
    ('table', 3): (((3, 0), (3, 1)), ((3, 0), (3, 1), (3, 2), (3, 3))),
}
MESH = pl.DeviceIdType.MESH

EB1, EB2, EG, EH, NB1, NB2, NG, NH, CM = 0, 1, 2, 3, 4, 5, 6, 7, 8


def dot(a, b):
    return jnp.dot(a, b, preferred_element_type=F32)


def dot_tn(a, b):
    return lax.dot_general(a, b, (((0,), (0,)), ((), ())), preferred_element_type=F32)


def dot_nt(a, b):
    return lax.dot_general(a, b, (((1,), (1,)), ((), ())), preferred_element_type=F32)


def one_hot_low(ids):
    low = ids & (LOW - 1)
    rows = lax.broadcasted_iota(jnp.int32, (LOW, ids.shape[1]), 0)
    return (rows == low).astype(F32).astype(BF16)


def high_of(ids, rows):
    high = ids >> (LOW.bit_length() - 1)
    return jnp.broadcast_to(high.astype(F32).astype(BF16), (rows, ids.shape[1]))


def stack_table(table_ref, value):
    rows = value.shape[0]
    for h in range(value.shape[1] // LOW):
        table_ref[h * rows : (h + 1) * rows, :] = value[:, h * LOW : (h + 1) * LOW]


def gather_columns(table, ids, rows):
    picked = dot(table, one_hot_low(ids)).astype(BF16)
    high = high_of(ids, rows)
    out = picked[:rows]
    for h in range(1, table.shape[0] // rows):
        out = jnp.where(high == BF16(h), picked[h * rows : (h + 1) * rows], out)
    return out


def scatter_columns(values, ids, count):
    rows = values.shape[0]
    high = high_of(ids, rows)
    zero = jnp.zeros_like(values)
    spread = jnp.concatenate(
        [jnp.where(high == BF16(h), values, zero) for h in range(count // LOW)], axis=0
    )
    return dot_nt(spread, one_hot_low(ids))


def column(cols, index):
    return cols[:, index : index + 1]


def mean_rows(v):
    return jnp.mean(v, axis=0, keepdims=True)


def lane_sums(v):
    out = v[:, :128]
    for k in range(1, v.shape[1] // 128):
        out = out + v[:, k * 128 : (k + 1) * 128]
    return out


def branch_forward(w1t, w2t, b1, b2, stacked):
    pre = dot(w1t, stacked) + b1
    hidden = (pre * (1.0 / (1.0 + jnp.exp(-pre)))).astype(BF16)
    outer = dot(w2t, hidden) + b2
    shifted = outer - mean_rows(outer)
    inverse = lax.rsqrt(mean_rows(shifted * shifted) + NORM_EPS)
    return pre, shifted * inverse, inverse


def branch_backward(w2, gain, grad, pre, normal, inverse):
    q = grad * gain
    outer_grad = (
        inverse * (q - mean_rows(q) - normal * mean_rows(q * normal))
    ).astype(BF16)
    s = 1.0 / (1.0 + jnp.exp(-pre))
    pre_grad = (dot(w2, outer_grad) * (s * (1.0 + pre * (1.0 - s)))).astype(BF16)
    return outer_grad, pre_grad, (pre * s).astype(BF16)


def split_dot(low, wide):
    top = wide.astype(BF16)
    rest = (wide - top.astype(F32)).astype(BF16)
    return dot(low, top) + dot(low, rest)


def layer_kernel(
    levels_count, reps,
    counts, nodes, edges_in, target_in, senders, receivers, levels, land, masks, ew1t, ew2, nw1t,
    nw2,
    eb1, eb2, eg, eh, nb1, nb2, ng, nh,
    new_nodes, node_grad, edge_grad, summed,
    edges, target, new_hold, node_hold, in_sem, out_sem, grad_sem, tabs, send_a, recv_s, recv_e, mine, ids_tab, count_send, count_recv, pre_s, normal_s,
    inverse_s, recv_c, send_d, recv_d, total, part, grads, sums, pieces, ew1, ew2t, nw1, nw2t, cols,
    tab_send, tab_recv, ids_send, ids_recv, a_send, a_recv, b_send, b_recv, count_out, count_in,
    plane_sums, piece_send, piece_recv, plane_send, plane_recv, sum_send, sum_recv,
):
    rows, count = nodes.shape
    owners = count_send.shape[0]
    cap = senders.shape[0] * senders.shape[1] // owners
    lines_of = cap // senders.shape[1]
    ring = owners // PLANES
    high_count = count // LOW
    chunks = tab_recv.shape[2]
    chunk = tabs.shape[2] // chunks
    e, rep = lax.axis_index("edge"), lax.axis_index("rep")
    z, r = e // ring, e % ring
    upper = z // 2

    def plane_at(k):
        low = z + upper * (3 - 2 * z)
        turned = lax.rem(k + 1, 3) * (1 - k // 3) + 3 * (k // 3)
        place = k * (1 - low) + turned * low
        return place + upper * (3 - 2 * place)

    order = tuple(plane_at(k) for k in range(PLANES))
    middle = lax.rem(z, 3) != 0
    toward = 3 - 2 * z

    def at(plane, place):
        return (plane * ring + place, rep)

    def remote(src, dst, send, recv, device):
        return pltpu.make_async_remote_copy(
            src, dst, send, recv, device_id=device, device_id_type=MESH
        )

    def loop(low, high, body):
        def step(i, carry):
            body(i)
            return carry

        lax.fori_loop(low, high, step, 0)

    group, mine_of_group = ring * reps, r * reps + rep

    def group_device(g):
        return (z * ring + g // reps, lax.rem(g, reps))

    def others(body):
        def one(t):
            g = lax.rem(mine_of_group + t, group)
            body(g, group_device(g))

        loop(1, group, one)

    load_edges = pltpu.make_async_copy(edges_in, edges, in_sem.at[0])
    load_target = pltpu.make_async_copy(target_in, target, in_sem.at[1])
    load_edges.start()
    load_target.start()

    barrier = pltpu.get_barrier_semaphore()

    def greet(device):
        pl.semaphore_signal(barrier, inc=1, device_id=device, device_id_type=MESH)

    loop(1, owners, lambda t: greet((lax.rem(e + t, owners), rep)))

    def greet_other_cores(t):
        loop(0, ring, lambda place: greet((z * ring + place, lax.rem(rep + t, reps))))

    loop(1, reps, greet_other_cores)
    stack_table(tabs.at[0, z], nodes[...])
    pl.semaphore_wait(barrier, owners - 1 + ring * (reps - 1))

    def part_of(phase, plane, c):
        return tabs.at[phase, plane, pl.ds(c * chunk, chunk)]

    def table_copy(phase, plane, c, lane, to):
        return remote(
            part_of(phase, plane, c), part_of(phase, plane, c),
            tab_send.at[phase, lane, c], tab_recv.at[phase, plane, c], at(to, r),
        )

    def await_table(phase, plane, c):
        table_copy(phase, plane, c, 0, z).wait_recv()

    def send_own(phase, c):
        @pl.when(z < PLANES - 1)
        def _():
            table_copy(phase, z, c, 0, z + 1).start()

        @pl.when(z > 0)
        def _():
            table_copy(phase, z, c, 1, z - 1).start()

    def relay(phase, slot, low=0, high=None):
        @pl.when(middle)
        def _():
            for c in range(low, chunks if high is None else high):
                if slot == 0:
                    await_table(phase, z - toward, c)
                    table_copy(phase, z - toward, c, 2, z + toward).start()
                    await_table(phase, z + toward, c)
                    table_copy(phase, z + toward, c, 3, z - toward).start()
                else:
                    await_table(phase, z + 2 * toward, c)
                    table_copy(phase, z + 2 * toward, c, 4, z - toward).start()

    def end_wait(phase, k):
        @pl.when(jnp.logical_not(middle))
        def _():
            for c in range(chunks):
                await_table(phase, order[k], c)

    def drain_tables(phase):
        for c in range(chunks):
            @pl.when(z < PLANES - 1)
            def _():
                table_copy(phase, z, c, 0, z + 1).wait_send()

            @pl.when(z > 0)
            def _():
                table_copy(phase, z, c, 1, z - 1).wait_send()

            @pl.when(middle)
            def _():
                table_copy(phase, z - toward, c, 2, z + toward).wait_send()
                table_copy(phase, z + toward, c, 3, z - toward).wait_send()
                table_copy(phase, z + 2 * toward, c, 4, z - toward).wait_send()

    def ids_rows(plane):
        size = ring * lines_of
        return pl.ds(pl.multiple_of(plane * size, size), size)

    def ids_of(ids, j):
        block = ids[pl.ds(pl.multiple_of(j * lines_of, lines_of), lines_of), :]
        return side_by_side([block[i : i + 1] for i in range(lines_of)])

    def ids_copy(phase, ids, k):
        plane = lax.rem(z + k, PLANES)
        return remote(
            ids.at[ids_rows(plane)], ids_tab.at[phase, ids_rows(z)],
            ids_send.at[phase, plane], ids_recv.at[phase, z], at(plane, r),
        )

    def ids_arrival(phase, plane):
        rows_of = ids_tab.at[phase, ids_rows(plane)]
        return remote(
            rows_of, rows_of, ids_send.at[phase, plane], ids_recv.at[phase, plane], at(plane, r)
        )

    def plane_copy(phase, plane, to, into):
        return remote(
            send_a.at[plane * ring + to], into.at[plane * ring + r],
            a_send.at[phase, plane * ring + to], a_recv.at[phase, plane * ring + r], at(z, to),
        )

    def plane_arrival(phase, j, into):
        return remote(
            send_a.at[j], into.at[j], a_send.at[phase, j], a_recv.at[phase, j], at(z, r)
        )

    def hand_over(phase, plane, to, t, got, into):
        @pl.when(t < ring)
        def _():
            send_a[plane * ring + to] = got
            plane_copy(phase, plane, to, into).start()

        @pl.when(t == ring)
        def _():
            into[plane * ring + r] = got

    def gather_step(phase, k, into):
        plane = plane_at(k)

        def two(ts):
            tos = [lax.rem(r + t + 1, ring) for t in ts]
            got = gather_columns(
                tabs[phase, plane],
                side_by_side([ids_of(ids_tab.at[phase], plane * ring + to) for to in tos]), rows,
            )
            for i, (t, to) in enumerate(zip(ts, tos)):
                hand_over(phase, plane, to, t + 1, got[:, i * cap : (i + 1) * cap], into)

        in_pairs(two)

    def drain_planes(phase, into):
        for plane in range(PLANES):
            loop(1, ring, lambda t: plane_copy(phase, plane, lax.rem(r + t, ring), into).wait_send())

    def lanes(j):
        return pl.ds(pl.multiple_of(j * cap, cap), cap)

    def edges_copy(j):
        return remote(
            edges.at[:, lanes(j)], recv_e.at[e], b_send.at[0, j], b_recv.at[0, e], (j, rep)
        )

    def edges_arrival(a):
        return remote(
            edges.at[:, lanes(a)], recv_e.at[a], b_send.at[0, a], b_recv.at[0, a], (e, rep)
        )

    def count_copy(j):
        return remote(
            count_send.at[j], count_recv.at[e], count_out.at[j], count_in.at[e], (j, rep)
        )

    def count_arrival(a):
        return remote(
            count_send.at[a], count_recv.at[a], count_out.at[a], count_in.at[a], (e, rep)
        )

    def back_copy(a):
        return remote(
            send_d.at[a], recv_d.at[e], b_send.at[1, a], b_recv.at[1, e], (a, rep)
        )

    def back_arrival(j):
        return remote(
            send_d.at[j], recv_d.at[j], b_send.at[1, j], b_recv.at[1, j], (e, rep)
        )

    def peers(body):
        loop(1, owners, lambda t: body(lax.rem(e + t, owners)))

    def in_pairs(body):
        loop(0, ring // 2, lambda h: body((2 * h, 2 * h + 1)))

    half = ring // 2

    def turns_of(low, high, body):
        def one(turn):
            k, h = turn // half, lax.rem(turn, half)
            ts = (2 * h, 2 * h + 1)
            body(turn, plane_at(k), ts, [k + t > 0 for t in ts])

        loop(low, high, one)

    def side_by_side(blocks):
        return jnp.concatenate(blocks, axis=1)

    def send_edges(k, low, high):
        loop(low, high, lambda t: edges_copy(order[k] * ring + lax.rem(r + t, ring)).start())

    place = lax.broadcasted_iota(jnp.int32, (1, cap), 1)

    def live_here(a):
        line = count_recv[a]
        wide = jnp.concatenate([line] * (cap // line.shape[1]), axis=1)
        return (place < wide).astype(F32)

    def edge_forward(a):
        own = recv_e[a]
        pre, normal, inverse = branch_forward(
            ew1t[...], ew2t[...], column(cols, EB1), column(cols, EB2),
            jnp.concatenate([own, recv_s[a], mine[a]], axis=0),
        )
        pre_s[a] = pre
        normal_s[a] = normal
        inverse_s[a] = inverse
        updated = own.astype(F32) + (normal * column(cols, EG) + column(cols, EH))
        return (updated * live_here(a)).astype(BF16)

    turns = PLANES * (ring // 2)

    def forward_pair(turn, plane, ts, remotes):
        emit_at(EDGE_PLAN, "edges", turn, turns, send_edges)
        froms = [plane * ring + lax.rem(r + ring - t, ring) for t in ts]
        for t, a, there in zip(ts, froms, remotes):
            @pl.when(t > 0)
            def _():
                plane_arrival(0, a, recv_s).wait_recv()

            @pl.when(there)
            def _():
                count_arrival(a).wait_recv()
                edges_arrival(a).wait_recv()

        total[...] += scatter_columns(
            side_by_side([edge_forward(a) for a in froms]),
            side_by_side([ids_of(receivers, a) for a in froms]), count,
        )

    def edge_backward(a, got):
        grad = got.astype(F32) * live_here(a)
        normal = normal_s[a]
        outer_grad, pre_grad, hidden = branch_backward(
            ew2[...], column(cols, EG), grad, pre_s[a], normal, inverse_s[a]
        )
        grads[...] += dot_nt(
            jnp.concatenate([recv_e[a], recv_s[a], mine[a], hidden], axis=0),
            jnp.concatenate([pre_grad, outer_grad], axis=0),
        )
        for k, v in enumerate((pre_grad.astype(F32), outer_grad.astype(F32), grad * normal, grad)):
            sums[k] += lane_sums(v)
        return pre_grad

    def backward_step(k):
        plane = plane_at(k)

        def two(ts):
            tos = [lax.rem(r + t + 1, ring) for t in ts]
            froms = [plane * ring + to for to in tos]
            both = gather_columns(
                tabs[1, z], side_by_side([ids_of(receivers, a) for a in froms]), rows
            )
            for i, (t, to, a) in enumerate(zip(ts, tos, froms)):
                got = both[:, i * cap : (i + 1) * cap]

                @pl.when(k == 0)
                def _():
                    hand_over(1, z, to, t + 1, got, recv_c)

                send_d[a] = edge_backward(a, got)

        in_pairs(two)

    def send_back(k, low, high):
        loop(low, high, lambda t: back_copy(order[k] * ring + lax.rem(r + t, ring)).start())

    def emit(plan, slot, send):
        for body_at, parts in zip((at_ends, at_middle), plan.get(slot, ((), ()))):
            if parts:
                @body_at
                def _():
                    for k, q in parts:
                        send(k, q * ring // 4, (q + 1) * ring // 4)

    def at_ends(body):
        pl.when(jnp.logical_not(middle))(body)

    def at_middle(body):
        pl.when(middle)(body)

    def emit_at(plan, slot, turn, turns, send):
        for i in range(turns):
            if (slot, i) in plan:
                @pl.when(turn == i)
                def _():
                    emit(plan, (slot, i), send)

    for c in range(chunks):
        send_own(0, c)
    for k in range(1, PLANES):
        ids_copy(0, senders, k).start()
    load_edges.wait()
    send_edges(0, 1, ring)
    for k in range(1, PLANES):
        ids_copy(1, receivers, k).start()
    ids_tab[0, ids_rows(z)] = senders[ids_rows(z)]
    for j in range(owners):
        count_send[j] = jnp.full(count_send.shape[1:], counts[j], jnp.int32)
    count_recv[e] = count_send[e]
    recv_e[e] = edges[:, lanes(e)]
    total[...] = jnp.zeros_like(total)
    grads[...] = jnp.zeros_like(grads)
    sums[...] = jnp.zeros_like(sums)

    def eye(n):
        return (
            lax.broadcasted_iota(jnp.int32, (n, n), 0) == lax.broadcasted_iota(jnp.int32, (n, n), 1)
        ).astype(F32).astype(BF16)

    unit = eye(rows)
    ew1[...] = dot_tn(ew1t[...], unit).astype(BF16)
    nw1[...] = dot_tn(nw1t[...], unit).astype(BF16)
    ew2t[...] = dot_tn(ew2[...], unit).astype(BF16)
    nw2t[...] = dot_tn(nw2[...], unit).astype(BF16)
    lines = [v[...].astype(F32)[None, :] for v in (eb1, eb2, eg, eh, nb1, nb2, ng, nh)]
    lines.append(masks[...].astype(F32))
    lines.append(jnp.zeros((-(8 + levels_count) % 16, rows), F32))
    cols[...] = dot_nt(unit, jnp.concatenate(lines, axis=0).astype(BF16))

    def forward_gathers(k):
        @pl.when(k == 1)
        def _():
            relay(0, 0)
            for other in range(1, PLANES):
                ids_arrival(0, order[other]).wait_recv()
            end_wait(0, 1)

        @pl.when(k == 2)
        def _():
            relay(0, 1)
            end_wait(0, 2)

        @pl.when(k == 3)
        def _():
            end_wait(0, 3)

        emit_at(EDGE_PLAN, "table", k, PLANES, send_edges)
        gather_step(0, k, recv_s)
        emit_at(EDGE_PLAN, "gather", k, PLANES, send_edges)

        def mine_pair(turn, plane, ts, _):
            js = [plane * ring + t for t in ts]
            both = gather_columns(tabs[0, z], side_by_side([ids_of(receivers, j) for j in js]), rows)
            for i, j in enumerate(js):
                mine[j] = both[:, i * cap : (i + 1) * cap]

        @pl.when(k < 3)
        def _():
            turns_of((k + k // 2) * half, (k + 1 + (k + 1) // 2) * half, mine_pair)

    peers(lambda j: count_copy(j).start())

    early = half * (2 - z * (3 - z) // 2)

    def forward_steps(k):
        last = k // PLANES
        turns_of(last * early, k // 3 * early + last * (turns - early), forward_pair)

        @pl.when(k < PLANES)
        def _():
            forward_gathers(k)

    loop(0, PLANES + 1, forward_steps)
    drain_planes(0, recv_s)

    load_target.wait()

    node_parts = math.gcd(high_count, NODE_PARTS)
    per = high_count // node_parts
    wide = per * LOW
    node_first = jnp.zeros((2 * rows, rows), F32)
    node_second = jnp.zeros((rows, rows), F32)
    node_sums = [jnp.zeros((rows, 128), F32)] * 4
    for c in range(node_parts):
        here = slice(c * wide, (c + 1) * wide)
        aggregate = jnp.concatenate(
            [total[h * rows : (h + 1) * rows, :] for h in range(c * per, (c + 1) * per)], axis=1
        ).astype(BF16)
        own = nodes[:, here]
        stacked = jnp.concatenate([own, aggregate], axis=0)
        pre, normal, inverse = branch_forward(
            nw1t[...], nw2t[...], column(cols, NB1), column(cols, NB2), stacked
        )
        gain = column(cols, NG)
        state = own.astype(F32) + (normal * gain + column(cols, NH))
        new_hold[:, here] = state.astype(BF16)
        weight = jnp.zeros((rows, wide), F32)
        for l in range(levels_count):
            weight = jnp.where(levels[:, here] == l, column(cols, CM + l), weight)
        weight = weight * land[:, here].astype(F32)
        grad = weight * (state - target[:, here].astype(F32))
        outer_grad, pre_grad, hidden = branch_backward(nw2[...], gain, grad, pre, normal, inverse)
        stacked_grad = dot(nw1[...], pre_grad)
        part[:, here] = grad + stacked_grad[:rows]
        low = stacked_grad[rows:].astype(BF16)
        for h in range(per):
            tabs[1, z, (c * per + h) * rows : (c * per + h + 1) * rows, :] = low[
                :, h * LOW : (h + 1) * LOW
            ]
        for part_c in range(c * chunks // node_parts, (c + 1) * chunks // node_parts):
            send_own(1, part_c)
        node_first = node_first + dot_nt(stacked, pre_grad)
        node_second = node_second + dot_nt(hidden, outer_grad)
        for k, v in enumerate((pre_grad.astype(F32), outer_grad.astype(F32), grad * normal, grad)):
            node_sums[k] = node_sums[k] + lane_sums(v)

    new_copy = pltpu.make_async_copy(new_hold, new_nodes, out_sem.at[0])
    new_copy.start()

    def backward_steps(k):
        backward_step(k)

        @pl.when(k == 0)
        def _():
            send_back(0, 1, ring)

        @pl.when(k == 1)
        def _():
            relay(1, 0)
            for other in range(1, PLANES):
                ids_arrival(1, order[other]).wait_recv()
            end_wait(1, 1)

        @pl.when(k == 2)
        def _():
            relay(1, 1)
            end_wait(1, 2)

        @pl.when((k == 1) | (k == 2))
        def _():
            emit_at(BACK_PLAN, "table", k, PLANES, send_back)
            gather_step(1, k, recv_c)
            emit_at(BACK_PLAN, "gather", k, PLANES, send_back)

    loop(0, PLANES, backward_steps)

    grads[: 2 * rows, rows:] = node_first
    grads[2 * rows : 3 * rows, rows:] = node_second
    grads[3 * rows :, :8] = jnp.concatenate(
        [sums[k].sum(axis=1, keepdims=True) for k in range(4)]
        + [v.sum(axis=1, keepdims=True) for v in node_sums],
        axis=1,
    )
    reducers = min(group, grads.shape[0] // 8)
    height = grads.shape[0] // reducers

    def piece(g):
        return pl.ds(pl.multiple_of(g * height, 8), height)

    def piece_copy(g, device):
        return remote(
            grads.at[piece(g)], pieces.at[mine_of_group],
            piece_send.at[g], piece_recv.at[mine_of_group], device,
        )

    def piece_arrival(g):
        return remote(
            grads.at[piece(0)], pieces.at[g], piece_send.at[0], piece_recv.at[g], (e, rep)
        )

    def plane_sum_copy(k):
        plane = lax.rem(z + k, PLANES)
        return remote(
            plane_sums.at[z], plane_sums.at[z], plane_send.at[plane], plane_recv.at[z],
            at(plane, r),
        )

    def plane_sum_arrival(k):
        plane = lax.rem(z + k, PLANES)
        here = plane_sums.at[plane]
        return remote(here, here, plane_send.at[plane], plane_recv.at[plane], (e, rep))

    def sum_copy(g, device):
        return remote(
            summed.at[piece(mine_of_group)], summed.at[piece(mine_of_group)],
            sum_send.at[g], sum_recv.at[mine_of_group], device,
        )

    def sum_arrival(g):
        return remote(
            summed.at[piece(g)], summed.at[piece(g)], sum_send.at[0], sum_recv.at[g], (e, rep)
        )

    def to_reducers(body):
        def one(g, device):
            if reducers == group:
                body(g, device)
            else:
                @pl.when(g < reducers)
                def _():
                    body(g, device)

        others(one)

    def as_reducer(body):
        if reducers == group:
            body()
        else:
            pl.when(mine_of_group < reducers)(body)

    to_reducers(lambda g, device: piece_copy(g, device).start())

    total[...] = jnp.zeros_like(total)

    def by_receiver(h):
        emit_at(BACK_PLAN, "sums", h, owners // 2, send_back)
        total[...] += scatter_columns(
            side_by_side([send_d[2 * h], send_d[2 * h + 1]]),
            side_by_side([ids_of(receivers, 2 * h), ids_of(receivers, 2 * h + 1)]), count,
        )

    loop(0, owners // 2, by_receiver)

    def node_total(w_rows):
        sums_here = side_by_side([total[h * rows : (h + 1) * rows, :] for h in range(high_count)])
        part[...] += split_dot(ew1[w_rows, :], sums_here)

    node_total(slice(2 * rows, 3 * rows))
    total[...] = jnp.zeros_like(total)

    @as_reducer
    def _():
        pieces[mine_of_group] = grads[piece(mine_of_group), :]
        others(lambda g, device: piece_arrival(g).wait_recv())
        running = pieces[0]
        for g in range(1, group):
            running = running + pieces[g]
        plane_sums[z] = running
        for k in range(1, PLANES):
            plane_sum_copy(k).start()

    end_wait(1, 3)
    emit_at(BACK_PLAN, "table", PLANES - 1, PLANES, send_back)
    gather_step(1, PLANES - 1, recv_c)
    emit_at(BACK_PLAN, "gather", PLANES - 1, PLANES, send_back)

    def grad_copy(j):
        return pltpu.make_async_copy(recv_c.at[j], edge_grad.at[:, lanes(j)], grad_sem.at[j])

    def finish_edges(j, pre_grad):
        grad = recv_c[j].astype(F32) * (place < counts[j]).astype(F32)
        recv_c[j] = (grad + dot(ew1[:rows, :], pre_grad)).astype(BF16)
        grad_copy(j).start()

    recv_d[e] = send_d[e]

    def finish(turn, plane, ts, remotes):
        emit_at(BACK_PLAN, "finish", turn, turns, send_back)
        js = [plane * ring + lax.rem(r + ring - t, ring) for t in ts]
        for t, j, there in zip(ts, js, remotes):
            @pl.when(t > 0)
            def _():
                plane_arrival(1, j, recv_c).wait_recv()

            @pl.when(there)
            def _():
                back_arrival(j).wait_recv()

            finish_edges(j, recv_d[j])
        total[...] += scatter_columns(
            side_by_side([recv_d[j] for j in js]), side_by_side([ids_of(senders, j) for j in js]), count
        )

    def finish_step(k):
        @pl.when(k == 2)
        def _():
            @as_reducer
            def _():
                for other in range(1, PLANES):
                    plane_sum_arrival(other).wait_recv()
                running = plane_sums[0]
                for plane in range(1, PLANES):
                    running = running + plane_sums[plane]
                summed[piece(mine_of_group), :] = running
                others(lambda g, device: sum_copy(g, device).start())

        turns_of(k * half, (k + 1) * half, finish)

    loop(0, PLANES, finish_step)
    node_total(slice(rows, 2 * rows))
    node_hold[...] = part[...].astype(BF16)
    node_copy = pltpu.make_async_copy(node_hold, node_grad, out_sem.at[1])
    node_copy.start()

    drain_tables(0)
    drain_tables(1)
    drain_planes(1, recv_c)
    for k in range(1, PLANES):
        ids_copy(0, senders, k).wait_send()
        ids_copy(1, receivers, k).wait_send()
    peers(lambda j: count_copy(j).wait_send())
    peers(lambda j: edges_copy(j).wait_send())
    peers(lambda j: back_copy(j).wait_send())
    to_reducers(lambda g, device: piece_copy(g, device).wait_send())

    @as_reducer
    def _():
        for k in range(1, PLANES):
            plane_sum_copy(k).wait_send()
        others(lambda g, device: sum_copy(g, device).wait_send())

    to_reducers(lambda g, device: sum_arrival(g).wait_recv())
    loop(0, owners, lambda j: grad_copy(j).wait())
    new_copy.wait()
    node_copy.wait()


def layer(counts, nodes, edges, target, senders, receivers, levels, land, masks, *weights):
    rows, count = nodes.shape
    owners = lax.axis_size("edge")
    slots = edges.shape[1]
    cap = slots // owners
    reps = lax.axis_size("rep")
    group = owners // PLANES * reps
    chunks = math.gcd(count // LOW, TABLE_PARTS)
    grad_shape = (4 * rows, 2 * rows)
    reducers = min(group, grad_shape[0] // 8)
    blocks = (owners, rows, cap)
    dma = pltpu.SemaphoreType.DMA
    vmem = pl.BlockSpec(memory_space=pltpu.VMEM)
    stay = pl.BlockSpec(memory_space=pl.ANY)
    return pl.pallas_call(
        functools.partial(layer_kernel, masks.shape[0], reps),
        in_specs=[pl.BlockSpec(memory_space=pltpu.SMEM), vmem, stay, stay]
        + [vmem] * (5 + len(weights)),
        out_specs=[stay, stay, stay, vmem],
        out_shape=[
            jax.ShapeDtypeStruct((rows, count), BF16),
            jax.ShapeDtypeStruct((rows, count), BF16),
            jax.ShapeDtypeStruct((rows, slots), BF16),
            jax.ShapeDtypeStruct(grad_shape, F32),
        ],
        scratch_shapes=[
            pltpu.VMEM((rows, slots), BF16),
            pltpu.VMEM((rows, count), BF16),
            pltpu.VMEM((rows, count), BF16),
            pltpu.VMEM((rows, count), BF16),
            dma((2,)),
            dma((2,)),
            dma((owners,)),
            pltpu.VMEM((2, PLANES, rows * (count // LOW), LOW), BF16),
            pltpu.VMEM(blocks, BF16),
            pltpu.VMEM(blocks, BF16),
            pltpu.VMEM(blocks, BF16),
            pltpu.VMEM(blocks, BF16),
            pltpu.VMEM((2,) + senders.shape, jnp.int32),
            pltpu.VMEM((owners, 1, 128), jnp.int32),
            pltpu.VMEM((owners, 1, 128), jnp.int32),
            pltpu.VMEM(blocks, F32),
            pltpu.VMEM(blocks, F32),
            pltpu.VMEM((owners, 1, cap), F32),
            pltpu.VMEM(blocks, BF16),
            pltpu.VMEM(blocks, BF16),
            pltpu.VMEM(blocks, BF16),
            pltpu.VMEM((rows * (count // LOW), LOW), F32),
            pltpu.VMEM((rows, count), F32),
            pltpu.VMEM(grad_shape, F32),
            pltpu.VMEM((4, rows, 128), F32),
            pltpu.VMEM((group, grad_shape[0] // reducers, grad_shape[1]), F32),
            pltpu.VMEM((3 * rows, rows), BF16),
            pltpu.VMEM((rows, rows), BF16),
            pltpu.VMEM((2 * rows, rows), BF16),
            pltpu.VMEM((rows, rows), BF16),
            pltpu.VMEM((rows, 16 * -(-(8 + masks.shape[0]) // 16)), F32),
            dma((2, 5, chunks)),
            dma((2, PLANES, chunks)),
            dma((2, PLANES)),
            dma((2, PLANES)),
            dma((2, owners)),
            dma((2, owners)),
            dma((2, owners)),
            dma((2, owners)),
            dma((owners,)),
            dma((owners,)),
            pltpu.VMEM((PLANES, grad_shape[0] // reducers, grad_shape[1]), F32),
            dma((group,)),
            dma((group,)),
            dma((PLANES,)),
            dma((PLANES,)),
            dma((group,)),
            dma((group,)),
        ],
        compiler_params=pltpu.CompilerParams(
            vmem_limit_bytes=VMEM_LIMIT, collective_id=0, has_side_effects=True
        ),
        cost_estimate=pl.CostEstimate(
            flops=64 * 2**30, bytes_accessed=16 * 2**20, transcendentals=4 * 2**20
        ),
        name="layer",
    )(counts, nodes, edges, target, senders, receivers, levels, land, masks, *weights)


def hand_out_kernel(edge_in, new_in, node_in, packed, edge_grad, new_nodes, node_grad, *outs):
    edge_grad[...] = edge_in[...]
    new_nodes[...] = new_in[...]
    node_grad[...] = node_in[...]
    rows = packed.shape[1] // 2
    lines = packed[3 * rows :, :].T
    edge_first, edge_b1, edge_second, edge_b2, edge_g, edge_h = outs[:6]
    node_first, node_b1, node_second, node_b2, node_g, node_h = outs[6:]
    edge_first[...] = packed[: 3 * rows, :].T[:rows, :]
    edge_second[...] = packed[3 * rows :, rows:]
    node_first[...] = packed[: 2 * rows, :].T[rows:, :]
    node_second[...] = packed[2 * rows : 3 * rows, rows:]
    for k, out in enumerate((edge_b1, edge_b2, edge_g, edge_h, node_b1, node_b2, node_g, node_h)):
        out[...] = lines[k, :rows]


def hand_out(new_nodes, node_grad, edge_grad, packed):
    rows = packed.shape[1] // 2
    vmem = pl.BlockSpec(memory_space=pltpu.VMEM)
    shapes = [
        (rows, 3 * rows), (rows,), (rows, rows), (rows,), (rows,), (rows,),
        (rows, 2 * rows), (rows,), (rows, rows), (rows,), (rows,), (rows,),
    ]
    large = (edge_grad, new_nodes, node_grad)
    edge_grad, new_nodes, node_grad, *small = pl.pallas_call(
        hand_out_kernel,
        in_specs=[vmem] * 4,
        out_specs=[vmem] * (3 + len(shapes)),
        out_shape=[jax.ShapeDtypeStruct(a.shape, a.dtype) for a in large]
        + [jax.ShapeDtypeStruct(s, F32) for s in shapes],
        compiler_params=pltpu.CompilerParams(vmem_limit_bytes=VMEM_LIMIT),
        name="hand_out",
    )(*large, packed)
    small[0], small[6] = small[0].T, small[6].T
    return (new_nodes, node_grad, edge_grad, *small)


def per_device(
    nodes, edges, target, senders, receivers, counts, levels, land, channel_mask,
    edge_in, edge_in_bias, edge_out, edge_out_bias, edge_gain, edge_shift,
    node_in, node_in_bias, node_out, node_out_bias, node_gain, node_shift,
):
    count = nodes.shape[1]
    return hand_out(
        *layer(
            counts, nodes, edges, target,
            senders.reshape(-1, 128), receivers.reshape(-1, 128),
            levels.reshape(1, count), land.reshape(1, count), channel_mask,
            edge_in.T, edge_out, node_in.T, node_out,
            edge_in_bias, edge_out_bias, edge_gain, edge_shift,
            node_in_bias, node_out_bias, node_gain, node_shift,
        )
    )


def solution(mesh):
    over = ("edge", "rep")
    wide, line, same = P(None, over), P(over), P()
    return jax.shard_map(
        per_device,
        mesh=mesh,
        in_specs=(wide, wide, wide, line, line, line, line, line) + (same,) * 13,
        out_specs=(wide, wide, wide) + (same,) * 12,
        check_vma=False,
    )
```
